32 devices in a mesh: expert: 4 (over x, core), shard: 8 (over z, y).
Axes of the slice: x: 2, y: 2, z: 4, core: 2. Of those that a mesh axis runs over, the one named last changes fastest.
Arguments:
- tokens: bfloat16 [16384, 768], P(('expert', 'shard')), may hold values from -6 to 6
- gate_input: float32 [16384, 8], P(('expert', 'shard')), may hold values from -3 to 3
- routes: int32 [16384, 2], P(('expert', 'shard')), may hold values from 0 to 7, all different within a row; in each aligned block of 512 rows (0 to 511, 512 to 1023, ...) at most 160 rows name the same one
- block_ids: int32 [32, 512], P(('expert', 'shard')), may hold values from 0 to 3, never falling along the last dimension, each value on 1 to 256 neighbouring positions
- cotangent: bfloat16 [16384, 768], P(('expert', 'shard')), may hold values from -6 to 6
- norm_gain: bfloat16 [1, 2, 768], P(None, None, ('expert', 'shard')), may hold values from 0.5 to 1.5
- attn_in: bfloat16 [1, 3, 768, 768], P(None, None, ('expert', 'shard')), may hold values from -0.21875 to 0.21875
- attn_out: bfloat16 [1, 768, 768], P(None, ('expert', 'shard')), may hold values from -0.875 to 0.875
- router: bfloat16 [1, 768, 12], P(None, ('expert', 'shard')), may hold values from -0.125 to 0.125
- const_vec: bfloat16 [1, 2, 768], P(None, None, ('expert', 'shard')), may hold values from -5 to 5
- expert_gu: bfloat16 [1, 4, 2, 768, 2048], P(None, 'expert', None, 'shard'), may hold values from -0.21875 to 0.21875
- expert_down: bfloat16 [1, 4, 2048, 768], P(None, 'expert', 'shard'), may hold values from -0.1875 to 0.1875
Outputs:
- output: bfloat16 [16384, 768], P(('expert', 'shard'))
- input_grad: float32 [16384, 768], P(('expert', 'shard'))
- gate_input_grad: float32 [16384, 8], P(('expert', 'shard'))
- norm_gain_grad: float32 [1, 2, 768], P(None, None, ('expert', 'shard'))
- attn_in_grad: float32 [1, 3, 768, 768], P(None, None, ('expert', 'shard'))
- attn_out_grad: float32 [1, 768, 768], P(None, ('expert', 'shard'))
- router_grad: float32 [1, 768, 12], P(None, ('expert', 'shard'))
- const_vec_grad: float32 [1, 2, 768], P(None, None, ('expert', 'shard'))
- expert_gu_grad: float32 [1, 4, 2, 768, 2048], P(None, 'expert', None, 'shard')
- expert_down_grad: float32 [1, 4, 2048, 768], P(None, 'expert', 'shard')
The draws below stay inside these ranges and needn't reach their ends.
Inputs may be any that keep to these rules, and one draw needn't show every extreme that they name: `routes`: the two entries of a row differ; among the rows of one sequence no expert is named more than 160 times. `block_ids`: never falling along a sequence; each block holds 1 to 256 positions.
All inputs are finite; a program needn't handle non-finite values.
Results may differ from the reference program's by a relative error of at most 0.013.
Values may be sent and summed in bfloat16 or wider, within the bound.
A program may use at most 192 MiB of HBM per device.

```python
import math
import jax
import jax.numpy as jnp
import numpy as np
from jax import lax

D = 768
H = 12
HD = 64
FF = 2048
LAYERS = 1
TOK_DEV = 512
BLOCK = 256
CAP = 160
FFN_EXPERTS = 4
EXPERTS = 8
N_SEQ = 32
TOKENS = 16384


def level_of(own_key, dims, split, smallest, high):
    gain, own = 1.0, jax.random.fold_in(own_key, 6)
    for dim, shards_of in split:
        draws = jnp.exp(jax.random.uniform(jax.random.fold_in(own, dim), (shards_of,), jnp.float32, smallest / len(split), high / len(split)))
        gain = gain * jnp.repeat(draws, dims[dim] // shards_of).reshape([-1 if axis == dim else 1 for axis in range(len(dims))])
    return gain


def length_profile(count, total, reach, lean):
    portions = [(1 << 20) // math.isqrt(grade ** lean) + 1 for grade in range(2, count + 1)]
    surplus, counts = total - reach - (count - 1), [1] * (count - 1)
    while surplus > 0:
        candidates = [i for i in range(count - 1) if counts[i] < reach]
        pool, budget = sum([portions[i] for i in candidates]), surplus
        for i in candidates:
            addition = min(reach - counts[i], max(1, budget * portions[i] // pool), surplus)
            counts[i] = counts[i] + addition
            surplus = surplus - addition
    return np.array([reach] + counts)


def uneven(rng, count, total, reach, lean):
    if count == 2:
        one = jax.random.randint(rng, (), max(1, total - reach), min(reach, total - 1) + 1)
        return jnp.stack([one, total - one])
    lengths = jnp.asarray(length_profile(count, total, reach, lean), jnp.int32)
    twos = (count - 1) // 2
    giver, sink = lengths[1:1 + 2 * twos:2], lengths[2:2 + 2 * twos:2]
    slack = jnp.minimum(giver - 1, reach - sink)
    moved = jax.random.randint(jax.random.fold_in(rng, 1), (twos,), 0, 1 << 20) % (slack + 1)
    lengths = lengths.at[1:1 + 2 * twos:2].set(giver - moved).at[2:2 + 2 * twos:2].set(sink + moved)
    return lengths[jax.random.permutation(jax.random.fold_in(rng, 2), count)]


def routed_block(own_key, own, number, rows, amount, top, reach, lean):
    ranking = jax.random.permutation(own_key, amount)
    heavy_load, common = shares(amount, rows * top, reach, lean, True), shares(amount, rows * top, reach, lean, False)
    places = jnp.arange(amount)

    def named(lengths, turn):
        used = int((lengths > 0).sum())
        fixed = max(1, used // 4)
        shifted = fixed + (places - fixed + turn * (used - fixed)) % max(1, amount - fixed)
        return jnp.zeros((amount,), jnp.int32).at[ranking[jnp.where(places < fixed, places, shifted)]].set(jnp.asarray(lengths, jnp.int32))

    lengths = jnp.where(number % 4 == 0, named(heavy_load, number // 4), named(common, number - number // 4 - 1))
    mixed = jax.random.permutation(jax.random.fold_in(own, 3), amount)
    donor, sink = mixed[0:amount // 2 * 2:2], mixed[1:amount // 2 * 2:2]
    slack = jnp.minimum(lengths[donor] - 1, reach - lengths[sink]) // 2
    slack = jnp.where((donor == ranking[0]) | (sink == ranking[0]) | (lengths[sink] == 0), 0, jnp.maximum(slack, 0))
    shifted = jax.random.randint(jax.random.fold_in(own, 4), (amount // 2,), 0, 1 << 20) % (slack + 1)
    lengths = lengths.at[donor].add(-shifted).at[sink].add(shifted)
    members = jnp.searchsorted(jnp.cumsum(lengths), jnp.arange(rows * top), side="right").astype(jnp.int32)
    grid = members.reshape(top, rows).T
    grid = grid[jax.random.permutation(jax.random.fold_in(own, 1), rows)]
    turn = jax.random.randint(jax.random.fold_in(own, 2), (rows, 1), 0, top)
    return jnp.take_along_axis(grid, (jnp.arange(top)[None, :] + turn) % top, axis=1)


def shares(count, total, limit, lean, full):
    loads = [(1 << 20) // math.isqrt(grade ** lean) + 1 for grade in range(1, count + 1)]
    largest = limit if full else min(limit, max(-(-total // count), total * loads[0] // sum(loads)))
    least = 1 if total - largest >= count - 1 else 0
    counts, rest = [largest] + [least] * (count - 1), total - largest - least * (count - 1)
    while rest > 0:
        free = [i for i in range(1, count) if counts[i] < largest] or [i for i in range(1, count) if counts[i] < limit]
        mass, remaining = sum([loads[i] for i in free]), rest
        for i in free:
            addition = min(limit - counts[i], max(1, remaining * loads[i] // mass), rest)
            counts[i] = counts[i] + addition
            rest = rest - addition
    return np.array(counts)


def normal_values(stream_key, shape, width, most, cuts=(), held_as=jnp.bfloat16):
    gain = level_of(stream_key, shape, cuts, -0.22, 0.18) if cuts else 1.0
    array = jax.random.normal(stream_key, shape, jnp.float32) * width * gain
    return jnp.minimum(jnp.maximum(array, -most), most).astype(held_as)


def setup_inputs(seed: int = 0) -> dict:
    splits = jax.random.split(jax.random.key(seed), 13)
    tokens = normal_values(splits[0], (TOKENS, D), 1.0, 6.0, ((0, 32),))
    gate_input = normal_values(splits[1], (TOKENS, EXPERTS), 0.4, 3.0, ((0, 32),), jnp.float32)
    routes_keys = jax.random.split(jax.random.fold_in(splits[2], 1), TOKENS // TOK_DEV)
    routes_turns = jax.random.permutation(jax.random.fold_in(splits[2], 3), TOKENS // TOK_DEV)
    routes = jax.vmap(lambda own, number: routed_block(jax.random.fold_in(splits[2], 2), own, number, TOK_DEV, EXPERTS, 2, CAP, 2))(routes_keys, routes_turns).reshape((TOKENS, 2))
    block_ids = jax.vmap(lambda own: jnp.searchsorted(jnp.cumsum(uneven(own, 2 * TOK_DEV // BLOCK, TOK_DEV, BLOCK, 2)), jnp.arange(TOK_DEV), side="right"))(jax.random.split(splits[3], N_SEQ)).reshape((N_SEQ, TOK_DEV)).astype(jnp.int32)
    cotangent = normal_values(splits[4], (TOKENS, D), 1.0, 6.0, ((0, 32),))
    norm_gain = jnp.clip(1.0 + 0.1 * jax.random.normal(splits[5], (LAYERS, 2, D), jnp.float32), 0.5, 1.5).astype(jnp.bfloat16)
    attn_in = normal_values(splits[6], (LAYERS, 3, D, D), D ** -0.5, 0.21875, ((2, 32),))
    attn_out = normal_values(splits[7], (LAYERS, D, D), (D // 16) ** -0.5, 0.875, ((1, 32),))
    router = normal_values(splits[8], (LAYERS, D, EXPERTS + 4), (3 * D) ** -0.5, 0.125, ((1, 32),))
    const_vec = normal_values(splits[9], (LAYERS, 2, D), 1.0, 5.0, ((2, 32),))
    expert_gu = normal_values(splits[10], (LAYERS, FFN_EXPERTS, 2, D, FF), D ** -0.5, 0.21875, ((1, 4), (3, 8)))
    expert_down = normal_values(splits[11], (LAYERS, FFN_EXPERTS, FF, D), (FF // 2) ** -0.5, 0.1875, ((1, 4), (2, 8)))
    return dict(tokens=tokens, gate_input=gate_input, routes=routes, block_ids=block_ids, cotangent=cotangent, norm_gain=norm_gain, attn_in=attn_in, attn_out=attn_out, router=router, const_vec=const_vec, expert_gu=expert_gu, expert_down=expert_down)


HIGHEST = lax.Precision.HIGHEST

@jax.custom_vjp
def low(v):
    return lax.optimization_barrier(v.astype(jnp.bfloat16)).astype(jnp.float32)

@jax.custom_vjp
def low_back(v):
    return v

def low_keep(v):
    return (low(v), None)

def low_pass(kept, grad):
    return (grad,)

def back_keep(v):
    return (v, None)

def back_low(kept, grad):
    return (low(grad),)
low.defvjp(low_keep, low_pass)
low_back.defvjp(back_keep, back_low)

def matmul_high(left, right):
    return jnp.dot(left, right, precision=HIGHEST, preferred_element_type=jnp.float32)

def rms_normal(values):
    return values * lax.rsqrt(lax.optimization_barrier(jnp.mean(values * values, axis=-1, keepdims=True)) + 1e-06)

def rounded_both(values):
    return low_back(low(values))

def slot_table(route_pair, ffn_count, capacity):
    flat_route = route_pair.reshape(-1).astype(jnp.int32)
    pair_count = flat_route.shape[0]
    one_hot = (flat_route[:, None] == jnp.arange(ffn_count, dtype=jnp.int32)[None, :]).astype(jnp.int32)
    running = jnp.cumsum(one_hot, axis=0) - 1
    position = lax.optimization_barrier(jnp.sum(running * one_hot, axis=1))
    is_routed = flat_route < ffn_count
    destination = jnp.where(is_routed, flat_route * capacity + position, ffn_count * capacity).astype(jnp.int32)
    pair_index = jnp.arange(pair_count, dtype=jnp.int32)
    owner_pair = jnp.zeros((ffn_count * capacity,), jnp.int32).at[destination].set(pair_index, mode='drop')
    filled = jnp.zeros((ffn_count * capacity,), jnp.int32).at[destination].set(jnp.ones_like(pair_index), mode='drop')
    return (destination, is_routed, owner_pair, filled)

def branch_outputs(route_pair, ffn_rows, second_in, const_weights, vectors, ffn_count):
    const_rows = const_weights[:, :, 0:1] * second_in[:, None, :] + const_weights[:, :, 1:2] * vectors[None, :, :]
    result = ffn_rows + jnp.where((route_pair == ffn_count + 1)[:, :, None], second_in[:, None, :], 0.0)
    for member in range(2):
        chosen_const = (route_pair == ffn_count + 2 + member)[:, :, None]
        result = result + jnp.where(chosen_const, const_rows[:, member][:, None, :], 0.0)
    return result

def moe_layer(hidden, previous, route_pair, blocks, params):
    gain_rows, w_in, w_out, w_router, vectors, w_gate_up, w_down = params
    tok_count = hidden.shape[0]
    first_in = low(rms_normal(hidden) * gain_rows[0])
    queries = rounded_both(matmul_high(first_in, w_in[0])).reshape(tok_count, H, HD)
    key_rows = rounded_both(matmul_high(first_in, w_in[1])).reshape(tok_count, H, HD)
    value_rows = rounded_both(matmul_high(first_in, w_in[2])).reshape(tok_count, H, HD)
    raw_scores = low_back(jnp.einsum('thd,shd->hts', queries, key_rows, precision=HIGHEST) * 0.125)
    allowed = blocks[None, :] <= blocks[:, None]
    raw_scores = jnp.where(allowed[None, :, :], raw_scores, -1e+30)
    attn_probs = jax.nn.softmax(raw_scores, axis=-1)
    mixed_heads = jnp.einsum('hts,shd->thd', low(attn_probs), value_rows, precision=HIGHEST)
    mixed_heads = rounded_both(mixed_heads.reshape(tok_count, D))
    after_attn = hidden + low_back(matmul_high(mixed_heads, w_out))
    second_in = low(rms_normal(after_attn) * gain_rows[1])
    all_logits = matmul_high(second_in, w_router)
    logits = all_logits[:, :EXPERTS] + previous
    picked = route_pair[:, :, None] == jnp.arange(EXPERTS, dtype=jnp.int32)[None, None, :]
    chosen = lax.optimization_barrier(jnp.sum(jnp.where(picked, logits[:, None, :], 0.0), axis=-1))
    first_gate = jax.nn.sigmoid(chosen[:, 0] - chosen[:, 1])
    gate_pair = jnp.stack([first_gate, 1.0 - first_gate], axis=1)
    const_weights = jax.nn.softmax(all_logits[:, EXPERTS:].reshape(tok_count, 2, 2), axis=-1)
    destination, is_routed, owner_pair, filled = slot_table(route_pair, FFN_EXPERTS, CAP)
    slot_rows = jnp.where(filled[:, None] > 0, second_in[owner_pair // 2], 0.0).reshape(FFN_EXPERTS, CAP, D)
    gate_pre = low_back(jnp.einsum('ecd,edf->ecf', slot_rows, w_gate_up[:, 0], precision=HIGHEST))
    up_pre = low_back(jnp.einsum('ecd,edf->ecf', slot_rows, w_gate_up[:, 1], precision=HIGHEST))
    activated = low(jax.nn.silu(gate_pre) * up_pre)
    expert_out = rounded_both(jnp.einsum('ecf,efd->ecd', activated, w_down, precision=HIGHEST))
    expert_out = expert_out.reshape(FFN_EXPERTS * CAP, D)
    safe_dest = jnp.minimum(destination, FFN_EXPERTS * CAP - 1)
    ffn_rows = jnp.where(is_routed[:, None], expert_out[safe_dest], 0.0).reshape(tok_count, 2, D)
    pair_out = branch_outputs(route_pair, ffn_rows, second_in, const_weights, vectors, FFN_EXPERTS)
    return (after_attn + lax.optimization_barrier(jnp.sum(gate_pair[:, :, None] * pair_out, axis=1)), logits)

def network(hidden, previous, route_pair, blocks, weights):
    for level_index in range(LAYERS):
        params = tuple((weight[level_index] for weight in weights))
        hidden, previous = moe_layer(hidden, previous, route_pair, blocks, params)
    return hidden

def reference(tokens, gate_input, routes, block_ids, cotangent, norm_gain, attn_in, attn_out, router, const_vec, expert_gu, expert_down):
    weights = tuple((weight.astype(jnp.float32) for weight in (norm_gain, attn_in, attn_out, router, const_vec, expert_gu, expert_down)))
    seq_tokens = tokens.astype(jnp.float32).reshape(N_SEQ, TOK_DEV, D)
    seq_gates = gate_input.astype(jnp.float32).reshape(N_SEQ, TOK_DEV, EXPERTS)
    seq_routes = routes.reshape(N_SEQ, TOK_DEV, 2)
    seq_upstream = cotangent.astype(jnp.float32).reshape(N_SEQ, TOK_DEV, D)

    def one_sequence(totals, item):
        hidden, previous, route_pair, blocks, upstream = item

        def forward(hidden_in, previous_in, *weight_list):
            return network(hidden_in, previous_in, route_pair, blocks, weight_list)
        result, pullback = jax.vjp(forward, hidden, previous, *weights)
        grads = pullback(upstream)
        totals = tuple((total_grad + new_grad for total_grad, new_grad in zip(totals, grads[2:])))
        return (totals, (result.astype(jnp.bfloat16), grads[0], grads[1]))
    zeros = tuple((jnp.zeros_like(weight) for weight in weights))
    totals, (outputs, hidden_grad, gate_grad) = lax.scan(one_sequence, zeros, (seq_tokens, seq_gates, seq_routes, block_ids, seq_upstream))
    return (outputs.reshape(TOKENS, D), hidden_grad.reshape(TOKENS, D), gate_grad.reshape(TOKENS, EXPERTS), totals[0], totals[1], totals[2], totals[3], totals[4], totals[5], totals[6])
```

```python
from types import SimpleNamespace

import jax
import jax.numpy as jnp
from jax import lax
from jax.experimental import pallas as pl
from jax.experimental.pallas import tpu as pltpu
from jax.sharding import PartitionSpec as P

EVERY = ("expert", "shard")
H = 12
CAP = 160
EPSILON = 1e-06
MESH = pl.DeviceIdType.MESH
F32 = jnp.float32
BF16 = jnp.bfloat16
NN = (((1,), (0,)), ((), ()))
NT = (((1,), (1,)), ((), ()))
TN = (((0,), (0,)), ((), ()))


def mm(a, b, dims=NN):
    return lax.dot_general(a, b, dims, preferred_element_type=F32)


def iota(shape, dim):
    return lax.broadcasted_iota(jnp.int32, shape, dim)


def where_am_i():
    e, s = lax.axis_index("expert"), lax.axis_index("shard")
    return e // 2, e % 2, s // 2, s % 2


def device(x, c, z, y):
    return (x * 2 + c, z * 2 + y)


def remote(src, dst, send, recv, to):
    return pltpu.make_async_remote_copy(
        src_ref=src, dst_ref=dst, send_sem=send, recv_sem=recv, device_id=to, device_id_type=MESH
    )


def split3(v):
    hi = v.astype(BF16)
    rest = v - hi.astype(F32)
    mid = rest.astype(BF16)
    return hi, mid, (rest - mid.astype(F32)).astype(BF16)


def forward_kernel(
    tokens, cot, prev, routes, routes_t, blk_c, blk_r, unit_a, unit_b, gu_in, dn_in,
    gu, dn, rows_x, rows_c, w4, smalls, probs, qkv, mixed, x1, second, scal,
    ga, gb, bias, first, p0, p1, stage_c, stage_x,
    loc, sz, rz, s1, r1, s2, r2, sc_, rc, se, re, sy, ry, sd, rd, sx, rx, own,
):
    x, c, z, y = where_am_i()
    e = x * 2 + c
    units = (
        (ga, unit_a, y, x, lambda t: device(x, c, z, 1 - y), lambda t: device(1 - x, c, z, y)),
        (gb, unit_b, x, y, lambda t: device(1 - x, c, z, y), lambda t: device(x, c, z, 1 - y)),
    )

    def slot(h2, h1, zb):
        return ((c * 2 + h2) * 2 + h1) * 4 + zb

    def inside(v):
        return (v >= 0) & (v <= 3)

    def put_z(u, zb, way):
        g, _, h1, h2, _, _ = units[u]
        at = g.at[slot(h2, h1, zb)]
        i = (u * 2 + (way + 1) // 2) * 4 + zb
        to = device(x, c, jnp.clip(z + way, 0, 3), y)
        return remote(at, at, sz.at[i], rz.at[u * 4 + zb], to)

    def put_1(u, zb, got=False):
        g, _, h1, h2, to1, _ = units[u]
        at = g.at[slot(h2, (1 - h1) if got else h1, zb)]
        return remote(at, at, s1.at[u * 4 + zb], r1.at[u * 4 + zb], to1(0))

    def put_2(u, hh, zb, got=False):
        g, _, h1, h2, _, to2 = units[u]
        at = g.at[slot((1 - h2) if got else h2, hh, zb)]
        i = u * 8 + hh * 4 + zb
        return remote(at, at, s2.at[i], r2.at[i], to2(0))

    def put_c(u, hh, got=False):
        g = units[u][0]
        at = g.at[pl.ds((((1 - c) if got else c) * 2 + hh) * 8, 8)]
        return remote(at, at, sc_.at[u * 2 + hh], rc.at[u * 2 + hh], device(x, 1 - c, z, y))

    for u in range(2):
        g, src, h1, h2, _, _ = units[u]
        pltpu.make_async_copy(src, g.at[slot(h2, h1, z)], loc.at[u]).start()
    for u in range(2):
        g, src, h1, h2, _, _ = units[u]
        pltpu.make_async_copy(src, g.at[slot(h2, h1, z)], loc.at[u]).wait()
        for way in (-1, 1):
            pl.when(inside(z + way))(lambda: put_z(u, z, way).start())
        put_1(u, z).start()
        put_2(u, units[u][2], z).start()
    bias[...] = jnp.where(blk_r[...] <= blk_c[...], 0.0, -1e30)
    r_t = routes_t[...]
    expert_row = iota((16, 512), 0)
    named = ((expert_row == r_t[0:1]) | (expert_row == r_t[1:2])).astype(BF16)
    upper = (iota((512, 512), 0) < iota((512, 512), 1)).astype(BF16)
    count_t = mm(named, upper).astype(jnp.int32) + expert_row * CAP
    for k, ref in ((0, p0), (1, p1)):
        r = r_t[k : k + 1]
        spot = jnp.sum(jnp.where((expert_row == r) & (r < 4), count_t, 0), axis=0, keepdims=True)
        spot = jnp.where(r < 4, spot, -1)
        ref[...] = (iota((640, 512), 0) == spot).astype(BF16)
    for r in range(1, 4):
        for way in (1, -1):
            zb = z + way * r
            for u in range(2):

                @pl.when(inside(zb))
                def _():
                    put_z(u, zb, way).wait_recv()
                    pl.when(inside(z - way))(lambda: put_z(u, zb, -way).start())
                    put_1(u, zb).start()
                    put_2(u, units[u][2], zb).start()

    def piece(k, zb):
        if k == 1:
            return dn.at[pl.ds(pl.multiple_of(zb * 256, 256), 256)]
        yy = y if k == 0 else 1 - y
        return gu.at[:, pl.ds(pl.multiple_of(zb * 192 + yy * 96, 32), 96), :]

    def put_e(k, zb, way, src=None):
        at = piece(k, zb)
        to = device(x, c, jnp.clip(z + way, 0, 3), y)
        i = k * 8 + ((way + 1) // 2) * 4 + zb
        return remote(at if src is None else src, at, se.at[i], re.at[k * 4 + zb], to)

    def put_y():
        there = gu.at[:, pl.ds(pl.multiple_of(z * 192 + y * 96, 32), 96), :]
        return remote(gu_in.at[1 - y], there, sy.at[0], ry.at[0], device(x, c, z, 1 - y))

    def got_y():
        here = gu.at[:, pl.ds(pl.multiple_of(z * 192 + (1 - y) * 96, 32), 96), :]
        return remote(gu_in.at[1 - y], here, sy.at[0], ry.at[0], device(x, c, z, 1 - y))

    put_y().start()
    own_gu = pltpu.make_async_copy(gu_in.at[y], piece(0, z), loc.at[2])
    own_dn = pltpu.make_async_copy(dn_in, piece(1, z), loc.at[3])
    own_gu.start()
    own_dn.start()
    for k, src in ((0, gu_in.at[y]), (1, dn_in)):
        for way in (-1, 1):
            pl.when(inside(z + way))(lambda: put_e(k, z, way, src).start())

    for r in range(4):
        for way in (1, -1) if r else (1,):
            zb = z + way * r
            for u in range(2):

                @pl.when(inside(zb))
                def _():
                    put_1(u, zb, True).wait_recv()
                    put_2(u, 1 - units[u][2], zb).start()

    for u in range(2):
        put_c(u, units[u][3]).start()
    for u in range(2):
        h1 = units[u][2]
        for hh in (h1, 1 - h1):
            for zb in range(4):
                put_2(u, hh, zb, True).wait_recv()
        put_c(u, 1 - units[u][3]).start()
    for u in range(2):
        for hh in range(2):
            put_c(u, hh, True).wait_recv()

    got_y().wait_recv()
    for way in (-1, 1):
        pl.when(inside(z + way))(lambda: put_e(2, z, way).start())

    def serve(k, r):
        for way in (1, -1):
            zb = z + way * r

            @pl.when(inside(zb))
            def _():
                put_e(k, zb, way).wait_recv()
                pl.when(inside(z - way))(lambda: put_e(k, zb, -way).start())

    def assemble(m, _):
        xx, cc, zz = m // 8, (m // 4) % 2, m % 4
        a = [((cc * 2 + xx) * 2 + yy) * 4 + zz for yy in range(2)]
        b = [((cc * 2 + yy) * 2 + xx) * 4 + zz for yy in range(2)]
        at = pl.ds(pl.multiple_of(m * 48, 16), 48)
        for j in range(2):
            rows = slice(24 * j, 24 * j + 24)
            w4[j, at, :] = jnp.concatenate([ga[a[0], rows, 0:768], ga[a[1], rows, 0:768]], axis=0)
            w4[2 + j, at, :] = jnp.concatenate([gb[b[0], rows, :], gb[b[1], rows, :]], axis=0)
        smalls[at, :] = jnp.concatenate([ga[a[0], 0:24, 768:896], ga[a[1], 0:24, 768:896]], axis=0)
        return 0

    lax.fori_loop(0, 16, assemble, 0)
    eye = (iota((128, 128), 0) == iota((128, 128), 1)).astype(BF16)
    across = mm(eye, smalls[...], NT)
    hidden = tokens[...].astype(F32)
    scale = lax.rsqrt(jnp.mean(hidden * hidden, axis=-1, keepdims=True) + EPSILON)
    first[...] = (hidden * scale * across[12:13]).astype(BF16)

    def project(i, _):
        j, at = i // 2, pl.ds(pl.multiple_of((i % 2) * 256, 256), 256)
        qkv[j, at, :] = mm(first[at, :], w4[j]).astype(BF16)
        return 0

    lax.fori_loop(0, 6, project, 0)

    def dispatch(stage, landing, sends, recvs, j, got):
        if got:
            es, ys = (e + j % 4) % 4, (y + j // 4) % 2
            at = landing.at[ys, es]
            return remote(stage.at[0], at, sends.at[j], recvs.at[ys * 4 + es], device(x, c, z, 1 - y))
        ed, yd = (e + j % 4) % 4, (y + j // 4) % 2
        return remote(
            stage.at[ed], landing.at[y, e], sends.at[j], recvs.at[y * 4 + e], (ed, z * 2 + yd)
        )

    both = p0[...] + p1[...]
    for ed in range(4):
        stage_c[ed] = mm(both[ed * CAP : ed * CAP + CAP], cot[...]).astype(BF16)
    for j in (7, 5, 6, 4, 3, 1, 2):
        dispatch(stage_c, rows_c, sd, rd, j, False).start()
    own_c = pltpu.make_async_copy(stage_c.at[e], rows_c.at[y, e], own.at[0])
    own_c.start()

    lane = iota((256, 128), 1)

    def heads(pair, _):
        cols = pl.ds(pl.multiple_of(pair * 128, 128), 128)
        for t in range(2):
            rows = slice(256 * t, 256 * t + 256)
            outs = []
            for hh in range(2):
                q = jnp.where((lane < 64) == (hh == 0), qkv[0, rows, cols] * BF16(0.125), BF16(0))
                s = mm(q, qkv[1, :, cols], NT) + bias[rows]
                ex = jnp.exp(s - jnp.max(s, axis=-1, keepdims=True))
                p = (ex * (1.0 / jnp.sum(ex, axis=-1, keepdims=True))).astype(BF16)
                probs[2 * pair + hh, rows, :] = p
                outs.append(mm(p, qkv[2, :, cols]))
            mixed[rows, cols] = jnp.where(lane < 64, outs[0], outs[1]).astype(BF16)
        return 0

    lax.fori_loop(0, 2, heads, 0)
    serve(0, 1)
    serve(1, 1)
    lax.fori_loop(2, 4, heads, 0)
    serve(2, 1)
    lax.fori_loop(4, 6, heads, 0)
    serve(0, 2)
    serve(1, 2)

    r_c = routes[...]
    lanes = iota((512, 128), 1)
    named_c = ((lanes == r_c[:, 0:1]) | (lanes == r_c[:, 1:2])).astype(BF16)
    lower = (iota((512, 512), 1) < iota((512, 512), 0)).astype(BF16)
    count = mm(lower, named_c) + lanes.astype(F32) * CAP
    for t in range(2):
        rows = slice(256 * t, 256 * t + 256)
        after = tokens[rows].astype(F32) + mm(mixed[rows], w4[3])
        x1[rows] = after
        scale = lax.rsqrt(jnp.mean(after * after, axis=-1, keepdims=True) + EPSILON)
        second[rows] = (after * scale * across[13:14]).astype(BF16)
        score = mm(second[rows], smalls[...])
        r0, r1_ = r_c[rows, 0:1], r_c[rows, 1:2]
        logits = score[:, 0:8] + prev[rows]
        lane8 = iota((256, 8), 1)
        picked = [jnp.sum(jnp.where(lane8 == r, logits, 0.0), axis=-1, keepdims=True) for r in (r0, r1_)]
        g0 = jax.nn.sigmoid(picked[0] - picked[1])
        values = [g0, 1.0 - g0]
        for m in range(2):
            diff = score[:, 8 + 2 * m : 9 + 2 * m] - score[:, 9 + 2 * m : 10 + 2 * m]
            values += [jax.nn.sigmoid(diff), jax.nn.sigmoid(-diff)]
        for r in (r0, r1_):
            spot = jnp.sum(jnp.where(lane == r, count[rows], 0.0), axis=-1, keepdims=True)
            values.append(jnp.where(r < 4, spot, -1.0))
        out = jnp.zeros((256, 128), F32)
        for i, v in enumerate(values):
            out = jnp.where(lane == i, v, out)
        scal[rows] = out

    parts = []
    for k in range(2):
        hi, mid, lo = split3(scal[:, k : k + 1])
        zero = BF16(0)
        parts.append(
            jnp.where(lanes == 0, hi, zero) + jnp.where(lanes == 1, mid, zero) + jnp.where(lanes == 2, lo, zero)
        )
    for ed in range(4):
        rows = slice(ed * CAP, ed * CAP + CAP)
        stage_x[ed, :, 0:768] = mm(p0[rows] + p1[rows], second[...]).astype(BF16)
        stage_x[ed, :, 768:896] = (mm(p0[rows], parts[0]) + mm(p1[rows], parts[1])).astype(BF16)
    for j in (7, 5, 6, 4, 3, 1, 2):
        dispatch(stage_x, rows_x, sx, rx, j, False).start()
    own_x = pltpu.make_async_copy(stage_x.at[e], rows_x.at[y, e], own.at[1])
    own_x.start()
    serve(2, 2)
    for k in range(3):
        serve(k, 3)
    own_gu.wait()
    own_dn.wait()
    own_c.wait()
    own_x.wait()
    put_y().wait_send()
    for j in range(1, 8):
        for args in ((stage_c, rows_c, sd, rd), (stage_x, rows_x, sx, rx)):
            dispatch(*args, j, False).wait_send()
            dispatch(*args, j, True).wait_recv()
    for u in range(2):
        for zb in range(4):
            put_1(u, zb).wait_send()
            put_2(u, 0, zb).wait_send()
            put_2(u, 1, zb).wait_send()
            pl.when((zb >= z) & (z > 0))(lambda: put_z(u, zb, -1).wait_send())
            pl.when((zb <= z) & (z < 3))(lambda: put_z(u, zb, 1).wait_send())
        for hh in range(2):
            put_c(u, hh).wait_send()
    for k in range(3):
        for zb in range(4):
            pl.when((zb >= z) & (z > 0))(lambda: put_e(k, zb, -1).wait_send())
            pl.when((zb <= z) & (z < 3))(lambda: put_e(k, zb, 1).wait_send())


def vm():
    return pl.BlockSpec(memory_space=pltpu.VMEM)


def hbm():
    return pl.BlockSpec(memory_space=pl.ANY)


def forward_call(tokens, cot, prev, routes, block_ids, unit_a, unit_b, gu_in, dn_in):
    out = lambda *shape, t=BF16: jax.ShapeDtypeStruct(shape, t)
    dma = lambda n: pltpu.SemaphoreType.DMA((n,))
    return pl.pallas_call(
        forward_kernel,
        out_shape=(
            out(2, 768, 1024), out(1024, 768), out(2, 4, CAP, 896), out(2, 4, CAP, 768),
            out(4, 768, 768), out(768, 128), out(12, 512, 512), out(3, 512, 768), out(512, 768),
            out(512, 768, t=F32), out(512, 768), out(512, 128, t=F32),
        ),
        in_specs=[vm()] * 9 + [hbm()] * 2,
        out_specs=(hbm(),) * 4 + (vm(),) * 8,
        scratch_shapes=[
            pltpu.VMEM((32, 48, 896), BF16), pltpu.VMEM((32, 48, 768), BF16), pltpu.VMEM((512, 512), F32),
            pltpu.VMEM((512, 768), BF16), pltpu.VMEM((640, 512), BF16), pltpu.VMEM((640, 512), BF16),
            pltpu.VMEM((4, CAP, 768), BF16), pltpu.VMEM((4, CAP, 896), BF16),
            dma(4), dma(16), dma(8), dma(8), dma(8), dma(16), dma(16), dma(4), dma(4), dma(24), dma(12),
            dma(1), dma(1), dma(8), dma(8), dma(8), dma(8), dma(2),
        ],
        compiler_params=pltpu.CompilerParams(has_side_effects=True, vmem_limit_bytes=60 * 2**20),
        name="forward",
    )(tokens, cot, prev, routes, routes.T, block_ids.reshape(512, 1), block_ids, unit_a, unit_b, gu_in, dn_in)


def packed(norm_gain, attn_in, attn_out, router, const_vec, expert_gu, expert_down):
    small = jnp.concatenate([router[0], norm_gain[0].T, const_vec[0].T], axis=1)
    small = jnp.pad(small, ((0, 24), (0, 112)))
    unit_a = jnp.concatenate([attn_in[0, 0:2].reshape(48, 768), small], axis=1)
    unit_b = jnp.concatenate([attn_in[0, 2], attn_out[0]], axis=0)
    gu = expert_gu[0, 0].reshape(2, 96, 4, 2, 256).transpose(3, 0, 1, 2, 4).reshape(2, 2, 96, 1024)
    return unit_a, unit_b, gu, expert_down[0, 0]


def backward_kernel(
    tokens, cot, routes, mixed, x1, second, scal, smalls,
    qkv, gu_in, dn_in, rows_x, rows_c, w4, probs,
    out, in_grad, gate_grad, small_sum, unit_a, unit_b, gu_out, dn_out,
    gu, dn, wo, rx, rc, deo, act, dgate, dup, turned, ggu, gdn, rgu, rdn, land_b, land_e, pbuf,
    c_in, two_in, one_in, z_in, y_in, sm, sm_in,
    loc, sb, rb, sv, rv, sg, rg, sy, ry, sc_, rc_, s2, r2, s1, r1, sz, rz, ss, rs, lp, lq, own,
):
    x, c, z, y = where_am_i()
    e = x * 2 + c

    def inside(v):
        return (v >= 0) & (v <= 3)

    loads = [(rows_x, rx), (gu_in, gu), (rows_c, rc), (dn_in, dn), (w4.at[3], wo)]
    loads = [pltpu.make_async_copy(a, b, loc.at[i]) for i, (a, b) in enumerate(loads)]
    for load in loads:
        load.start()
    for load in (loads[0], loads[2]):
        load.wait()

    def scaled(i, _):
        g = jnp.sum(rx[i, :, 768:896].astype(F32), axis=-1, keepdims=True)
        deo[pl.ds(pl.multiple_of(i * CAP, 32), CAP), :] = (g * rc[i].astype(F32)).astype(BF16)
        return 0

    lax.fori_loop(0, 8, scaled, 0)
    for t in range(5):
        both = rx.reshape(1280, 896)[256 * t : 256 * t + 256, 0:768]
        turned[:, 256 * t : 256 * t + 256] = both.T
    loads[1].wait()
    loads[3].wait()
    dgate2, dup2 = dgate.reshape(1536, 1024), dup.reshape(1536, 1024)
    rx2, rc2 = rx.reshape(1280, 896), rc.reshape(1280, 768)

    def hidden_part(i, _):
        at = pl.ds(pl.multiple_of(i * 320, 64), 320)
        for f in range(2):
            cols = slice(512 * f, 512 * f + 512)
            rows = rx2[at, 0:768]
            u, w = mm(rows, gu[0, :, cols]), mm(rows, gu[1, :, cols])
            dact = mm(deo[at, :], dn[cols, :], NT)
            sig = jax.nn.sigmoid(u)
            silu = u * sig
            act[at, cols] = (silu * w).astype(BF16)
            dgate2[at, cols] = (dact * w * sig * (1.0 + u * (1.0 - sig))).astype(BF16)
            dup2[at, cols] = (dact * silu).astype(BF16)
        return 0

    lax.fori_loop(0, 4, hidden_part, 0)

    def grad_block(zb):
        for yo in range(2):
            rows = pl.ds(pl.multiple_of(zb * 192 + yo * 96, 32), 96)
            for f in range(2):
                cols = slice(512 * f, 512 * f + 512)
                ggu[zb, yo, 0, :, cols] = mm(turned[rows, :], dgate2[0:1280, cols]).astype(BF16)
                ggu[zb, yo, 1, :, cols] = mm(turned[rows, :], dup2[0:1280, cols]).astype(BF16)
        cols = pl.ds(pl.multiple_of(zb * 256, 256), 256)
        gdn[zb] = mm(act[0:1280, cols], deo[...], TN).astype(BF16)

    def put_g(zb, k, up):
        to = device(x, c, jnp.clip(z + (1 if up else -1), 0, 3), y)
        land = zb if up else jnp.where(zb == z - 1, 4, zb)
        src, dst = (gdn.at[zb], rdn.at[land]) if k == 2 else (ggu.at[zb, k], rgu.at[land, k])
        return remote(src, dst, sg.at[zb * 3 + k], rg.at[land * 3 + k], to)

    def got_g(land, k):
        src, dst = (gdn.at[0], rdn.at[land]) if k == 2 else (ggu.at[0, k], rgu.at[land, k])
        return remote(src, dst, sg.at[k], rg.at[land * 3 + k], device(x, c, z, 1 - y))

    def first_send(zb):
        for k in range(3):
            pl.when((z == 0) & (zb > 0))(lambda: put_g(zb, k, True).start())
            pl.when((z == 3) & (zb < 3))(lambda: put_g(zb, k, False).start())

    def add_block(zb, land, k):
        if k == 2:
            gdn[zb] = (gdn[zb].astype(F32) + rdn[land].astype(F32)).astype(BF16)
        else:
            ggu[zb, k] = (ggu[zb, k].astype(F32) + rgu[land, k].astype(F32)).astype(BF16)

    def serve(far, k):
        for up in (True, False):
            zb = 3 - far if up else far
            middle = ((z >= 1) & (zb > z)) if up else ((z <= 2) & (zb < z))

            @pl.when(middle)
            def _():
                got_g(zb, k).wait_recv()
                add_block(zb, zb, k)
                put_g(zb, k, up).start()

    def nth(n):
        pick = lambda vals: vals[n]
        return jnp.where(
            z == 0, pick((3, 2, 1, 0)),
            jnp.where(z == 1, pick((3, 2, 0, 1)), jnp.where(z == 2, pick((0, 1, 3, 2)), pick((0, 1, 2, 3)))),
        )

    def make(n, _):
        zb = nth_dynamic(n)
        grad_block(zb)
        first_send(zb)
        return 0

    def nth_dynamic(n):
        return jnp.where(n == 0, nth(0), jnp.where(n == 1, nth(1), jnp.where(n == 2, nth(2), nth(3))))

    lax.fori_loop(0, 1, make, 0)

    def returned(stage, landing, sends, recvs, b, got=False):
        ys, es = b // 4, b % 4
        if got:
            return remote(stage.at[0], landing.at[ys, es], sends.at[b], recvs.at[b], device(x, c, z, 1 - y))
        return remote(stage.at[b], landing.at[y, e], sends.at[b], recvs.at[y * 4 + e], (es, z * 2 + ys))

    def back(stage, landing, sends, recvs, b, i):
        mine = b == y * 4 + e

        @pl.when(mine)
        def _():
            pltpu.make_async_copy(stage.at[b], landing.at[y, e], own.at[i]).start()

        @pl.when(jnp.logical_not(mine))
        def _():
            returned(stage, landing, sends, recvs, b).start()

    def row_part(i, _):
        at = pl.ds(pl.multiple_of(i * 320, 64), 320)
        dbuf = mm(dgate2[at, :], gu[0], NT) + mm(dup2[at, :], gu[1], NT)
        eo = mm(act[at, :], dn[...])
        dg = jnp.sum(eo * rc2[at, :].astype(F32), axis=-1, keepdims=True)
        lane = iota((320, 128), 1)
        hi, mid, lo = split3(dg)
        zero = BF16(0)
        more = jnp.where(lane == 0, hi, zero) + jnp.where(lane == 1, mid, zero) + jnp.where(lane == 2, lo, zero)
        rx2[at, 0:768] = dbuf.astype(BF16)
        rx2[at, 768:896] = more
        rc2[at, :] = eo.astype(BF16)
        for b in (2 * i, 2 * i + 1):
            back(rx, land_b, sb, rb, b, 0)
        return 0

    lax.fori_loop(0, 4, row_part, 0)
    weights = [(w4.at[0], gu.at[0, :, pl.ds(0, 768)]), (w4.at[1], gu.at[1, :, pl.ds(0, 768)]), (w4.at[2], dn.at[pl.ds(0, 768)])]
    weights = [pltpu.make_async_copy(a, b, loc.at[5 + i]) for i, (a, b) in enumerate(weights)]
    for load in weights:
        load.start()
    lax.fori_loop(1, 4, make, 0)
    for b in range(8):
        back(rc, land_e, sv, rv, b, 1)

    def head_load(head, half):
        return pltpu.make_async_copy(probs.at[head], pbuf.at[half], lp.at[half])

    def spare(pair):
        return pl.ds(pl.multiple_of(768 + 128 * (pair % 2), 128), 128)

    def pair_load(pair):
        cols = pl.ds(pl.multiple_of(pair * 128, 128), 128)
        return pltpu.make_async_copy(qkv.at[:, cols], act.at[:, spare(pair)], lq.at[pair % 2])

    head_load(0, 0).start()
    pair_load(0).start()
    eye = (iota((128, 128), 0) == iota((128, 128), 1)).astype(BF16)
    across = mm(eye, smalls[...], NT)
    turned[:, 512:1024] = mixed[...].T
    scale_one = []
    for t in range(2):
        rows = slice(256 * t, 256 * t + 256)
        hidden = tokens[rows].astype(F32)
        scale_one.append(lax.rsqrt(jnp.mean(hidden * hidden, axis=-1, keepdims=True) + EPSILON))
        turned[:, rows] = (hidden * scale_one[t] * across[12:13]).astype(BF16).T
    loads[4].wait()
    serve(0, 0)

    for b in range(8):
        mine = b == y * 4 + e

        @pl.when(mine)
        def _():
            pltpu.make_async_copy(rx.at[b], land_b.at[y, e], own.at[0]).wait()

        @pl.when(jnp.logical_not(mine))
        def _():
            returned(rx, land_b, sb, rb, b, True).wait_recv()

    lane = iota((256, 128), 1)
    total = jnp.zeros((128, 768), F32)
    gain_two = jnp.zeros((1, 768), F32)
    for t in range(2):
        rows = slice(256 * t, 256 * t + 256)
        at = lambda i: scal[rows, i : i + 1]
        g = (at(0), at(1))
        a = ((at(2), at(3)), (at(4), at(5)))
        r = (routes[rows, 0:1], routes[rows, 1:2])
        place = [(iota((256, 640), 1) == at(6 + k).astype(jnp.int32)).astype(BF16) for k in range(2)]
        dsec = jnp.zeros((256, 768), F32)
        dg = [jnp.zeros((256, 1), F32)] * 2
        for yh in range(2):
            got = land_b[yh].reshape(640, 896)
            dsec = dsec + mm(place[0] + place[1], got[:, 0:768])
            for k in range(2):
                dg[k] = dg[k] + jnp.sum(mm(place[k], got[:, 768:896]), axis=-1, keepdims=True)
        dx2 = cot[rows].astype(F32)
        sec = second[rows].astype(F32)
        dot_s = jnp.sum(dx2 * sec, axis=-1, keepdims=True)
        coef = jnp.zeros((256, 1), F32)
        dz = jnp.zeros((256, 128), F32)
        for k in range(2):
            dg[k] = dg[k] + jnp.where(r[k] == 5, dot_s, 0.0)
            coef = coef + jnp.where(r[k] == 5, g[k], 0.0)
        const = jnp.zeros((256, 128), F32)
        for m in range(2):
            dot_v = jnp.sum(dx2 * across[14 + m : 15 + m], axis=-1, keepdims=True)
            weight = jnp.zeros((256, 1), F32)
            for k in range(2):
                chosen = r[k] == 6 + m
                dg[k] = dg[k] + jnp.where(chosen, a[m][0] * dot_s + a[m][1] * dot_v, 0.0)
                weight = weight + jnp.where(chosen, g[k], 0.0)
            coef = coef + a[m][0] * weight
            const = const + jnp.where(lane == 14 + m, a[m][1] * weight, 0.0)
            da = (weight * dot_s, weight * dot_v)
            mean = a[m][0] * da[0] + a[m][1] * da[1]
            for i in range(2):
                dz = jnp.where(lane == 8 + 2 * m + i, a[m][i] * (da[i] - mean), dz)
        diff = g[0] * g[1] * (dg[0] - dg[1])
        dz = dz + jnp.where(lane == r[0], diff, 0.0) - jnp.where(lane == r[1], diff, 0.0)
        gate_grad[rows, :] = dz[:, 0:8]
        hi, mid, _ = split3(dz)
        dsec = dsec + coef * dx2 + mm(hi, smalls[...], NT) + mm(mid, smalls[...], NT)
        total = total + mm(hi, second[rows], TN) + mm(mid, second[rows], TN)
        hi, mid, _ = split3(const)
        total = total + mm(hi, cot[rows], TN) + mm(mid, cot[rows], TN)
        after = x1[rows]
        scale = lax.rsqrt(jnp.mean(after * after, axis=-1, keepdims=True) + EPSILON)
        normal = after * scale
        gain_two = gain_two + jnp.sum(dsec * normal, axis=0, keepdims=True)
        lift = dsec * across[13:14]
        dx1 = dx2 + scale * (lift - normal * jnp.mean(lift * normal, axis=-1, keepdims=True))
        in_grad[rows, :] = dx1
        deo[rows, :] = mm(dx1.astype(BF16), wo[...], NT).astype(BF16)
    row16 = iota((16, 768), 0)
    sm[...] = total[0:16] + jnp.where(row16 == 13, gain_two, 0.0)
    serve(0, 1)
    serve(0, 2)

    def scatter(stage, place_of, j, left, right):
        def some(ee, _):
            rows = pl.ds(pl.multiple_of(ee * 192, 64), 192)
            got = mm(turned[rows, left], right()).astype(BF16)
            for s in range(8):
                stage[place_of(ee // 2, ee % 2, s // 2, s % 2), 24 * j : 24 * j + 24, 0:768] = got[24 * s : 24 * s + 24]
            return 0

        lax.fori_loop(0, 4, some, 0)

    place_a = lambda xx, cc, zz, yy: ((cc * 2 + xx) * 2 + yy) * 4 + zz
    place_b = lambda xx, cc, zz, yy: ((cc * 2 + yy) * 2 + xx) * 4 + zz
    scatter(dup, place_b, 1, slice(512, 1024), lambda: in_grad[...].astype(BF16))

    lane5 = iota((512, 128), 1)

    def heads(pair, _):
        cols = pl.ds(pl.multiple_of(pair * 128, 128), 128)
        pair_load(pair).wait()
        pl.when(pair < 5)(lambda: pair_load(pair + 1).start())
        now = spare(pair)
        grads = []
        for hh in range(2):
            head_load(2 * pair + hh, hh).wait()
            if hh == 0:
                head_load(2 * pair + 1, 1).start()
            else:
                pl.when(pair < 5)(lambda: head_load(2 * pair + 2, 0).start())
            mine = (lane5 < 64) == (hh == 0)
            do = jnp.where(mine, deo[0:512, cols], BF16(0))
            inner = jnp.sum(do.astype(F32) * mixed[:, cols].astype(F32), axis=-1, keepdims=True)
            dq, dk, dv = [], jnp.zeros((512, 128), F32), jnp.zeros((512, 128), F32)
            for t in range(2):
                rows = slice(256 * t, 256 * t + 256)
                p = pbuf[hh, rows, :]
                ds = (p.astype(F32) * (mm(do[rows], act[1024:1536, now], NT) - inner[rows])).astype(BF16)
                dq.append(mm(ds, act[512:1024, now]))
                dk = dk + mm(ds, act[rows, now], TN)
                dv = dv + mm(p, deo[rows, cols], TN)
            grads.append((jnp.concatenate(dq, axis=0) * 0.125, dk * 0.125, dv))
        for j in range(3):
            act[512 * j : 512 * j + 512, cols] = jnp.where(lane5 < 64, grads[0][j], grads[1][j]).astype(BF16)
        return 0

    lax.fori_loop(0, 2, heads, 0)
    serve(1, 0)
    lax.fori_loop(2, 4, heads, 0)
    serve(1, 1)
    lax.fori_loop(4, 6, heads, 0)
    serve(1, 2)
    for load in weights:
        load.wait()
    for j, (stage, place_of, i) in enumerate(((dgate, place_a, 0), (dgate, place_a, 1), (dup, place_b, 0))):
        scatter(stage, place_of, i, slice(0, 512), lambda: act[512 * j : 512 * j + 512, 0:768])

    units = (
        (dgate, y, x, lambda: device(x, c, z, 1 - y), lambda: device(1 - x, c, z, y)),
        (dup, x, y, lambda: device(1 - x, c, z, y), lambda: device(x, c, z, 1 - y)),
    )
    wide = pl.ds(0, 768)

    def put_c(u, hh):
        src = units[u][0].at[pl.ds(((1 - c) * 2 + hh) * 8, 8), :, wide]
        return remote(src, c_in.at[u, hh], sc_.at[u * 2 + hh], rc_.at[u * 2 + hh], device(x, 1 - c, z, y))

    def put_2(u, hh):
        g, h1, h2, _, to2 = units[u]
        src = g.at[pl.ds(((c * 2 + 1 - h2) * 2 + hh) * 4, 4), :, wide]
        return remote(src, two_in.at[u, hh], s2.at[u * 2 + hh], r2.at[u * 2 + hh], to2())

    def put_1(u):
        g, h1, h2, to1, _ = units[u]
        src = g.at[pl.ds(((c * 2 + h2) * 2 + 1 - h1) * 4, 4), :, wide]
        return remote(src, one_in.at[u], s1.at[u], r1.at[u], to1())

    def put_z(u, zb, up):
        g, h1, h2, _, _ = units[u]
        src = g.at[((c * 2 + h2) * 2 + h1) * 4 + zb, :, wide]
        land = zb if up else jnp.where(zb == z - 1, 4, zb)
        to = device(x, c, jnp.clip(z + (1 if up else -1), 0, 3), y)
        return remote(src, z_in.at[u, land], sz.at[u * 4 + zb], rz.at[u * 5 + land], to)

    def got_z(u, land):
        src = units[u][0].at[0, :, wide]
        return remote(src, z_in.at[u, land], sz.at[u * 4], rz.at[u * 5 + land], device(x, c, z, 1 - y))

    def gather_in(g, at, n, other):
        def one(i, _):
            g[at + i, :, 0:768] = (g[at + i, :, 0:768].astype(F32) + other(i).astype(F32)).astype(BF16)
            return 0

        lax.fori_loop(0, n, one, 0)

    for u in range(2):
        h2 = units[u][2]
        put_c(u, 1 - h2).start()
        put_c(u, h2).start()

    gain_one = jnp.zeros((1, 768), F32)
    for t in range(2):
        rows = slice(256 * t, 256 * t + 256)
        dfirst = mm(act[256 * t : 256 * t + 256, 0:768], gu[0, :, 0:768], NT)
        dfirst = dfirst + mm(act[512 + 256 * t : 768 + 256 * t, 0:768], gu[1, :, 0:768], NT)
        dfirst = dfirst + mm(act[1024 + 256 * t : 1280 + 256 * t, 0:768], dn[0:768, :], NT)
        scale = scale_one[t]
        normal = tokens[rows].astype(F32) * scale
        gain_one = gain_one + jnp.sum(dfirst * normal, axis=0, keepdims=True)
        lift = dfirst * across[12:13]
        in_grad[rows, :] = in_grad[rows, :] + scale * (lift - normal * jnp.mean(lift * normal, axis=-1, keepdims=True))
    sm[...] = sm[...] + jnp.where(row16 == 12, gain_one, 0.0)

    def small_step(i, to):
        return remote(sm.at[...], sm_in.at[i], ss.at[i], rs.at[i], to)

    small_step(0, device(x, 1 - c, z, y)).start()
    for u in range(2):
        g, h1, h2, _, _ = units[u]
        put_c(u, 1 - h2).wait_recv()
        for hh in (1 - h1, h1):
            gather_in(g, ((c * 2 + 1 - h2) * 2 + hh) * 4, 4, lambda i: c_in[u, 1 - h2, hh * 4 + i])
            put_2(u, hh).start()
    small_step(0, device(x, 1 - c, z, y)).wait()
    sm[...] = sm[...] + sm_in[0]
    small_step(1, device(1 - x, c, z, y)).start()
    for u in range(2):
        g, h1, h2, _, _ = units[u]
        put_c(u, h2).wait_recv()
        gather_in(g, (c * 2 + h2) * 8, 8, lambda i: c_in[u, h2, i])
    small_step(1, device(1 - x, c, z, y)).wait()
    sm[...] = sm[...] + sm_in[1]
    small_step(2, device(x, c, z, 1 - y)).start()
    for u in range(2):
        g, h1, h2, _, _ = units[u]
        put_2(u, 1 - h1).wait_recv()
        gather_in(g, ((c * 2 + h2) * 2 + 1 - h1) * 4, 4, lambda i: two_in[u, 1 - h1, i])
        put_1(u).start()
    for u in range(2):
        g, h1, h2, _, _ = units[u]
        put_2(u, h1).wait_recv()
        gather_in(g, ((c * 2 + h2) * 2 + h1) * 4, 4, lambda i: two_in[u, h1, i])
    small_step(2, device(x, c, z, 1 - y)).wait()
    sm[...] = sm[...] + sm_in[2]

    def small_z(way, got=False):
        zt = lax.rem(z + way, 4)
        if got:
            zt = lax.rem(z - way + 4, 4)
            return remote(sm.at[...], sm_in.at[3 + zt], ss.at[2 + way], rs.at[3 + zt], device(x, c, zt, y))
        return remote(sm.at[...], sm_in.at[3 + z], ss.at[2 + way], rs.at[3 + z], device(x, c, zt, y))

    for way in (1, 2, 3):
        small_z(way).start()

    for b in range(8):
        mine = b == y * 4 + e

        @pl.when(mine)
        def _():
            pltpu.make_async_copy(rc.at[b], land_e.at[y, e], own.at[1]).wait()

        @pl.when(jnp.logical_not(mine))
        def _():
            returned(rc, land_e, sv, rv, b, True).wait_recv()

    for t in range(2):
        rows = slice(256 * t, 256 * t + 256)
        at = lambda i: scal[rows, i : i + 1]
        g = (at(0), at(1))
        a = ((at(2), at(3)), (at(4), at(5)))
        r = (routes[rows, 0:1], routes[rows, 1:2])
        result = x1[rows]
        coef = jnp.zeros((256, 1), F32)
        for k in range(2):
            place = (iota((256, 640), 1) == at(6 + k).astype(jnp.int32)).astype(BF16)
            branch = mm(place, land_e[0].reshape(640, 768)) + mm(place, land_e[1].reshape(640, 768))
            result = result + g[k] * branch
            coef = coef + jnp.where(r[k] == 5, g[k], 0.0)
        for m in range(2):
            weight = jnp.zeros((256, 1), F32)
            for k in range(2):
                weight = weight + jnp.where(r[k] == 6 + m, g[k], 0.0)
            coef = coef + a[m][0] * weight
            result = result + a[m][1] * weight * across[14 + m : 15 + m]
        result = result + coef * second[rows].astype(F32)
        out[rows, :] = result.astype(BF16)

    for u in range(2):
        g, h1, h2, _, _ = units[u]
        put_1(u).wait_recv()
        base = ((c * 2 + h2) * 2 + h1) * 4
        gather_in(g, base, 4, lambda i: one_in[u, i])
        for zb in (1, 2, 3):
            pl.when((z == 0))(lambda: put_z(u, 4 - zb, True).start())
            pl.when((z == 3))(lambda: put_z(u, zb - 1, False).start())
    for far in range(2):
        for u in range(2):
            g, h1, h2, _, _ = units[u]
            base = ((c * 2 + h2) * 2 + h1) * 4
            for up in (True, False):
                zb = 3 - far if up else far
                middle = ((z >= 1) & (zb > z)) if up else ((z <= 2) & (zb < z))

                @pl.when(middle)
                def _():
                    got_z(u, zb).wait_recv()
                    gather_in(g, base + zb, 1, lambda i: z_in[u, zb])
                    put_z(u, zb, up).start()

    def final(k):
        @pl.when(z > 0)
        def _():
            got_g(z, k).wait_recv()
            add_block(z, z, k)

        @pl.when(z < 3)
        def _():
            got_g(4, k).wait_recv()
            add_block(z, 4, k)

    def swap():
        return remote(ggu.at[z, 1 - y], y_in.at[...], sy.at[0], ry.at[0], device(x, c, z, 1 - y))

    for k in range(3):
        final(k)
    swap().start()
    dn_out[...] = gdn[z].astype(F32)
    for way in (1, 2, 3):
        small_z(way, True).wait_recv()
    result = sm[...]
    for way in (1, 2, 3):
        result = result + sm_in[3 + lax.rem(z + way, 4)]
    small_sum[...] = result
    for u, ref in ((0, unit_a), (1, unit_b)):
        g, h1, h2, _, _ = units[u]
        at = ((c * 2 + h2) * 2 + h1) * 4 + z
        ref[...] = g[at, :, 0:768].astype(F32)

        @pl.when(z > 0)
        def _():
            got_z(u, z).wait_recv()
            ref[...] = ref[...] + z_in[u, z].astype(F32)

        @pl.when(z < 3)
        def _():
            got_z(u, 4).wait_recv()
            ref[...] = ref[...] + z_in[u, 4].astype(F32)

    for half in range(2):
        if half == 1:
            swap().wait_recv()
        for q in range(4):
            parity = y if half == 0 else 1 - y
            cols = pl.ds(pl.multiple_of((2 * q + parity) * 256, 256), 256)
            for i in range(2):
                block = ggu[z, y, i, :, 256 * q : 256 * q + 256] if half == 0 else y_in[i, :, 256 * q : 256 * q + 256]
                gu_out[i, :, cols] = block.astype(F32)
    swap().wait_send()
    for way in (1, 2, 3):
        small_z(way).wait_send()
    for b in range(8):

        @pl.when(b != y * 4 + e)
        def _():
            returned(rx, land_b, sb, rb, b).wait_send()
            returned(rc, land_e, sv, rv, b).wait_send()

    for zb in range(4):
        for k in range(3):
            pl.when(zb > z)(lambda: put_g(zb, k, True).wait_send())
            pl.when(zb < z)(lambda: put_g(zb, k, False).wait_send())
        for u in range(2):
            pl.when(zb > z)(lambda: put_z(u, zb, True).wait_send())
            pl.when(zb < z)(lambda: put_z(u, zb, False).wait_send())
    for u in range(2):
        put_1(u).wait_send()
        for hh in range(2):
            put_c(u, hh).wait_send()
            put_2(u, hh).wait_send()


def backward_call(tokens, cot, routes, kept):
    gu, dn, rows_x, rows_c, w4, smalls, probs, qkv, mixed, x1, second, scal = kept
    out = lambda *shape, t=F32: jax.ShapeDtypeStruct(shape, t)
    dma = lambda n: pltpu.SemaphoreType.DMA((n,))
    mem = lambda *shape, t=BF16: pltpu.VMEM(shape, t)
    return pl.pallas_call(
        backward_kernel,
        out_shape=(
            out(512, 768, t=BF16), out(512, 768), out(512, 8), out(16, 768), out(48, 768), out(48, 768),
            out(2, 96, 2048), out(256, 768),
        ),
        in_specs=[vm()] * 8 + [hbm()] * 7,
        out_specs=(vm(),) * 8,
        scratch_shapes=[
            mem(2, 768, 1024), mem(1024, 768), mem(768, 768), mem(8, CAP, 896), mem(8, CAP, 768),
            mem(1280, 768), mem(1536, 1024), mem(32, 48, 1024), mem(32, 48, 1024), mem(768, 1280),
            mem(4, 2, 2, 96, 1024), mem(4, 256, 768), mem(5, 2, 2, 96, 1024), mem(5, 256, 768),
            mem(2, 4, CAP, 896), mem(2, 4, CAP, 768), mem(2, 512, 512),
            mem(2, 2, 8, 48, 768), mem(2, 2, 4, 48, 768), mem(2, 4, 48, 768), mem(2, 5, 48, 768),
            mem(2, 96, 1024), mem(16, 768, t=F32), mem(7, 16, 768, t=F32),
            dma(8), dma(8), dma(8), dma(8), dma(8), dma(12), dma(15), dma(1), dma(1), dma(4), dma(4), dma(4), dma(4),
            dma(2), dma(2), dma(8), dma(10), dma(6), dma(7), dma(2), dma(2), dma(2),
        ],
        compiler_params=pltpu.CompilerParams(has_side_effects=True, vmem_limit_bytes=60 * 2**20),
        name="backward",
    )(
        tokens, cot, routes, mixed, x1, second, scal, smalls,
        qkv.reshape(1536, 768), gu, dn, rows_x.reshape(8, CAP, 896), rows_c.reshape(8, CAP, 768), w4, probs,
    )


def finished(outs):
    result, in_grad, gate_grad, small, unit_a, unit_b, gu, dn = outs
    d = lax.axis_index("expert") * lax.axis_size("shard") + lax.axis_index("shard")
    mine = lax.dynamic_slice(small, (0, d * 24), (16, 24))
    attn_in = jnp.stack([unit_a[0:24], unit_a[24:48], unit_b[0:24]])[None]
    return (
        result, in_grad, gate_grad, mine[None, 12:14], attn_in, unit_b[None, 24:48],
        mine[0:12].T[None], mine[None, 14:16], gu[None, None], dn[None, None],
    )


def small_body(tokens, gate_input, routes, block_ids, cotangent, norm_gain, attn_in, attn_out, router, const_vec, expert_gu, expert_down):
    ua, ub, gu, dn = packed(norm_gain, attn_in, attn_out, router, const_vec, expert_gu, expert_down)
    kept = forward_call(tokens, cotangent, gate_input, routes, block_ids, ua, ub, gu, dn)
    return finished(backward_call(tokens, cotangent, routes, kept))


LAYERS = 1
HIGHEST = lax.Precision.HIGHEST


def normed(values):
    inv_scale = lax.rsqrt(jnp.mean(values * values, axis=-1, keepdims=True) + EPSILON)
    return (values * inv_scale, inv_scale)


def norm_back(upstream, normal, inv_scale):
    return inv_scale * (upstream - normal * jnp.mean(upstream * normal, axis=-1, keepdims=True))


def slot_table(route_pair, ffn_count, capacity):
    flat_route = route_pair.reshape(-1)
    pair_count = flat_route.shape[0]
    one_hot = (flat_route[:, None] == jnp.arange(ffn_count, dtype=jnp.int32)[None, :]).astype(
        jnp.int32
    )
    earlier = jnp.arange(pair_count)[None, :] < jnp.arange(pair_count)[:, None]
    running = jnp.dot(
        earlier.astype(jnp.bfloat16), one_hot.astype(jnp.bfloat16), preferred_element_type=jnp.float32
    ).astype(jnp.int32)
    position = jnp.sum(running * one_hot, axis=1)
    is_routed = flat_route < ffn_count
    destination = jnp.where(is_routed, flat_route * capacity + position, ffn_count * capacity)
    pair_index = jnp.arange(pair_count, dtype=jnp.int32)
    owner_pair = (
        jnp.zeros((ffn_count * capacity,), jnp.int32).at[destination].set(pair_index, mode="drop")
    )
    filled = (
        jnp.zeros((ffn_count * capacity,), jnp.int32)
        .at[destination]
        .set(jnp.ones_like(pair_index), mode="drop")
    )
    return (destination, is_routed, owner_pair, filled)


def masked_scores(queries, key_rows, allowed):
    raw_scores = (
        jnp.einsum("thd,shd->hts", queries, key_rows, preferred_element_type=jnp.float32) * 0.125
    )
    return jnp.where(allowed[None, :, :], raw_scores, -1e30)


def layer_forward(hidden, previous, route_pair, blocks, dense_set, expert_set):
    w_in, w_out, gain_rows, w_router, vectors = dense_set
    w_gate_up, w_down = expert_set
    tok_count, model_width = hidden.shape
    head_size = model_width // H
    experts = previous.shape[1]
    gain_float = gain_rows.astype(jnp.float32)
    normal_one, scale_one = normed(hidden)
    first_in = (normal_one * gain_float[0]).astype(jnp.bfloat16)
    projected = jnp.einsum(
        "td,jde->jte", first_in, w_in, preferred_element_type=jnp.float32
    ).astype(jnp.bfloat16)
    projected = projected.reshape(3, tok_count, H, head_size)
    queries, key_rows, value_rows = (projected[0], projected[1], projected[2])
    allowed = blocks[None, :] <= blocks[:, None]
    raw_scores = masked_scores(queries, key_rows, allowed)
    row_peak = jnp.max(raw_scores, axis=-1, keepdims=True)
    log_total = row_peak + jnp.log(jnp.sum(jnp.exp(raw_scores - row_peak), axis=-1, keepdims=True))
    attn_probs = jnp.exp(raw_scores - log_total).astype(jnp.bfloat16)
    mixed_heads = jnp.einsum(
        "hts,shd->thd", attn_probs, value_rows, preferred_element_type=jnp.float32
    )
    mixed_heads = mixed_heads.reshape(tok_count, model_width).astype(jnp.bfloat16)
    after_attn = hidden + jnp.dot(mixed_heads, w_out, preferred_element_type=jnp.float32)
    normal_two, scale_two = normed(after_attn)
    second_in = (normal_two * gain_float[1]).astype(jnp.bfloat16)
    second_float = second_in.astype(jnp.float32)
    all_logits = jnp.dot(second_in, w_router, preferred_element_type=jnp.float32)
    logits = all_logits[:, :experts] + previous
    picked = route_pair[:, :, None] == jnp.arange(experts, dtype=jnp.int32)[None, None, :]
    chosen = jnp.sum(jnp.where(picked, logits[:, None, :], 0.0), axis=-1)
    first_gate = jax.nn.sigmoid(chosen[:, 0] - chosen[:, 1])
    gate_pair = jnp.stack([first_gate, 1.0 - first_gate], axis=1)
    const_weights = jax.nn.softmax(all_logits[:, experts:].reshape(tok_count, 2, 2), axis=-1)
    ffn_count = lax.axis_size("expert")
    destination, is_routed, owner_pair, filled = slot_table(route_pair, ffn_count, CAP)
    has_row = filled[:, None] > 0
    send_rows = jnp.where(has_row, second_in[owner_pair // 2], jnp.zeros((), jnp.bfloat16))
    send_rows = send_rows.reshape(ffn_count, CAP, model_width)
    slot_rows = lax.all_to_all(
        send_rows, "expert", split_axis=0, concat_axis=0, tiled=True
    ).reshape(ffn_count * CAP, model_width)
    gate_pre = jnp.dot(slot_rows, w_gate_up[0, 0], preferred_element_type=jnp.float32)
    up_pre = jnp.dot(slot_rows, w_gate_up[0, 1], preferred_element_type=jnp.float32)
    activated = (jax.nn.silu(gate_pre) * up_pre).astype(jnp.bfloat16)
    expert_out = jnp.dot(activated, w_down[0], preferred_element_type=jnp.float32).astype(
        jnp.bfloat16
    )
    expert_out = expert_out.reshape(ffn_count, CAP, model_width)
    returned = lax.all_to_all(
        expert_out, "expert", split_axis=0, concat_axis=0, tiled=True
    ).reshape(ffn_count * CAP, model_width)
    safe_dest = jnp.minimum(destination, ffn_count * CAP - 1)
    ffn_rows = jnp.where(is_routed[:, None], returned[safe_dest].astype(jnp.float32), 0.0)
    ffn_rows = ffn_rows.reshape(tok_count, 2, model_width)
    vector_float = vectors.astype(jnp.float32)
    const_rows = (
        const_weights[:, :, 0:1] * second_float[:, None, :]
        + const_weights[:, :, 1:2] * vector_float[None, :, :]
    )
    pair_out = ffn_rows + jnp.where(
        (route_pair == ffn_count + 1)[:, :, None], second_float[:, None, :], 0.0
    )
    for member in range(2):
        chosen_const = (route_pair == ffn_count + 2 + member)[:, :, None]
        pair_out = pair_out + jnp.where(chosen_const, const_rows[:, member][:, None, :], 0.0)
    result = after_attn + jnp.sum(gate_pair[:, :, None] * pair_out, axis=1)
    kept_state = SimpleNamespace(
        normal_one=normal_one,
        scale_one=scale_one,
        first_in=first_in,
        queries=queries,
        key_rows=key_rows,
        value_rows=value_rows,
        allowed=allowed,
        log_total=log_total,
        mixed_heads=mixed_heads,
        normal_two=normal_two,
        scale_two=scale_two,
        second_float=second_float,
        picked=picked,
        first_gate=first_gate,
        gate_pair=gate_pair,
        const_weights=const_weights,
        safe_dest=safe_dest,
        is_routed=is_routed,
        owner_pair=owner_pair,
        has_row=has_row,
        slot_rows=slot_rows,
        gate_pre=gate_pre,
        up_pre=up_pre,
        pair_out=pair_out,
        route_pair=route_pair,
    )
    return (result, logits, kept_state)


def layer_backward(upstream, kept_state, dense_set, expert_set):
    w_in, w_out, gain_rows, w_router, vectors = dense_set
    w_gate_up, w_down = expert_set
    tok_count, model_width = upstream.shape
    head_size = model_width // H
    ffn_count = lax.axis_size("expert")
    gain_float = gain_rows.astype(jnp.float32)
    vector_float = vectors.astype(jnp.float32)
    route_pair = kept_state.route_pair
    gate_pair = kept_state.gate_pair
    second_float = kept_state.second_float
    const_weights = kept_state.const_weights
    scaled = gate_pair[:, :, None] * upstream[:, None, :]
    grad_gates = jnp.sum(kept_state.pair_out * upstream[:, None, :], axis=-1)
    grad_slots = jnp.where(
        kept_state.has_row, scaled.reshape(-1, model_width)[kept_state.owner_pair], 0.0
    )
    grad_slots = grad_slots.astype(jnp.bfloat16).reshape(ffn_count, CAP, model_width)
    grad_rows = lax.all_to_all(
        grad_slots, "expert", split_axis=0, concat_axis=0, tiled=True
    ).reshape(ffn_count * CAP, model_width)
    gate_pre = kept_state.gate_pre
    up_pre = kept_state.up_pre
    slot_rows = kept_state.slot_rows
    sigmoid_gate = jax.nn.sigmoid(gate_pre)
    silu_gate = gate_pre * sigmoid_gate
    activated = (silu_gate * up_pre).astype(jnp.bfloat16)
    grad_down = jnp.einsum("rf,rd->fd", activated, grad_rows, preferred_element_type=jnp.float32)
    grad_act = jnp.einsum("rd,fd->rf", grad_rows, w_down[0], preferred_element_type=jnp.float32)
    grad_gate_pre = (
        grad_act * up_pre * sigmoid_gate * (1.0 + gate_pre * (1.0 - sigmoid_gate))
    ).astype(jnp.bfloat16)
    grad_up_pre = (grad_act * silu_gate).astype(jnp.bfloat16)
    grad_w_gate = jnp.einsum(
        "rd,rf->df", slot_rows, grad_gate_pre, preferred_element_type=jnp.float32
    )
    grad_w_up = jnp.einsum("rd,rf->df", slot_rows, grad_up_pre, preferred_element_type=jnp.float32)
    expert_grads = (jnp.stack([grad_w_gate, grad_w_up], axis=1), grad_down)
    grad_in_rows = jnp.einsum(
        "rf,df->rd", grad_gate_pre, w_gate_up[0, 0], preferred_element_type=jnp.float32
    )
    grad_in_rows = grad_in_rows + jnp.einsum(
        "rf,df->rd", grad_up_pre, w_gate_up[0, 1], preferred_element_type=jnp.float32
    )
    grad_back = lax.all_to_all(
        grad_in_rows.reshape(ffn_count, CAP, model_width).astype(jnp.bfloat16),
        "expert",
        split_axis=0,
        concat_axis=0,
        tiled=True,
    ).astype(jnp.float32)
    grad_back = grad_back.reshape(ffn_count * CAP, model_width)
    grad_second = jnp.where(
        kept_state.is_routed[:, None], grad_back[kept_state.safe_dest], 0.0
    )
    grad_second = jnp.sum(grad_second.reshape(tok_count, 2, model_width), axis=1)
    grad_second = grad_second + jnp.sum(
        jnp.where((route_pair == ffn_count + 1)[:, :, None], scaled, 0.0), axis=1
    )
    grad_vectors = []
    grad_const = []
    for member in range(2):
        grad_member = jnp.sum(
            jnp.where((route_pair == ffn_count + 2 + member)[:, :, None], scaled, 0.0), axis=1
        )
        grad_second = grad_second + const_weights[:, member, 0:1] * grad_member
        grad_vectors.append(jnp.sum(const_weights[:, member, 1:2] * grad_member, axis=0))
        grad_first_weight = jnp.sum(grad_member * second_float, axis=-1)
        grad_second_weight = jnp.sum(grad_member * vector_float[member][None, :], axis=-1)
        weight_mean = (
            const_weights[:, member, 0] * grad_first_weight
            + const_weights[:, member, 1] * grad_second_weight
        )
        grad_const.append(const_weights[:, member, 0] * (grad_first_weight - weight_mean))
        grad_const.append(const_weights[:, member, 1] * (grad_second_weight - weight_mean))
    first_gate = kept_state.first_gate
    grad_diff = first_gate * (1.0 - first_gate) * (grad_gates[:, 0] - grad_gates[:, 1])
    grad_chosen = jnp.stack([grad_diff, -grad_diff], axis=1)
    grad_logits = jnp.sum(jnp.where(kept_state.picked, grad_chosen[:, :, None], 0.0), axis=1)
    grad_all = jnp.concatenate([grad_logits, jnp.stack(grad_const, axis=1)], axis=1)
    grad_router = jnp.einsum(
        "td,tc->dc", second_float, grad_all, precision=HIGHEST, preferred_element_type=jnp.float32
    )
    grad_second = grad_second + jnp.einsum(
        "tc,dc->td",
        grad_all,
        w_router.astype(jnp.float32),
        precision=HIGHEST,
        preferred_element_type=jnp.float32,
    )
    normal_two = kept_state.normal_two
    grad_gain_two = jnp.sum(grad_second * normal_two, axis=0)
    grad_after = upstream + norm_back(
        grad_second * gain_float[1], normal_two, kept_state.scale_two
    )
    grad_attn = grad_after.astype(jnp.bfloat16)
    grad_w_out = jnp.einsum(
        "td,te->de", kept_state.mixed_heads, grad_attn, preferred_element_type=jnp.float32
    )
    grad_mixed = jnp.einsum(
        "te,de->td", grad_attn, w_out, preferred_element_type=jnp.float32
    ).astype(jnp.bfloat16)
    grad_mixed = grad_mixed.reshape(tok_count, H, head_size)
    queries = kept_state.queries
    key_rows = kept_state.key_rows
    value_rows = kept_state.value_rows
    raw_scores = masked_scores(queries, key_rows, kept_state.allowed)
    attn_probs = jnp.exp(raw_scores - kept_state.log_total)
    grad_probs = jnp.einsum(
        "thd,shd->hts", grad_mixed, value_rows, preferred_element_type=jnp.float32
    )
    grad_values = jnp.einsum(
        "hts,thd->shd",
        attn_probs.astype(jnp.bfloat16),
        grad_mixed,
        preferred_element_type=jnp.float32,
    )
    row_sum = jnp.sum(grad_probs * attn_probs, axis=-1, keepdims=True)
    grad_raw = (attn_probs * (grad_probs - row_sum)).astype(jnp.bfloat16)
    grad_queries = (
        jnp.einsum("hts,shd->thd", grad_raw, key_rows, preferred_element_type=jnp.float32) * 0.125
    )
    grad_keys = (
        jnp.einsum("hts,thd->shd", grad_raw, queries, preferred_element_type=jnp.float32) * 0.125
    )
    stacked = (
        jnp.stack([grad_queries, grad_keys, grad_values])
        .reshape(3, tok_count, model_width)
        .astype(jnp.bfloat16)
    )
    grad_w_in = jnp.einsum(
        "td,jte->dje", kept_state.first_in, stacked, preferred_element_type=jnp.float32
    )
    grad_first = jnp.einsum("jte,jde->td", stacked, w_in, preferred_element_type=jnp.float32)
    normal_one = kept_state.normal_one
    grad_gain_one = jnp.sum(grad_first * normal_one, axis=0)
    grad_hidden = grad_after + norm_back(
        grad_first * gain_float[0], normal_one, kept_state.scale_one
    )
    dense_grads = (
        grad_w_in,
        grad_w_out,
        jnp.stack([grad_gain_one, grad_gain_two], axis=1),
        grad_router,
        jnp.stack(grad_vectors, axis=1),
    )
    return (grad_hidden, grad_logits, dense_grads, expert_grads)


def plain_body(
    tokens,
    gate_input,
    routes,
    block_ids,
    cotangent,
    norm_gain,
    attn_in,
    attn_out,
    router,
    const_vec,
    expert_gu,
    expert_down,
):
    hidden = tokens.astype(jnp.float32)
    previous = gate_input
    blocks = block_ids[0]
    dense_kept = []
    expert_kept = []
    level_index = 0
    dense_set = (
        lax.all_gather(attn_in[level_index], EVERY, axis=1, tiled=True),
        lax.all_gather(attn_out[level_index], EVERY, axis=0, tiled=True),
        lax.all_gather(norm_gain[level_index], EVERY, axis=1, tiled=True),
        lax.all_gather(router[level_index], EVERY, axis=0, tiled=True),
        lax.all_gather(const_vec[level_index], EVERY, axis=1, tiled=True),
    )
    expert_set = (
        lax.all_gather(expert_gu[level_index], "shard", axis=2, tiled=True),
        lax.all_gather(expert_down[level_index], "shard", axis=1, tiled=True),
    )
    hidden, previous, kept_state = layer_forward(
        hidden, previous, routes, blocks, dense_set, expert_set
    )
    dense_kept.append(dense_set)
    expert_kept.append(expert_set)
    states = [kept_state]
    upstream = cotangent.astype(jnp.float32)
    logits_next = jnp.zeros(gate_input.shape, jnp.float32)
    dense_out = [None] * LAYERS
    expert_out = [None] * LAYERS
    for level_index in reversed(range(LAYERS)):
        dense_set = (
            lax.all_gather(attn_in[level_index], EVERY, axis=1, tiled=True),
            lax.all_gather(attn_out[level_index], EVERY, axis=0, tiled=True),
            lax.all_gather(norm_gain[level_index], EVERY, axis=1, tiled=True),
            lax.all_gather(router[level_index], EVERY, axis=0, tiled=True),
            lax.all_gather(const_vec[level_index], EVERY, axis=1, tiled=True),
        )
        expert_set = (
            lax.all_gather(expert_gu[level_index], "shard", axis=2, tiled=True),
            lax.all_gather(expert_down[level_index], "shard", axis=1, tiled=True),
        )
        upstream, logits_next, dense_grads, expert_grads = layer_backward(
            upstream, states[level_index], dense_set, expert_set
        )
        dense_done = (
            lax.psum_scatter(dense_grads[0], EVERY, scatter_dimension=0, tiled=True),
            lax.psum_scatter(dense_grads[1], EVERY, scatter_dimension=0, tiled=True),
            lax.psum_scatter(dense_grads[2], EVERY, scatter_dimension=0, tiled=True),
            lax.psum_scatter(dense_grads[3], EVERY, scatter_dimension=0, tiled=True),
            lax.psum_scatter(dense_grads[4], EVERY, scatter_dimension=0, tiled=True),
        )
        expert_grads = (
            lax.psum_scatter(expert_grads[0], "shard", scatter_dimension=0, tiled=True),
            lax.psum_scatter(expert_grads[1], "shard", scatter_dimension=0, tiled=True),
        )
        dense_out[level_index] = (
            jnp.transpose(dense_done[0], (1, 0, 2)),
            dense_done[1],
            dense_done[2].T,
            dense_done[3],
            dense_done[4].T,
        )
        expert_out[level_index] = (
            jnp.transpose(expert_grads[0], (1, 0, 2))[None],
            expert_grads[1][None],
        )
    dense_pairs = tuple((jnp.stack([dense_out[0][member]]) for member in range(5)))
    expert_pairs = tuple((jnp.stack([expert_out[0][member]]) for member in range(2)))
    attn_in_grad, attn_out_grad, norm_gain_grad, router_grad, const_vec_grad = dense_pairs
    expert_gu_grad, expert_down_grad = expert_pairs
    return (
        hidden.astype(jnp.bfloat16),
        upstream,
        logits_next,
        norm_gain_grad,
        attn_in_grad,
        attn_out_grad,
        router_grad,
        const_vec_grad,
        expert_gu_grad,
        expert_down_grad,
    )


def solution(mesh):
    in_specs = (
        P(EVERY, None),
        P(EVERY, None),
        P(EVERY, None),
        P(EVERY, None),
        P(EVERY, None),
        P(None, None, EVERY),
        P(None, None, EVERY, None),
        P(None, EVERY, None),
        P(None, EVERY, None),
        P(None, None, EVERY),
        P(None, "expert", None, "shard", None),
        P(None, "expert", "shard", None),
    )
    out_specs = (
        P(EVERY, None),
        P(EVERY, None),
        P(EVERY, None),
        P(None, None, EVERY),
        P(None, None, EVERY, None),
        P(None, EVERY, None),
        P(None, EVERY, None),
        P(None, None, EVERY),
        P(None, "expert", None, "shard", None),
        P(None, "expert", "shard", None),
    )
    step = small_body if dict(mesh.shape) == {"expert": 4, "shard": 8} else plain_body
    return jax.shard_map(step, mesh=mesh, in_specs=in_specs, out_specs=out_specs, check_vma=False)
```

```python
from types import SimpleNamespace

import jax
import jax.numpy as jnp
from jax import lax
from jax.experimental import pallas as pl
from jax.experimental.pallas import tpu as pltpu
from jax.sharding import PartitionSpec as P

EVERY = ("expert", "shard")
H = 12
CAP = 160
EPSILON = 1e-06
MESH = pl.DeviceIdType.MESH
F32 = jnp.float32
BF16 = jnp.bfloat16
NN = (((1,), (0,)), ((), ()))
NT = (((1,), (1,)), ((), ()))
TN = (((0,), (0,)), ((), ()))


def mm(a, b, dims=NN):
    return lax.dot_general(a, b, dims, preferred_element_type=F32)


def iota(shape, dim):
    return lax.broadcasted_iota(jnp.int32, shape, dim)


def where_am_i():
    e, s = lax.axis_index("expert"), lax.axis_index("shard")
    return e // 2, e % 2, s // 2, s % 2


def device(x, c, z, y):
    return (x * 2 + c, z * 2 + y)


def remote(src, dst, send, recv, to):
    return pltpu.make_async_remote_copy(
        src_ref=src, dst_ref=dst, send_sem=send, recv_sem=recv, device_id=to, device_id_type=MESH
    )


def split3(v):
    hi = v.astype(BF16)
    rest = v - hi.astype(F32)
    mid = rest.astype(BF16)
    return hi, mid, (rest - mid.astype(F32)).astype(BF16)


def inside(v):
    return (v >= 0) & (v <= 3)


def layer_kernel(
    ai_in, ao_in, router_in, gain_in, const_in, routes_in, prev_in, blk_in,
    tokens, cotangent, gu_in, dn_in,
    out, in_grad, gate_grad, attn_in_grad, attn_out_grad, router_grad, gain_grad, const_grad,
    gu_out, dn_out, probs,
    tok, cot, gu, dn, w4, smalls, ga, gb, qkv, act, dgate, dup, deo, turned, rx, rc, ggu, gdn, rgu, rdn,
    land_b, land_e, half_b, half_e, pbuf, mixed, second, scal, z_in, sm, sm_in,
    loc, sz, rz, s1, r1, s2, r2, sc_, rc_, se, re, sy, ry, sd, rd, sx, rx_, own,
    sb, rb, sv, rv, sg, rg, sw, rw, lp, tc, qc, t2, q2, t1, q1, tz, qz, ss, rs,
):
    x, c, z, y = where_am_i()
    e = x * 2 + c
    act2, dgate2, dup2 = act, dgate.reshape(1536, 1024), dup.reshape(1536, 1024)
    rx2, rc2 = rx.reshape(1280, 896), rc.reshape(1280, 768)
    p0, p1, bias = dup2.at[0:640, 0:512], dup2.at[0:640, 512:1024], dup2.at[640:1152, 0:512]
    first, stage_x, stage_c = dgate2.at[0:512, 0:768], dgate2.at[640:1280, 0:896], act.at[0:640, 0:768]
    units = (
        (ga, y, x, device(x, c, z, 1 - y), device(1 - x, c, z, y)),
        (gb, x, y, device(1 - x, c, z, y), device(x, c, z, 1 - y)),
    )
    core = device(x, 1 - c, z, y)

    def block_of(i, size=256):
        return pl.ds(pl.multiple_of(i * size, size), size)

    load_tok = pltpu.make_async_copy(tokens, tok, loc.at[0])
    load_cot = pltpu.make_async_copy(cotangent, cot, loc.at[1])
    load_cot.start()
    load_tok.start()

    def slot(h2, h1, zb):
        return ((c * 2 + h2) * 2 + h1) * 4 + zb

    def put_z(u, zb, way):
        g, h1, h2, _, _ = units[u]
        at = g.at[slot(h2, h1, zb)]
        i = (u * 2 + (way + 1) // 2) * 4 + zb
        return remote(at, at, sz.at[i], rz.at[u * 4 + zb], device(x, c, jnp.clip(z + way, 0, 3), y))

    def put_1(u, zb, got=False):
        g, h1, h2, to1, _ = units[u]
        at = g.at[slot(h2, (1 - h1) if got else h1, zb)]
        return remote(at, at, s1.at[u * 4 + zb], r1.at[u * 4 + zb], to1)

    def put_2(u, hh, zb, got=False):
        g, h1, h2, _, to2 = units[u]
        at = g.at[slot((1 - h2) if got else h2, hh, zb)]
        i = u * 8 + hh * 4 + zb
        return remote(at, at, s2.at[i], r2.at[i], to2)

    def put_c(u, hh, got=False):
        at = units[u][0].at[pl.ds((((1 - c) if got else c) * 2 + hh) * 8, 8)]
        return remote(at, at, sc_.at[u * 2 + hh], rc_.at[u * 2 + hh], core)

    few = jnp.concatenate([router_in[...].astype(F32), gain_in[...].astype(F32), const_in[...].astype(F32)], axis=0)
    spread = (iota((16, 128), 0) == iota((16, 128), 1)).astype(BF16)
    few = mm(few.astype(BF16), spread, TN).astype(BF16)
    mine_a, mine_b = slot(x, y, z), slot(y, x, z)
    ga[mine_a, 0:24, 0:768] = ai_in[0]
    ga[mine_a, 24:48, 0:768] = ai_in[1]
    ga[mine_a, 0:24, 768:896] = few
    ga[mine_a, 24:48, 768:896] = jnp.zeros((24, 128), BF16)
    gb[mine_b, 0:24, :] = ai_in[2]
    gb[mine_b, 24:48, :] = ao_in[...]
    for u in range(2):
        for way in (-1, 1):
            pl.when(inside(z + way))(lambda: put_z(u, z, way).start())
        put_1(u, z).start()
        put_2(u, units[u][1], z).start()

    r_t = routes_in[...]
    prev = prev_in[...]
    flat = jnp.concatenate(
        [jnp.zeros((8, 512), F32), r_t.astype(F32), blk_in[...].astype(F32), jnp.zeros((5, 512), F32), prev, jnp.zeros((104, 512), F32)],
        axis=0,
    )
    scal[...] = flat.T
    bias[...] = jnp.where(blk_in[...].astype(F32) <= scal[:, 10:11], 0.0, -1e30).astype(BF16)
    expert_row = iota((16, 512), 0)
    named = ((expert_row == r_t[0:1]) | (expert_row == r_t[1:2])).astype(BF16)
    upper = (iota((512, 512), 0) < iota((512, 512), 1)).astype(BF16)
    count_t = mm(named, upper).astype(jnp.int32) + expert_row * CAP
    for k, ref in ((0, p0), (1, p1)):
        r = r_t[k : k + 1]
        spot = jnp.sum(jnp.where((expert_row == r) & (r < 4), count_t, 0), axis=0, keepdims=True)
        spot = jnp.where(r < 4, spot, -1)
        ref[...] = (iota((640, 512), 0) == spot).astype(BF16)
    load_cot.wait()
    for ed in range(4):
        rows = slice(ed * CAP, ed * CAP + CAP)
        stage_c[rows, :] = mm(p0[rows, :] + p1[rows, :], cot[...]).astype(BF16)

    for r in range(1, 4):
        for way in (1, -1):
            zb = z + way * r
            for u in range(2):

                @pl.when(inside(zb))
                def _():
                    put_z(u, zb, way).wait_recv()
                    pl.when(inside(z - way))(lambda: put_z(u, zb, -way).start())
                    put_1(u, zb).start()
                    put_2(u, units[u][1], zb).start()

    def piece(k, zb):
        if isinstance(k, int) and k == 4:
            return dn.at[block_of(zb)]
        return gu.at[:, pl.ds(pl.multiple_of(zb * 192, 64), 192), block_of(k)]

    def put_e(k, zb, way):
        at = piece(k, zb)
        i = ((way + 1) // 2) * 20 + k * 4 + zb
        return remote(at, at, se.at[i], re.at[k * 4 + zb], device(x, c, jnp.clip(z + way, 0, 3), y))

    at_home = c == y
    half_rows = lambda yy: pl.ds(pl.multiple_of(z * 192 + yy * 96, 32), 96)

    def own_gu(q):
        there = gu.at[:, half_rows(y), 256 * q : 256 * q + 256]
        return pltpu.make_async_copy(gu_in.at[:, :, block_of(2 * q + c)], there, loc.at[3 + q])

    def put_y(cc, q):
        there = gu.at[:, half_rows(y), 256 * q : 256 * q + 256]
        return remote(gu_in.at[:, :, 512 * q + 256 * cc : 512 * q + 256 * cc + 256], there, sy.at[cc * 4 + q], ry.at[y * 4 + q], device(x, cc, z, c))

    def got_y(yo, q):
        here = gu.at[:, half_rows(yo), 256 * q : 256 * q + 256]
        return remote(gu_in.at[:, :, 512 * q : 512 * q + 256], here, sy.at[q], ry.at[yo * 4 + q], core)

    def own_dn():
        return pltpu.make_async_copy(dn_in, dn.at[block_of(z)], loc.at[2])

    def put_dn():
        return remote(dn_in, dn.at[block_of(z)], sy.at[8], ry.at[8], device(x, y, z, c))

    def exchange(start):
        for q in range(4):
            for cc in range(2):
                home = at_home & (c == cc)
                if start:
                    pl.when(home)(lambda: own_gu(q).start())
                    pl.when(jnp.logical_not(home))(lambda: put_y(cc, q).start())
                else:
                    pl.when(jnp.logical_not(home))(lambda: put_y(cc, q).wait_send())
        if start:
            pl.when(at_home)(lambda: own_dn().start())
            pl.when(jnp.logical_not(at_home))(lambda: put_dn().start())
        else:
            pl.when(jnp.logical_not(at_home))(lambda: put_dn().wait_send())

    def exchanged(q):
        for yo in range(2):
            home = at_home & (y == yo)
            pl.when(home)(lambda: own_gu(q).wait())
            pl.when(jnp.logical_not(home))(lambda: got_y(yo, q).wait_recv())

    def serve(k, r):
        for way in (1, -1):
            zb = z + way * r

            @pl.when(inside(zb))
            def _():
                put_e(k, zb, way).wait_recv()
                pl.when(inside(z - way))(lambda: put_e(k, zb, -way).start())

    def first_round(k):
        for way in (-1, 1):
            pl.when(inside(z + way))(lambda: put_e(k, z, way).start())

    exchange(True)

    for r in range(4):
        for way in (1, -1) if r else (1,):
            zb = z + way * r
            for u in range(2):

                @pl.when(inside(zb))
                def _():
                    put_1(u, zb, True).wait_recv()
                    put_2(u, 1 - units[u][1], zb).start()

    for u in range(2):
        put_c(u, units[u][2]).start()
    for q in range(4):
        exchanged(q)
        first_round(q)
    pl.when(at_home)(lambda: own_dn().wait())
    pl.when(jnp.logical_not(at_home))(lambda: put_dn().wait_recv())
    first_round(4)
    for u in range(2):
        h1 = units[u][1]
        for hh in (h1, 1 - h1):
            for zb in range(4):
                put_2(u, hh, zb, True).wait_recv()
        put_c(u, 1 - units[u][2]).start()
    for u in range(2):
        for hh in range(2):
            put_c(u, hh, True).wait_recv()

    def assemble(m, _):
        xx, cc, zz = m // 8, (m // 4) % 2, m % 4
        a = [((cc * 2 + xx) * 2 + yy) * 4 + zz for yy in range(2)]
        b = [((cc * 2 + yy) * 2 + xx) * 4 + zz for yy in range(2)]
        at = pl.ds(pl.multiple_of(m * 48, 16), 48)
        for j in range(2):
            rows = slice(24 * j, 24 * j + 24)
            w4[j, at, :] = jnp.concatenate([ga[a[0], rows, 0:768], ga[a[1], rows, 0:768]], axis=0)
            w4[2 + j, at, :] = jnp.concatenate([gb[b[0], rows, :], gb[b[1], rows, :]], axis=0)
        smalls[at, :] = jnp.concatenate([ga[a[0], 0:24, 768:896], ga[a[1], 0:24, 768:896]], axis=0)
        return 0

    lax.fori_loop(0, 16, assemble, 0)

    eye = (iota((128, 128), 0) == iota((128, 128), 1)).astype(BF16)
    across = mm(eye, smalls[...], NT)[0:16]
    load_tok.wait()
    for t in range(2):
        rows = slice(256 * t, 256 * t + 256)
        hidden = tok[rows, :].astype(F32)
        scale = lax.rsqrt(jnp.mean(hidden * hidden, axis=-1, keepdims=True) + EPSILON)
        first[rows, :] = (hidden * scale * across[12:13]).astype(BF16)

    def project(i, _):
        j = i // 2
        at = block_of(i % 2)
        qkv[block_of(i), :] = mm(first[at, :], w4[j]).astype(BF16)
        return 0

    lax.fori_loop(0, 6, project, 0)

    expert = x * 2 + y
    me = c * 4 + expert

    def dispatch(stage, landing, sends, recvs, j, got=False):
        eo = (expert + j) % 4
        if got:
            return remote(stage.at[0:CAP], landing.at[c * 4 + eo], sends.at[j], recvs.at[eo], core)
        src = stage.at[pl.ds(pl.multiple_of(eo * CAP, 32), CAP)]
        return remote(src, landing.at[me], sends.at[j], recvs.at[expert], device(eo // 2, c, z, eo % 2))

    def share(landing, sends, recvs, j, got=False):
        eo = (expert + j) % 4
        at = landing.at[((1 - c) if got else c) * 4 + eo]
        return remote(at, at, sends.at[4 + j], recvs.at[4 + eo], core)

    for j in (3, 1, 2):
        dispatch(stage_c, rc, sd, rd, j).start()
    my_rows = pl.ds(pl.multiple_of(expert * CAP, 32), CAP)
    own_c = pltpu.make_async_copy(stage_c.at[my_rows], rc.at[me], own.at[0])
    own_c.start()
    for q in range(4):
        serve(q, 1)
    lane = iota((256, 128), 1)

    def head_store(head, half):
        return pltpu.make_async_copy(pbuf.at[half], probs.at[head], lp.at[half])

    def heads(pair, _):
        cols = block_of(pair, 128)
        outs = [[], []]
        for hh in range(2):
            pl.when(pair > 0)(lambda: head_store(2 * pair + hh - 2, hh).wait())
            for t in range(2):
                rows = slice(256 * t, 256 * t + 256)
                q = jnp.where((lane < 64) == (hh == 0), qkv[rows, cols] * BF16(0.125), BF16(0))
                s = mm(q, qkv[512:1024, cols], NT) + bias[rows, :].astype(F32)
                ex = jnp.exp(s - jnp.max(s, axis=-1, keepdims=True))
                p = (ex * (1.0 / jnp.sum(ex, axis=-1, keepdims=True))).astype(BF16)
                pbuf[hh, rows, :] = p
                outs[t].append(mm(p, qkv[1024:1536, cols]))
            head_store(2 * pair + hh, hh).start()
        for t in range(2):
            mixed[256 * t : 256 * t + 256, cols] = jnp.where(lane < 64, outs[t][0], outs[t][1]).astype(BF16)
        return 0

    lax.fori_loop(0, 2, heads, 0)
    serve(4, 1)
    own_c.wait()
    share(rc, sd, rd, 0).start()
    for j in (1, 2, 3):
        dispatch(stage_c, rc, sd, rd, j, True).wait_recv()
        share(rc, sd, rd, j).start()
    lax.fori_loop(2, 4, heads, 0)
    serve(0, 2)
    serve(1, 2)
    lax.fori_loop(4, 6, heads, 0)
    serve(2, 2)
    serve(3, 2)

    lanes = iota((512, 128), 1)
    named_c = ((lanes == scal[:, 8:9].astype(jnp.int32)) | (lanes == scal[:, 9:10].astype(jnp.int32))).astype(BF16)
    lower = (iota((512, 512), 1) < iota((512, 512), 0)).astype(BF16)
    count = mm(lower, named_c) + lanes.astype(F32) * CAP
    for t in range(2):
        rows = slice(256 * t, 256 * t + 256)
        after = tok[rows, :].astype(F32) + mm(mixed[rows, :], w4[3])
        in_grad[rows, :] = after
        scale = lax.rsqrt(jnp.mean(after * after, axis=-1, keepdims=True) + EPSILON)
        second[rows, :] = (after * scale * across[13:14]).astype(BF16)
        score = mm(second[rows, :], smalls[...])
        r = (scal[rows, 8:9].astype(jnp.int32), scal[rows, 9:10].astype(jnp.int32))
        lane8 = iota((256, 8), 1)
        logits = score[:, 0:8] + scal[rows, 16:24]
        picked = [jnp.sum(jnp.where(lane8 == r[k], logits, 0.0), axis=-1, keepdims=True) for k in range(2)]
        g0 = jax.nn.sigmoid(picked[0] - picked[1])
        values = [g0, 1.0 - g0]
        for m in range(2):
            diff = score[:, 8 + 2 * m : 9 + 2 * m] - score[:, 9 + 2 * m : 10 + 2 * m]
            values += [jax.nn.sigmoid(diff), jax.nn.sigmoid(-diff)]
        for k in range(2):
            spot = jnp.sum(jnp.where(lane == r[k], count[rows], 0.0), axis=-1, keepdims=True)
            values.append(jnp.where(r[k] < 4, spot, -1.0))
        filled = scal[rows, :]
        for i, v in enumerate(values):
            filled = jnp.where(lane == i, v, filled)
        scal[rows, :] = filled

    def three_lanes(v, width):
        hi, mid, lo = split3(v)
        zero, at = BF16(0), iota((width, 128), 1)
        return jnp.where(at == 0, hi, zero) + jnp.where(at == 1, mid, zero) + jnp.where(at == 2, lo, zero)

    parts = [three_lanes(scal[:, k : k + 1], 512) for k in range(2)]
    for j in (3, 1, 2, 0):
        eo = (expert + j) % 4
        at = pl.ds(pl.multiple_of(eo * CAP, 32), CAP)
        stage_x[at, 0:768] = mm(p0[at, :] + p1[at, :], second[...]).astype(BF16)
        stage_x[at, 768:896] = (mm(p0[at, :], parts[0]) + mm(p1[at, :], parts[1])).astype(BF16)
        if j:
            dispatch(stage_x, rx, sx, rx_, j).start()
    own_x = pltpu.make_async_copy(stage_x.at[my_rows], rx.at[me], own.at[1])
    own_x.start()
    serve(4, 2)
    own_x.wait()
    share(rx, sx, rx_, 0).start()
    for u in range(2):
        for zb in range(4):
            put_1(u, zb).wait_send()
            put_2(u, 0, zb).wait_send()
            put_2(u, 1, zb).wait_send()
            pl.when((zb >= z) & (z > 0))(lambda: put_z(u, zb, -1).wait_send())
            pl.when((zb <= z) & (z < 3))(lambda: put_z(u, zb, 1).wait_send())
        for hh in range(2):
            put_c(u, hh).wait_send()
    for hh in range(2):
        head_store(10 + hh, hh).wait()
    for j in (1, 2, 3):
        dispatch(stage_x, rx, sx, rx_, j, True).wait_recv()
        share(rx, sx, rx_, j).start()
    for j in range(4):
        share(rc, sd, rd, j, True).wait_recv()
        share(rc, sd, rd, j).wait_send()
        share(rx, sx, rx_, j, True).wait_recv()
        share(rx, sx, rx_, j).wait_send()
        if j:
            dispatch(stage_c, rc, sd, rd, j).wait_send()
            dispatch(stage_x, rx, sx, rx_, j).wait_send()

    def scaled(i, _):
        g = jnp.sum(rx[i, :, 768:896].astype(F32), axis=-1, keepdims=True)
        deo[pl.ds(pl.multiple_of(i * CAP, 32), CAP), :] = (g * rc[i].astype(F32)).astype(BF16)
        return 0

    lax.fori_loop(0, 8, scaled, 0)
    for t in range(5):
        turned[:, 256 * t : 256 * t + 256] = rx2[256 * t : 256 * t + 256, 0:768].T

    def nth(n):
        one = jnp.where(n == 0, 1, jnp.where(n == 1, 0, n))
        two = jnp.where(n == 0, 2, jnp.where(n == 1, 3, 3 - n))
        return jnp.where(z == 0, n, jnp.where(z == 3, 3 - n, jnp.where(z == 1, one, two)))

    def hidden_part(n):
        q = nth(n)
        cols = block_of(q)

        def some(i, _):
            at = pl.ds(pl.multiple_of(i * 320, 64), 320)
            rows = rx2[at, 0:768]
            u, w = mm(rows, gu[0, :, cols]), mm(rows, gu[1, :, cols])
            dact = mm(deo[at, :], dn[cols, :], NT)
            sig = jax.nn.sigmoid(u)
            silu = u * sig
            act[at, cols] = (silu * w).astype(BF16)
            dgate2[at, cols] = (dact * w * sig * (1.0 + u * (1.0 - sig))).astype(BF16)
            dup2[at, cols] = (dact * silu).astype(BF16)
            return 0

        lax.fori_loop(0, 4, some, 0)

    def put_g(zb, k, up):
        land = zb if up else jnp.where(zb == z - 1, 4, zb)
        src, dst = (gdn.at[zb], rdn.at[land]) if k == 4 else (ggu.at[zb, k], rgu.at[land, k])
        to = device(x, c, jnp.clip(z + (1 if up else -1), 0, 3), y)
        return remote(src, dst, sg.at[zb * 5 + k], rg.at[land * 5 + k], to)

    def got_g(land, k):
        src, dst = (gdn.at[0], rdn.at[land]) if k == 4 else (ggu.at[0, k], rgu.at[land, k])
        return remote(src, dst, sg.at[k], rg.at[land * 5 + k], core)

    def grad_part(n):
        q = nth(n)
        cols = block_of(q)
        for i, ref in ((0, dgate2), (1, dup2)):
            for h in range(2):
                got = mm(turned[384 * h : 384 * h + 384, :], ref[0:1280, cols]).astype(BF16)
                for s in range(4):
                    ggu[2 * h + s // 2, q, s % 2, i] = got[96 * s : 96 * s + 96]
        gdn[q] = mm(act[0:1280, cols], deo[...], TN).astype(BF16)

    def first_send(n):
        def up(k):
            for zb in (3, 2, 1):
                put_g(zb, k, True).start()
            if k:
                put_g(k, 4, True).start()

        def down(k):
            for zb in (0, 1, 2):
                put_g(zb, k, False).start()
            if k < 3:
                put_g(k, 4, False).start()

        for i in range(4):
            pl.when((z == 0) & (n == i))(lambda: up(i))
            pl.when((z == 3) & (n == i))(lambda: down(3 - i))

    def add_block(zb, land, k):
        if k == 4:
            gdn[zb] = (gdn[zb].astype(F32) + rdn[land].astype(F32)).astype(BF16)
        else:
            ggu[zb, k] = (ggu[zb, k].astype(F32) + rgu[land, k].astype(F32)).astype(BF16)

    def pass_on(zb, k, up, at):
        @pl.when(z == at)
        def _():
            got_g(zb, k).wait_recv()
            add_block(zb, zb, k)
            put_g(zb, k, up).start()

    def hop1(n):
        for zb in (3, 2):
            pass_on(zb, n, True, 1)
            pass_on(3 - zb, 3 - n, False, 2)
            if n == zb:
                pass_on(zb, 4, True, 1)
                pass_on(3 - zb, 4, False, 2)

    def hop2(n):
        pass_on(3, n, True, 2)
        pass_on(0, 3 - n, False, 1)
        if n == 3:
            pass_on(3, 4, True, 2)
            pass_on(0, 4, False, 1)

    def early(n, _):
        serve(nth(n), 3)
        hidden_part(n)
        grad_part(n)
        first_send(n)
        return 0

    def middle(n, _):
        serve(nth(n), 3)
        pl.when(n == 3)(lambda: serve(4, 3))
        hidden_part(n)
        return 0

    def late(n, _):
        grad_part(n)
        first_send(n)
        return 0

    def halve(src, landing, sends, recvs, k):
        return remote(src.at[(1 - c) * 4 + k], landing.at[k], sends.at[k], recvs.at[k], core)

    def back(src, landing, sends, recvs, j, got=False):
        eo = (expert + j) % 4
        if got:
            return remote(src.at[0], landing.at[eo], sends.at[4 + j], recvs.at[4 + eo], core)
        return remote(
            src.at[c * 4 + eo], landing.at[expert], sends.at[4 + j], recvs.at[4 + expert], device(eo // 2, c, z, eo % 2)
        )

    def own_back(src, landing, i):
        return pltpu.make_async_copy(src.at[me], landing.at[expert], own.at[i])

    def wait_back(src, landing, sends, recvs, i):
        own_back(src, landing, i).wait()
        for j in (1, 2, 3):
            back(src, landing, sends, recvs, j, True).wait_recv()

    def row_part(i, _):
        group = jnp.where(i < 2, 1 - c, c)
        at = pl.ds(pl.multiple_of((group * 4 + 2 * (i % 2)) * CAP, 64), 320)
        dbuf = mm(dgate2[at, :], gu[0], NT) + mm(dup2[at, :], gu[1], NT)
        rx2[at, 0:768] = dbuf.astype(BF16)
        eo = mm(act[at, :], dn[...])
        dg = jnp.sum(eo * rc2[at, :].astype(F32), axis=-1, keepdims=True)
        rx2[at, 768:896] = three_lanes(dg, 320)
        rc2[at, :] = eo.astype(BF16)

        @pl.when(i < 2)
        def _():
            for k in (2 * i, 2 * i + 1):
                halve(rx, half_b, sb, rb, k).start()

        return 0

    def join(j, _):
        eo = (expert + j) % 4
        halve(rx, half_b, sb, rb, eo).wait_recv()
        at = c * 4 + eo
        more = rx[at, :, 768:896].astype(F32) + half_b[eo, :, 768:896].astype(F32)
        rx[at, :, 768:896] = three_lanes(jnp.sum(more, axis=-1, keepdims=True), CAP)
        rx[at, :, 0:768] = (rx[at, :, 0:768].astype(F32) + half_b[eo, :, 0:768].astype(F32)).astype(BF16)
        pl.when(j != 0)(lambda: back(rx, land_b, sb, rb, j).start())
        pl.when(j == 0)(lambda: own_back(rx, land_b, 2).start())
        return 0

    def join_out(j, _):
        eo = (expert + j) % 4
        halve(rc, half_e, sv, rv, eo).wait_recv()
        at = c * 4 + eo
        rc[at] = (rc[at].astype(F32) + half_e[eo].astype(F32)).astype(BF16)
        pl.when(j != 0)(lambda: back(rc, land_e, sv, rv, j).start())
        pl.when(j == 0)(lambda: own_back(rc, land_e, 3).start())
        return 0

    lax.fori_loop(0, 2, early, 0)
    lax.fori_loop(2, 4, middle, 0)
    lax.fori_loop(0, 4, row_part, 0)
    lax.fori_loop(1, 4, join, 0)
    lax.fori_loop(0, 1, join, 0)
    for k in range(4):
        halve(rc, half_e, sv, rv, k).start()
    lax.fori_loop(2, 4, late, 0)

    for t in range(2):
        rows = slice(256 * t, 256 * t + 256)
        turned[:, 512 + 256 * t : 768 + 256 * t] = mixed[rows, :].T
        hidden = tok[rows, :].astype(F32)
        scale = lax.rsqrt(jnp.mean(hidden * hidden, axis=-1, keepdims=True) + EPSILON)
        turned[:, rows] = (hidden * scale * across[12:13]).astype(BF16).T

    def head_load(head, half):
        return pltpu.make_async_copy(probs.at[head], pbuf.at[half], lp.at[half])

    head_load(0, 0).start()
    hop1(0)
    wait_back(rx, land_b, sb, rb, 2)
    lax.fori_loop(0, 4, join_out, 0)

    def of_tile(rows):
        at = lambda i: scal[rows, i : i + 1]
        r = (at(8).astype(jnp.int32), at(9).astype(jnp.int32))
        place = [(iota((256, 640), 1) == at(6 + k).astype(jnp.int32)).astype(BF16) for k in range(2)]
        return (at(0), at(1)), ((at(2), at(3)), (at(4), at(5))), r, place

    total = jnp.zeros((128, 768), F32)
    gain_two = jnp.zeros((1, 768), F32)
    for t in range(2):
        rows = slice(256 * t, 256 * t + 256)
        g, a, r, place = of_tile(rows)
        dsec = jnp.zeros((256, 768), F32)
        dg = [jnp.zeros((256, 1), F32)] * 2
        got = land_b.reshape(640, 896)
        dsec = dsec + mm(place[0] + place[1], got[:, 0:768])
        for k in range(2):
            dg[k] = dg[k] + jnp.sum(mm(place[k], got[:, 768:896]), axis=-1, keepdims=True)
        dx2 = cot[rows, :].astype(F32)
        sec = second[rows, :].astype(F32)
        dot_s = jnp.sum(dx2 * sec, axis=-1, keepdims=True)
        coef = jnp.zeros((256, 1), F32)
        dz = jnp.zeros((256, 128), F32)
        for k in range(2):
            dg[k] = dg[k] + jnp.where(r[k] == 5, dot_s, 0.0)
            coef = coef + jnp.where(r[k] == 5, g[k], 0.0)
        const = jnp.zeros((256, 128), F32)
        for m in range(2):
            dot_v = jnp.sum(dx2 * across[14 + m : 15 + m], axis=-1, keepdims=True)
            weight = jnp.zeros((256, 1), F32)
            for k in range(2):
                chosen = r[k] == 6 + m
                dg[k] = dg[k] + jnp.where(chosen, a[m][0] * dot_s + a[m][1] * dot_v, 0.0)
                weight = weight + jnp.where(chosen, g[k], 0.0)
            coef = coef + a[m][0] * weight
            const = const + jnp.where(lane == 14 + m, a[m][1] * weight, 0.0)
            da = (weight * dot_s, weight * dot_v)
            mean = a[m][0] * da[0] + a[m][1] * da[1]
            for i in range(2):
                dz = jnp.where(lane == 8 + 2 * m + i, a[m][i] * (da[i] - mean), dz)
        diff = g[0] * g[1] * (dg[0] - dg[1])
        dz = dz + jnp.where(lane == r[0], diff, 0.0) - jnp.where(lane == r[1], diff, 0.0)
        gate_grad[:, rows] = dz.T[0:8]
        hi, mid, _ = split3(dz)
        dsec = dsec + coef * dx2 + mm(hi, smalls[...], NT) + mm(mid, smalls[...], NT)
        total = total + mm(hi, second[rows, :], TN) + mm(mid, second[rows, :], TN)
        hi, mid, _ = split3(const)
        total = total + mm(hi, cot[rows, :], TN) + mm(mid, cot[rows, :], TN)
        after = in_grad[rows, :]
        scale = lax.rsqrt(jnp.mean(after * after, axis=-1, keepdims=True) + EPSILON)
        normal = after * scale
        gain_two = gain_two + jnp.sum(dsec * normal, axis=0, keepdims=True)
        lift = dsec * across[13:14]
        dx1 = dx2 + scale * (lift - normal * jnp.mean(lift * normal, axis=-1, keepdims=True))
        in_grad[rows, :] = dx1
        deo[rows, :] = mm(dx1.astype(BF16), w4[3], NT).astype(BF16)
    row16 = iota((16, 768), 0)
    sm[...] = total[0:16] + jnp.where(row16 == 13, gain_two, 0.0)
    hop2(0)
    hop1(1)

    def place_a(d):
        xx, cc, zz, yy = d // 16, (d // 8) % 2, (d // 2) % 4, d % 2
        return ((cc * 2 + xx) * 2 + yy) * 4 + zz

    def place_b(d):
        xx, cc, zz, yy = d // 16, (d // 8) % 2, (d // 2) % 4, d % 2
        return ((cc * 2 + yy) * 2 + xx) * 4 + zz

    def stage(ref, place_of, i, left, right, cols):
        for h in range(2):
            got = mm(turned[384 * h : 384 * h + 384, left], right).astype(BF16)
            for d in range(16):
                ref[place_of(16 * h + d), 24 * i : 24 * i + 24, cols] = got[24 * d : 24 * d + 24]

    groups = [slice(256 * g, 256 * g + 256) for g in range(3)]
    for g in range(3):
        stage(dup, place_b, 1, slice(512, 1024), in_grad[:, groups[g]].astype(BF16), groups[g])

    stages = (dgate, dup)

    def give_c(u, hh, g):
        src = stages[u].at[pl.ds(((1 - c) * 2 + hh) * 8, 8), :, groups[g]]
        i = (u * 2 + hh) * 3 + g
        return remote(src, units[u][0].at[pl.ds(hh * 8, 8), :, groups[g]], tc.at[i], qc.at[i], core)

    def give_2(u, hh, g):
        h2 = units[u][2]
        src = stages[u].at[pl.ds(((c * 2 + 1 - h2) * 2 + hh) * 4, 4), :, groups[g]]
        i = (u * 2 + hh) * 3 + g
        return remote(src, units[u][0].at[pl.ds(16 + hh * 4, 4), :, groups[g]], t2.at[i], q2.at[i], units[u][4])

    def give_1(u, g):
        h1, h2 = units[u][1:3]
        src = stages[u].at[pl.ds(((c * 2 + h2) * 2 + 1 - h1) * 4, 4), :, groups[g]]
        return remote(src, units[u][0].at[24:28, :, groups[g]], t1.at[u * 3 + g], q1.at[u * 3 + g], units[u][3])

    def base(u):
        return ((c * 2 + units[u][2]) * 2 + units[u][1]) * 4

    def give_z(u, zb, up, g):
        land = zb if up else jnp.where(zb == z - 1, 4, zb)
        to = device(x, c, jnp.clip(z + (1 if up else -1), 0, 3), y)
        src = stages[u].at[base(u) + zb, :, groups[g]]
        return remote(src, z_in.at[u, land, :, groups[g]], tz.at[(u * 4 + zb) * 3 + g], qz.at[(u * 5 + land) * 3 + g], to)

    def come_z(u, land, g):
        src = stages[u].at[0, :, groups[g]]
        return remote(src, z_in.at[u, land, :, groups[g]], tz.at[g], qz.at[(u * 5 + land) * 3 + g], core)

    def add_in(u, at, n, other, g):
        def one(i, _):
            got = units[u][0][other + i, :, groups[g]]
            stages[u][at + i, :, groups[g]] = (stages[u][at + i, :, groups[g]].astype(F32) + got.astype(F32)).astype(BF16)
            return 0

        lax.fori_loop(0, n, one, 0)

    def step_c(g):
        for u in range(2):
            h2 = units[u][2]
            give_c(u, 1 - h2, g).start()
            give_c(u, h2, g).start()

    def step_2(g):
        for u in range(2):
            h1, h2 = units[u][1:3]
            give_c(u, 1 - h2, g).wait_recv()
            add_in(u, (c * 2 + 1 - h2) * 8, 8, (1 - h2) * 8, g)
            for hh in (1 - h1, h1):
                give_2(u, hh, g).start()
        for u in range(2):
            h2 = units[u][2]
            give_c(u, h2, g).wait_recv()
            add_in(u, (c * 2 + h2) * 8, 8, h2 * 8, g)

    def step_1(g):
        for u in range(2):
            h1, h2 = units[u][1:3]
            give_2(u, 1 - h1, g).wait_recv()
            add_in(u, ((c * 2 + h2) * 2 + 1 - h1) * 4, 4, 16 + (1 - h1) * 4, g)
            give_1(u, g).start()
        for u in range(2):
            h1, h2 = units[u][1:3]
            give_2(u, h1, g).wait_recv()
            add_in(u, base(u), 4, 16 + h1 * 4, g)

    def step_z(g):
        for u in range(2):
            give_1(u, g).wait_recv()
            add_in(u, base(u), 4, 24, g)
            for i in range(3):
                pl.when(z == 0)(lambda: give_z(u, 3 - i, True, g).start())
                pl.when(z == 3)(lambda: give_z(u, i, False, g).start())

    def relay_z(g):
        for far in range(2):
            for u in range(2):
                for up in (True, False):
                    zb = 3 - far if up else far

                    @pl.when(((z >= 1) & (zb > z)) if up else ((z <= 2) & (zb < z)))
                    def _():
                        come_z(u, zb, g).wait_recv()
                        at = base(u) + zb
                        got = z_in[u, zb, :, groups[g]]
                        stages[u][at, :, groups[g]] = (stages[u][at, :, groups[g]].astype(F32) + got.astype(F32)).astype(BF16)
                        give_z(u, zb, up, g).start()

    lane5 = iota((512, 128), 1)

    def heads_back(pair, _):
        cols = block_of(pair, 128)
        grads = []
        for hh in range(2):
            head_load(2 * pair + hh, hh).wait()
            if hh == 0:
                head_load(2 * pair + 1, 1).start()
            else:
                pl.when(pair < 5)(lambda: head_load(2 * pair + 2, 0).start())
            do = jnp.where((lane5 < 64) == (hh == 0), deo[0:512, cols], BF16(0))
            inner = jnp.sum(do.astype(F32) * mixed[:, cols].astype(F32), axis=-1, keepdims=True)
            dq, dk, dv = [], jnp.zeros((512, 128), F32), jnp.zeros((512, 128), F32)
            for t in range(2):
                rows = slice(256 * t, 256 * t + 256)
                p = pbuf[hh, rows, :]
                ds = (p.astype(F32) * (mm(do[rows], qkv[1024:1536, cols], NT) - inner[rows])).astype(BF16)
                dq.append(mm(ds, qkv[512:1024, cols]))
                dk = dk + mm(ds, qkv[rows, cols], TN)
                dv = dv + mm(p, deo[rows, cols], TN)
            grads.append((jnp.concatenate(dq, axis=0) * 0.125, dk * 0.125, dv))
        for j in range(3):
            act[512 * j : 512 * j + 512, cols] = jnp.where(lane5 < 64, grads[0][j], grads[1][j]).astype(BF16)
        return 0

    for g in range(3):
        lax.fori_loop(2 * g, 2 * g + 2, heads_back, 0)
        for ref, place_of, i, j in ((dgate, place_a, 0, 0), (dgate, place_a, 1, 1), (dup, place_b, 0, 2)):
            stage(ref, place_of, i, slice(0, 512), act[512 * j : 512 * j + 512, groups[g]], groups[g])
        step_c(g)
        if g == 0:
            hop2(1)
            hop1(2)
        if g == 1:
            step_2(0)
            hop2(2)
        if g == 2:
            step_2(1)
            step_1(0)
            hop1(3)

    gain_one = jnp.zeros((1, 768), F32)
    for t in range(2):
        rows = slice(256 * t, 256 * t + 256)
        dfirst = mm(act[256 * t : 256 * t + 256, 0:768], w4[0], NT)
        dfirst = dfirst + mm(act[512 + 256 * t : 768 + 256 * t, 0:768], w4[1], NT)
        dfirst = dfirst + mm(act[1024 + 256 * t : 1280 + 256 * t, 0:768], w4[2], NT)
        hidden = tok[rows, :].astype(F32)
        scale = lax.rsqrt(jnp.mean(hidden * hidden, axis=-1, keepdims=True) + EPSILON)
        normal = hidden * scale
        gain_one = gain_one + jnp.sum(dfirst * normal, axis=0, keepdims=True)
        lift = dfirst * across[12:13]
        in_grad[rows, :] = in_grad[rows, :] + scale * (lift - normal * jnp.mean(lift * normal, axis=-1, keepdims=True))
    sm[...] = sm[...] + jnp.where(row16 == 12, gain_one, 0.0)

    def small_step(i):
        to = (core, device(1 - x, c, z, y), device(x, c, z, 1 - y))[i]
        return remote(sm.at[...], sm_in.at[i], ss.at[i], rs.at[i], to)

    def small_z(way, got=False):
        zt = lax.rem(z + way, 4)
        if got:
            zt = lax.rem(z - way + 4, 4)
            return remote(sm.at[...], sm_in.at[3 + zt], ss.at[2 + way], rs.at[3 + zt], core)
        return remote(sm.at[...], sm_in.at[3 + z], ss.at[2 + way], rs.at[3 + z], device(x, c, zt, y))

    small_step(0).start()
    step_2(2)
    small_step(0).wait()
    sm[...] = sm[...] + sm_in[0]
    small_step(1).start()
    step_1(1)
    step_z(0)
    hop2(3)
    small_step(1).wait()
    sm[...] = sm[...] + sm_in[1]
    small_step(2).start()
    step_1(2)
    step_z(1)
    relay_z(0)
    small_step(2).wait()
    sm[...] = sm[...] + sm_in[2]
    for way in (1, 2, 3):
        small_z(way).start()

    def swap(q, yo):
        at = gu_out.at[:, :, block_of(2 * q + c)]
        return remote(ggu.at[z, q, yo], at, sw.at[q * 2 + yo], rw.at[q * 2 + c], device(x, y, z, yo))

    def swap_got(q, cc):
        at = gu_out.at[:, :, 512 * q + 256 * cc : 512 * q + 256 * cc + 256]
        return remote(ggu.at[z, q, 0], at, sw.at[q * 2], rw.at[q * 2 + cc], core)

    def keep(q):
        return pltpu.make_async_copy(ggu.at[z, q, y], gu_out.at[:, :, block_of(2 * q + c)], loc.at[3 + q])

    def swap_dn():
        return remote(gdn.at[z], dn_out, sw.at[8], rw.at[8], device(x, y, z, c))

    def keep_dn():
        return pltpu.make_async_copy(gdn.at[z], dn_out, loc.at[2])

    def final(k):
        @pl.when(z > 0)
        def _():
            got_g(z, k).wait_recv()
            add_block(z, z, k)

        @pl.when(z < 3)
        def _():
            got_g(4, k).wait_recv()
            add_block(z, 4, k)

        if k < 4:
            for yo in range(2):
                home = at_home & (y == yo)
                pl.when(home)(lambda: keep(k).start())
                pl.when(jnp.logical_not(home))(lambda: swap(k, yo).start())
        else:
            pl.when(at_home)(lambda: keep_dn().start())
            pl.when(jnp.logical_not(at_home))(lambda: swap_dn().start())

    wait_back(rc, land_e, sv, rv, 3)
    for t in range(2):
        rows = slice(256 * t, 256 * t + 256)
        g, a, r, place = of_tile(rows)
        result = tok[rows, :].astype(F32) + mm(mixed[rows, :], w4[3])
        coef = jnp.zeros((256, 1), F32)
        for k in range(2):
            result = result + g[k] * mm(place[k], land_e.reshape(640, 768)[...])
            coef = coef + jnp.where(r[k] == 5, g[k], 0.0)
        for m in range(2):
            weight = jnp.zeros((256, 1), F32)
            for k in range(2):
                weight = weight + jnp.where(r[k] == 6 + m, g[k], 0.0)
            coef = coef + a[m][0] * weight
            result = result + a[m][1] * weight * across[14 + m : 15 + m]
        out[rows, :] = (result + coef * second[rows, :].astype(F32)).astype(BF16)

    step_z(2)
    relay_z(1)
    relay_z(2)
    for k in (1, 2, 0, 3, 4):
        final(k)

    for way in (1, 2, 3):
        small_z(way, True).wait_recv()
    result = sm[...]
    for way in (1, 2, 3):
        result = result + sm_in[3 + lax.rem(z + way, 4)]
    chosen = (iota((768, 128), 0) == iota((768, 128), 1) + 24 * (e * 8 + z * 2 + y)).astype(BF16)
    result = sum(mm(part, chosen) for part in split3(result))
    router_grad[...] = result[0:12, 0:24]
    gain_grad[...] = result[12:14, 0:24]
    const_grad[...] = result[14:16, 0:24]

    for u, ref in ((0, (attn_in_grad.at[0], attn_in_grad.at[1])), (1, (attn_in_grad.at[2], attn_out_grad))):
        for i in range(2):
            ref[i][...] = stages[u][base(u) + z, 24 * i : 24 * i + 24, 0:768].astype(F32)
        for land, there in ((z, z > 0), (4, z < 3)):

            @pl.when(there)
            def _():
                for g in range(3):
                    come_z(u, land, g).wait_recv()
                for i in range(2):
                    ref[i][...] = ref[i][...] + z_in[u, land, 24 * i : 24 * i + 24, :].astype(F32)

    for q in range(4):
        pl.when(at_home)(lambda: keep(q).wait())
        for i in range(2):
            pl.when(jnp.logical_not(at_home & (y == i)))(lambda: swap(q, i).wait_send())
            pl.when(jnp.logical_not(at_home & (c == i)))(lambda: swap_got(q, i).wait_recv())
    pl.when(at_home)(lambda: keep_dn().wait())
    pl.when(jnp.logical_not(at_home))(lambda: swap_dn().wait())
    exchange(False)
    for way in (1, 2, 3):
        small_z(way).wait_send()
    for k in range(4):
        halve(rx, half_b, sb, rb, k).wait_send()
        halve(rc, half_e, sv, rv, k).wait_send()
        if k:
            back(rx, land_b, sb, rb, k).wait_send()
            back(rc, land_e, sv, rv, k).wait_send()

    for zb in range(4):
        for k in range(5):
            pl.when((zb >= z) & (z > 0))(lambda: put_e(k, zb, -1).wait_send())
            pl.when((zb <= z) & (z < 3))(lambda: put_e(k, zb, 1).wait_send())
        for k in range(5):
            pl.when(zb > z)(lambda: put_g(zb, k, True).wait_send())
            pl.when(zb < z)(lambda: put_g(zb, k, False).wait_send())
        for u in range(2):
            for g in range(3):
                pl.when(zb > z)(lambda: give_z(u, zb, True, g).wait_send())
                pl.when(zb < z)(lambda: give_z(u, zb, False, g).wait_send())
    for u in range(2):
        for g in range(3):
            give_1(u, g).wait_send()
            for hh in range(2):
                give_c(u, hh, g).wait_send()
                give_2(u, hh, g).wait_send()


def small_body(
    tokens, gate_input, routes, block_ids, cotangent, norm_gain, attn_in, attn_out, router, const_vec, expert_gu, expert_down
):
    out = lambda *shape, t=F32: jax.ShapeDtypeStruct(shape, t)
    dma = lambda n: pltpu.SemaphoreType.DMA((n,))
    mem = lambda *shape, t=BF16: pltpu.VMEM(shape, t)
    vm = pl.BlockSpec(memory_space=pltpu.VMEM)
    hbm = pl.BlockSpec(memory_space=pl.ANY)
    outs = pl.pallas_call(
        layer_kernel,
        out_shape=(
            out(512, 768, t=BF16), out(512, 768), out(8, 512), out(3, 24, 768), out(24, 768), out(12, 24), out(2, 24), out(2, 24),
            out(2, 96, 2048, t=BF16), out(256, 768, t=BF16), out(12, 512, 512, t=BF16),
        ),
        in_specs=[vm] * 8 + [hbm] * 4,
        out_specs=(vm,) * 8 + (hbm,) * 3,
        scratch_shapes=[
            mem(512, 768), mem(512, 768), mem(2, 768, 1024), mem(1024, 768), mem(4, 768, 768), mem(768, 128),
            mem(32, 48, 896), mem(32, 48, 768), mem(1536, 768), mem(1536, 1024), mem(32, 48, 1024), mem(32, 48, 1024),
            mem(1280, 768), mem(768, 1280), mem(8, CAP, 896), mem(8, CAP, 768),
            mem(4, 4, 2, 2, 96, 256), mem(4, 256, 768), mem(5, 4, 2, 2, 96, 256), mem(5, 256, 768),
            mem(4, CAP, 896), mem(4, CAP, 768), mem(4, CAP, 896), mem(4, CAP, 768), mem(2, 512, 512), mem(512, 768), mem(512, 768), mem(512, 128, t=F32),
            mem(2, 5, 48, 768), mem(16, 768, t=F32), mem(7, 16, 768, t=F32),
            *(dma(n) for n in (8, 16, 8, 8, 8, 16, 16, 4, 4, 40, 20, 9, 9, 8, 8, 8, 8, 4)),
            *(dma(n) for n in (8, 8, 8, 8, 20, 25, 9, 9, 2, 12, 12, 12, 12, 6, 6, 24, 30, 6, 7)),
        ],
        compiler_params=pltpu.CompilerParams(has_side_effects=True, vmem_limit_bytes=63_200_000),
        name="layer",
    )(
        attn_in[0], attn_out[0], router[0].T, norm_gain[0], const_vec[0], routes.T, gate_input.T, block_ids,
        tokens, cotangent, expert_gu[0, 0], expert_down[0, 0],
    )
    result, in_grad, gate, ai, ao, ro, ng, cv, gu, dn, _ = outs
    return (
        result, in_grad, gate.T, ng[None], ai[None], ao[None], ro.T[None], cv[None],
        gu.astype(F32)[None, None], dn.astype(F32)[None, None],
    )


LAYERS = 1
HIGHEST = lax.Precision.HIGHEST


def normed(values):
    inv_scale = lax.rsqrt(jnp.mean(values * values, axis=-1, keepdims=True) + EPSILON)
    return (values * inv_scale, inv_scale)


def norm_back(upstream, normal, inv_scale):
    return inv_scale * (upstream - normal * jnp.mean(upstream * normal, axis=-1, keepdims=True))


def slot_table(route_pair, ffn_count, capacity):
    flat_route = route_pair.reshape(-1)
    pair_count = flat_route.shape[0]
    one_hot = (flat_route[:, None] == jnp.arange(ffn_count, dtype=jnp.int32)[None, :]).astype(
        jnp.int32
    )
    earlier = jnp.arange(pair_count)[None, :] < jnp.arange(pair_count)[:, None]
    running = jnp.dot(
        earlier.astype(jnp.bfloat16), one_hot.astype(jnp.bfloat16), preferred_element_type=jnp.float32
    ).astype(jnp.int32)
    position = jnp.sum(running * one_hot, axis=1)
    is_routed = flat_route < ffn_count
    destination = jnp.where(is_routed, flat_route * capacity + position, ffn_count * capacity)
    pair_index = jnp.arange(pair_count, dtype=jnp.int32)
    owner_pair = (
        jnp.zeros((ffn_count * capacity,), jnp.int32).at[destination].set(pair_index, mode="drop")
    )
    filled = (
        jnp.zeros((ffn_count * capacity,), jnp.int32)
        .at[destination]
        .set(jnp.ones_like(pair_index), mode="drop")
    )
    return (destination, is_routed, owner_pair, filled)


def masked_scores(queries, key_rows, allowed):
    raw_scores = (
        jnp.einsum("thd,shd->hts", queries, key_rows, preferred_element_type=jnp.float32) * 0.125
    )
    return jnp.where(allowed[None, :, :], raw_scores, -1e30)


def layer_forward(hidden, previous, route_pair, blocks, dense_set, expert_set):
    w_in, w_out, gain_rows, w_router, vectors = dense_set
    w_gate_up, w_down = expert_set
    tok_count, model_width = hidden.shape
    head_size = model_width // H
    experts = previous.shape[1]
    gain_float = gain_rows.astype(jnp.float32)
    normal_one, scale_one = normed(hidden)
    first_in = (normal_one * gain_float[0]).astype(jnp.bfloat16)
    projected = jnp.einsum(
        "td,jde->jte", first_in, w_in, preferred_element_type=jnp.float32
    ).astype(jnp.bfloat16)
    projected = projected.reshape(3, tok_count, H, head_size)
    queries, key_rows, value_rows = (projected[0], projected[1], projected[2])
    allowed = blocks[None, :] <= blocks[:, None]
    raw_scores = masked_scores(queries, key_rows, allowed)
    row_peak = jnp.max(raw_scores, axis=-1, keepdims=True)
    log_total = row_peak + jnp.log(jnp.sum(jnp.exp(raw_scores - row_peak), axis=-1, keepdims=True))
    attn_probs = jnp.exp(raw_scores - log_total).astype(jnp.bfloat16)
    mixed_heads = jnp.einsum(
        "hts,shd->thd", attn_probs, value_rows, preferred_element_type=jnp.float32
    )
    mixed_heads = mixed_heads.reshape(tok_count, model_width).astype(jnp.bfloat16)
    after_attn = hidden + jnp.dot(mixed_heads, w_out, preferred_element_type=jnp.float32)
    normal_two, scale_two = normed(after_attn)
    second_in = (normal_two * gain_float[1]).astype(jnp.bfloat16)
    second_float = second_in.astype(jnp.float32)
    all_logits = jnp.dot(second_in, w_router, preferred_element_type=jnp.float32)
    logits = all_logits[:, :experts] + previous
    picked = route_pair[:, :, None] == jnp.arange(experts, dtype=jnp.int32)[None, None, :]
    chosen = jnp.sum(jnp.where(picked, logits[:, None, :], 0.0), axis=-1)
    first_gate = jax.nn.sigmoid(chosen[:, 0] - chosen[:, 1])
    gate_pair = jnp.stack([first_gate, 1.0 - first_gate], axis=1)
    const_weights = jax.nn.softmax(all_logits[:, experts:].reshape(tok_count, 2, 2), axis=-1)
    ffn_count = lax.axis_size("expert")
    destination, is_routed, owner_pair, filled = slot_table(route_pair, ffn_count, CAP)
    has_row = filled[:, None] > 0
    send_rows = jnp.where(has_row, second_in[owner_pair // 2], jnp.zeros((), jnp.bfloat16))
    send_rows = send_rows.reshape(ffn_count, CAP, model_width)
    slot_rows = lax.all_to_all(
        send_rows, "expert", split_axis=0, concat_axis=0, tiled=True
    ).reshape(ffn_count * CAP, model_width)
    gate_pre = jnp.dot(slot_rows, w_gate_up[0, 0], preferred_element_type=jnp.float32)
    up_pre = jnp.dot(slot_rows, w_gate_up[0, 1], preferred_element_type=jnp.float32)
    activated = (jax.nn.silu(gate_pre) * up_pre).astype(jnp.bfloat16)
    expert_out = jnp.dot(activated, w_down[0], preferred_element_type=jnp.float32).astype(
        jnp.bfloat16
    )
    expert_out = expert_out.reshape(ffn_count, CAP, model_width)
    returned = lax.all_to_all(
        expert_out, "expert", split_axis=0, concat_axis=0, tiled=True
    ).reshape(ffn_count * CAP, model_width)
    safe_dest = jnp.minimum(destination, ffn_count * CAP - 1)
    ffn_rows = jnp.where(is_routed[:, None], returned[safe_dest].astype(jnp.float32), 0.0)
    ffn_rows = ffn_rows.reshape(tok_count, 2, model_width)
    vector_float = vectors.astype(jnp.float32)
    const_rows = (
        const_weights[:, :, 0:1] * second_float[:, None, :]
        + const_weights[:, :, 1:2] * vector_float[None, :, :]
    )
    pair_out = ffn_rows + jnp.where(
        (route_pair == ffn_count + 1)[:, :, None], second_float[:, None, :], 0.0
    )
    for member in range(2):
        chosen_const = (route_pair == ffn_count + 2 + member)[:, :, None]
        pair_out = pair_out + jnp.where(chosen_const, const_rows[:, member][:, None, :], 0.0)
    result = after_attn + jnp.sum(gate_pair[:, :, None] * pair_out, axis=1)
    kept_state = SimpleNamespace(
        normal_one=normal_one,
        scale_one=scale_one,
        first_in=first_in,
        queries=queries,
        key_rows=key_rows,
        value_rows=value_rows,
        allowed=allowed,
        log_total=log_total,
        mixed_heads=mixed_heads,
        normal_two=normal_two,
        scale_two=scale_two,
        second_float=second_float,
        picked=picked,
        first_gate=first_gate,
        gate_pair=gate_pair,
        const_weights=const_weights,
        safe_dest=safe_dest,
        is_routed=is_routed,
        owner_pair=owner_pair,
        has_row=has_row,
        slot_rows=slot_rows,
        gate_pre=gate_pre,
        up_pre=up_pre,
        pair_out=pair_out,
        route_pair=route_pair,
    )
    return (result, logits, kept_state)


def layer_backward(upstream, kept_state, dense_set, expert_set):
    w_in, w_out, gain_rows, w_router, vectors = dense_set
    w_gate_up, w_down = expert_set
    tok_count, model_width = upstream.shape
    head_size = model_width // H
    ffn_count = lax.axis_size("expert")
    gain_float = gain_rows.astype(jnp.float32)
    vector_float = vectors.astype(jnp.float32)
    route_pair = kept_state.route_pair
    gate_pair = kept_state.gate_pair
    second_float = kept_state.second_float
    const_weights = kept_state.const_weights
    scaled = gate_pair[:, :, None] * upstream[:, None, :]
    grad_gates = jnp.sum(kept_state.pair_out * upstream[:, None, :], axis=-1)
    grad_slots = jnp.where(
        kept_state.has_row, scaled.reshape(-1, model_width)[kept_state.owner_pair], 0.0
    )
    grad_slots = grad_slots.astype(jnp.bfloat16).reshape(ffn_count, CAP, model_width)
    grad_rows = lax.all_to_all(
        grad_slots, "expert", split_axis=0, concat_axis=0, tiled=True
    ).reshape(ffn_count * CAP, model_width)
    gate_pre = kept_state.gate_pre
    up_pre = kept_state.up_pre
    slot_rows = kept_state.slot_rows
    sigmoid_gate = jax.nn.sigmoid(gate_pre)
    silu_gate = gate_pre * sigmoid_gate
    activated = (silu_gate * up_pre).astype(jnp.bfloat16)
    grad_down = jnp.einsum("rf,rd->fd", activated, grad_rows, preferred_element_type=jnp.float32)
    grad_act = jnp.einsum("rd,fd->rf", grad_rows, w_down[0], preferred_element_type=jnp.float32)
    grad_gate_pre = (
        grad_act * up_pre * sigmoid_gate * (1.0 + gate_pre * (1.0 - sigmoid_gate))
    ).astype(jnp.bfloat16)
    grad_up_pre = (grad_act * silu_gate).astype(jnp.bfloat16)
    grad_w_gate = jnp.einsum(
        "rd,rf->df", slot_rows, grad_gate_pre, preferred_element_type=jnp.float32
    )
    grad_w_up = jnp.einsum("rd,rf->df", slot_rows, grad_up_pre, preferred_element_type=jnp.float32)
    expert_grads = (jnp.stack([grad_w_gate, grad_w_up], axis=1), grad_down)
    grad_in_rows = jnp.einsum(
        "rf,df->rd", grad_gate_pre, w_gate_up[0, 0], preferred_element_type=jnp.float32
    )
    grad_in_rows = grad_in_rows + jnp.einsum(
        "rf,df->rd", grad_up_pre, w_gate_up[0, 1], preferred_element_type=jnp.float32
    )
    grad_back = lax.all_to_all(
        grad_in_rows.reshape(ffn_count, CAP, model_width).astype(jnp.bfloat16),
        "expert",
        split_axis=0,
        concat_axis=0,
        tiled=True,
    ).astype(jnp.float32)
    grad_back = grad_back.reshape(ffn_count * CAP, model_width)
    grad_second = jnp.where(
        kept_state.is_routed[:, None], grad_back[kept_state.safe_dest], 0.0
    )
    grad_second = jnp.sum(grad_second.reshape(tok_count, 2, model_width), axis=1)
    grad_second = grad_second + jnp.sum(
        jnp.where((route_pair == ffn_count + 1)[:, :, None], scaled, 0.0), axis=1
    )
    grad_vectors = []
    grad_const = []
    for member in range(2):
        grad_member = jnp.sum(
            jnp.where((route_pair == ffn_count + 2 + member)[:, :, None], scaled, 0.0), axis=1
        )
        grad_second = grad_second + const_weights[:, member, 0:1] * grad_member
        grad_vectors.append(jnp.sum(const_weights[:, member, 1:2] * grad_member, axis=0))
        grad_first_weight = jnp.sum(grad_member * second_float, axis=-1)
        grad_second_weight = jnp.sum(grad_member * vector_float[member][None, :], axis=-1)
        weight_mean = (
            const_weights[:, member, 0] * grad_first_weight
            + const_weights[:, member, 1] * grad_second_weight
        )
        grad_const.append(const_weights[:, member, 0] * (grad_first_weight - weight_mean))
        grad_const.append(const_weights[:, member, 1] * (grad_second_weight - weight_mean))
    first_gate = kept_state.first_gate
    grad_diff = first_gate * (1.0 - first_gate) * (grad_gates[:, 0] - grad_gates[:, 1])
    grad_chosen = jnp.stack([grad_diff, -grad_diff], axis=1)
    grad_logits = jnp.sum(jnp.where(kept_state.picked, grad_chosen[:, :, None], 0.0), axis=1)
    grad_all = jnp.concatenate([grad_logits, jnp.stack(grad_const, axis=1)], axis=1)
    grad_router = jnp.einsum(
        "td,tc->dc", second_float, grad_all, precision=HIGHEST, preferred_element_type=jnp.float32
    )
    grad_second = grad_second + jnp.einsum(
        "tc,dc->td",
        grad_all,
        w_router.astype(jnp.float32),
        precision=HIGHEST,
        preferred_element_type=jnp.float32,
    )
    normal_two = kept_state.normal_two
    grad_gain_two = jnp.sum(grad_second * normal_two, axis=0)
    grad_after = upstream + norm_back(
        grad_second * gain_float[1], normal_two, kept_state.scale_two
    )
    grad_attn = grad_after.astype(jnp.bfloat16)
    grad_w_out = jnp.einsum(
        "td,te->de", kept_state.mixed_heads, grad_attn, preferred_element_type=jnp.float32
    )
    grad_mixed = jnp.einsum(
        "te,de->td", grad_attn, w_out, preferred_element_type=jnp.float32
    ).astype(jnp.bfloat16)
    grad_mixed = grad_mixed.reshape(tok_count, H, head_size)
    queries = kept_state.queries
    key_rows = kept_state.key_rows
    value_rows = kept_state.value_rows
    raw_scores = masked_scores(queries, key_rows, kept_state.allowed)
    attn_probs = jnp.exp(raw_scores - kept_state.log_total)
    grad_probs = jnp.einsum(
        "thd,shd->hts", grad_mixed, value_rows, preferred_element_type=jnp.float32
    )
    grad_values = jnp.einsum(
        "hts,thd->shd",
        attn_probs.astype(jnp.bfloat16),
        grad_mixed,
        preferred_element_type=jnp.float32,
    )
    row_sum = jnp.sum(grad_probs * attn_probs, axis=-1, keepdims=True)
    grad_raw = (attn_probs * (grad_probs - row_sum)).astype(jnp.bfloat16)
    grad_queries = (
        jnp.einsum("hts,shd->thd", grad_raw, key_rows, preferred_element_type=jnp.float32) * 0.125
    )
    grad_keys = (
        jnp.einsum("hts,thd->shd", grad_raw, queries, preferred_element_type=jnp.float32) * 0.125
    )
    stacked = (
        jnp.stack([grad_queries, grad_keys, grad_values])
        .reshape(3, tok_count, model_width)
        .astype(jnp.bfloat16)
    )
    grad_w_in = jnp.einsum(
        "td,jte->dje", kept_state.first_in, stacked, preferred_element_type=jnp.float32
    )
    grad_first = jnp.einsum("jte,jde->td", stacked, w_in, preferred_element_type=jnp.float32)
    normal_one = kept_state.normal_one
    grad_gain_one = jnp.sum(grad_first * normal_one, axis=0)
    grad_hidden = grad_after + norm_back(
        grad_first * gain_float[0], normal_one, kept_state.scale_one
    )
    dense_grads = (
        grad_w_in,
        grad_w_out,
        jnp.stack([grad_gain_one, grad_gain_two], axis=1),
        grad_router,
        jnp.stack(grad_vectors, axis=1),
    )
    return (grad_hidden, grad_logits, dense_grads, expert_grads)


def plain_body(
    tokens,
    gate_input,
    routes,
    block_ids,
    cotangent,
    norm_gain,
    attn_in,
    attn_out,
    router,
    const_vec,
    expert_gu,
    expert_down,
):
    hidden = tokens.astype(jnp.float32)
    previous = gate_input
    blocks = block_ids[0]
    dense_kept = []
    expert_kept = []
    level_index = 0
    dense_set = (
        lax.all_gather(attn_in[level_index], EVERY, axis=1, tiled=True),
        lax.all_gather(attn_out[level_index], EVERY, axis=0, tiled=True),
        lax.all_gather(norm_gain[level_index], EVERY, axis=1, tiled=True),
        lax.all_gather(router[level_index], EVERY, axis=0, tiled=True),
        lax.all_gather(const_vec[level_index], EVERY, axis=1, tiled=True),
    )
    expert_set = (
        lax.all_gather(expert_gu[level_index], "shard", axis=2, tiled=True),
        lax.all_gather(expert_down[level_index], "shard", axis=1, tiled=True),
    )
    hidden, previous, kept_state = layer_forward(
        hidden, previous, routes, blocks, dense_set, expert_set
    )
    dense_kept.append(dense_set)
    expert_kept.append(expert_set)
    states = [kept_state]
    upstream = cotangent.astype(jnp.float32)
    logits_next = jnp.zeros(gate_input.shape, jnp.float32)
    dense_out = [None] * LAYERS
    expert_out = [None] * LAYERS
    for level_index in reversed(range(LAYERS)):
        dense_set = (
            lax.all_gather(attn_in[level_index], EVERY, axis=1, tiled=True),
            lax.all_gather(attn_out[level_index], EVERY, axis=0, tiled=True),
            lax.all_gather(norm_gain[level_index], EVERY, axis=1, tiled=True),
            lax.all_gather(router[level_index], EVERY, axis=0, tiled=True),
            lax.all_gather(const_vec[level_index], EVERY, axis=1, tiled=True),
        )
        expert_set = (
            lax.all_gather(expert_gu[level_index], "shard", axis=2, tiled=True),
            lax.all_gather(expert_down[level_index], "shard", axis=1, tiled=True),
        )
        upstream, logits_next, dense_grads, expert_grads = layer_backward(
            upstream, states[level_index], dense_set, expert_set
        )
        dense_done = (
            lax.psum_scatter(dense_grads[0], EVERY, scatter_dimension=0, tiled=True),
            lax.psum_scatter(dense_grads[1], EVERY, scatter_dimension=0, tiled=True),
            lax.psum_scatter(dense_grads[2], EVERY, scatter_dimension=0, tiled=True),
            lax.psum_scatter(dense_grads[3], EVERY, scatter_dimension=0, tiled=True),
            lax.psum_scatter(dense_grads[4], EVERY, scatter_dimension=0, tiled=True),
        )
        expert_grads = (
            lax.psum_scatter(expert_grads[0], "shard", scatter_dimension=0, tiled=True),
            lax.psum_scatter(expert_grads[1], "shard", scatter_dimension=0, tiled=True),
        )
        dense_out[level_index] = (
            jnp.transpose(dense_done[0], (1, 0, 2)),
            dense_done[1],
            dense_done[2].T,
            dense_done[3],
            dense_done[4].T,
        )
        expert_out[level_index] = (
            jnp.transpose(expert_grads[0], (1, 0, 2))[None],
            expert_grads[1][None],
        )
    dense_pairs = tuple((jnp.stack([dense_out[0][member]]) for member in range(5)))
    expert_pairs = tuple((jnp.stack([expert_out[0][member]]) for member in range(2)))
    attn_in_grad, attn_out_grad, norm_gain_grad, router_grad, const_vec_grad = dense_pairs
    expert_gu_grad, expert_down_grad = expert_pairs
    return (
        hidden.astype(jnp.bfloat16),
        upstream,
        logits_next,
        norm_gain_grad,
        attn_in_grad,
        attn_out_grad,
        router_grad,
        const_vec_grad,
        expert_gu_grad,
        expert_down_grad,
    )


def solution(mesh):
    in_specs = (
        P(EVERY, None),
        P(EVERY, None),
        P(EVERY, None),
        P(EVERY, None),
        P(EVERY, None),
        P(None, None, EVERY),
        P(None, None, EVERY, None),
        P(None, EVERY, None),
        P(None, EVERY, None),
        P(None, None, EVERY),
        P(None, "expert", None, "shard", None),
        P(None, "expert", "shard", None),
    )
    out_specs = (
        P(EVERY, None),
        P(EVERY, None),
        P(EVERY, None),
        P(None, None, EVERY),
        P(None, None, EVERY, None),
        P(None, EVERY, None),
        P(None, EVERY, None),
        P(None, None, EVERY),
        P(None, "expert", None, "shard", None),
        P(None, "expert", "shard", None),
    )
    step = small_body if dict(mesh.shape) == {"expert": 4, "shard": 8} else plain_body
    return jax.shard_map(step, mesh=mesh, in_specs=in_specs, out_specs=out_specs, check_vma=False)
```

```python
from types import SimpleNamespace

import jax
import jax.numpy as jnp
from jax import lax
from jax.experimental import pallas as pl
from jax.experimental.pallas import tpu as pltpu
from jax.sharding import PartitionSpec as P

EVERY = ("expert", "shard")
H = 12
CAP = 160
EPSILON = 1e-06
MESH = pl.DeviceIdType.MESH
F32 = jnp.float32
BF16 = jnp.bfloat16
NN = (((1,), (0,)), ((), ()))
NT = (((1,), (1,)), ((), ()))
TN = (((0,), (0,)), ((), ()))


def mm(a, b, dims=NN):
    return lax.dot_general(a, b, dims, preferred_element_type=F32)


def iota(shape, dim):
    return lax.broadcasted_iota(jnp.int32, shape, dim)


def where_am_i():
    e, s = lax.axis_index("expert"), lax.axis_index("shard")
    return e // 2, e % 2, s // 2, s % 2


def device(x, c, z, y):
    return (x * 2 + c, z * 2 + y)


def remote(src, dst, send, recv, to):
    return pltpu.make_async_remote_copy(
        src_ref=src, dst_ref=dst, send_sem=send, recv_sem=recv, device_id=to, device_id_type=MESH
    )


def split3(v):
    hi = v.astype(BF16)
    rest = v - hi.astype(F32)
    mid = rest.astype(BF16)
    return hi, mid, (rest - mid.astype(F32)).astype(BF16)


def inside(v):
    return (v >= 0) & (v <= 3)


def layer_kernel(
    ai_in, ao_in, router_in, gain_in, const_in, routes_in, prev_in, blk_in,
    tokens, cotangent, gu_in, dn_in,
    out, in_grad, gate_grad, attn_in_grad, attn_out_grad, router_grad, gain_grad, const_grad,
    gu_out, dn_out, probs,
    tok, cot, gu, dn, w4, smalls, ga, gb, qkv, act, dgate, dup, deo, turned, rx, rc, ggu, gdn, rgu, rdn,
    land_b, land_e, half_b, half_e, pbuf, mixed, second, scal, z_in, sm, sm_in,
    loc, sz, rz, s1, r1, s2, r2, sc_, rc_, se, re, sy, ry, sd, rd, sx, rx_, own,
    sb, rb, sv, rv, sg, rg, sw, rw, lp, tc, qc, t2, q2, t1, q1, tz, qz, ss, rs,
):
    x, c, z, y = where_am_i()
    e = x * 2 + c
    met = pltpu.get_barrier_semaphore()
    friends = [device(x, c, lax.rem(z + i, 4), y) for i in (1, 2, 3)]
    friends += [device(x, 1 - c, z, y), device(1 - x, c, z, y), device(x, c, z, 1 - y), device(1 - x, c, z, 1 - y)]
    friends += [device(x, 1 - c, z, 1 - y)]
    for friend in friends:
        pl.semaphore_signal(met, inc=1, device_id=friend, device_id_type=MESH)
    pl.semaphore_wait(met, 8)
    act2, dgate2, dup2 = act, dgate.reshape(1536, 1024), dup.reshape(1536, 1024)
    rx2, rc2 = rx.reshape(1280, 896), rc.reshape(1280, 768)
    p0, p1, bias = dup2.at[0:640, 0:512], dup2.at[0:640, 512:1024], dup2.at[640:1152, 0:512]
    first, stage_x, stage_c = dgate2.at[0:512, 0:768], dgate2.at[640:1280, 0:896], act.at[0:640, 0:768]
    units = (
        (ga, y, x, device(x, c, z, 1 - y), device(1 - x, c, z, y)),
        (gb, y, x, device(x, c, z, 1 - y), device(1 - x, c, z, y)),
    )
    core = device(x, 1 - c, z, y)

    def block_of(i, size=256):
        return pl.ds(pl.multiple_of(i * size, size), size)

    load_tok = pltpu.make_async_copy(tokens, tok, loc.at[0])
    load_cot = pltpu.make_async_copy(cotangent, cot, loc.at[1])
    load_cot.start()
    load_tok.start()

    def slot(h2, h1, zb):
        return ((c * 2 + h2) * 2 + h1) * 4 + zb

    def put_z(u, zb, way):
        g, h1, h2, _, _ = units[u]
        at = g.at[slot(h2, h1, zb)]
        i = (u * 2 + (way + 1) // 2) * 4 + zb
        return remote(at, at, sz.at[i], rz.at[u * 4 + zb], device(x, c, jnp.clip(z + way, 0, 3), y))

    def put_1(u, zb, got=False):
        g, h1, h2, to1, _ = units[u]
        at = g.at[slot(h2, (1 - h1) if got else h1, zb)]
        return remote(at, at, s1.at[u * 4 + zb], r1.at[u * 4 + zb], to1)

    def put_2(u, hh, zb, got=False):
        g, h1, h2, _, to2 = units[u]
        at = g.at[slot((1 - h2) if got else h2, hh, zb)]
        i = u * 8 + hh * 4 + zb
        return remote(at, at, s2.at[i], r2.at[i], to2)

    def put_c(u, hh, got=False):
        at = units[u][0].at[pl.ds((((1 - c) if got else c) * 2 + hh) * 8, 8)]
        return remote(at, at, sc_.at[u * 2 + hh], rc_.at[u * 2 + hh], core)

    few = jnp.concatenate([router_in[...].astype(F32), gain_in[...].astype(F32), const_in[...].astype(F32)], axis=0)
    spread = (iota((16, 128), 0) == iota((16, 128), 1)).astype(BF16)
    few = mm(few.astype(BF16), spread, TN).astype(BF16)
    mine_a = mine_b = slot(x, y, z)
    ga[mine_a, 0:24, 0:768] = ai_in[0]
    ga[mine_a, 24:48, 0:768] = ai_in[1]
    ga[mine_a, 0:24, 768:896] = few
    ga[mine_a, 24:48, 768:896] = jnp.zeros((24, 128), BF16)
    gb[mine_b, 0:24, :] = ai_in[2]
    gb[mine_b, 24:48, :] = ao_in[...]
    for u in range(2):
        for way in (-1, 1):
            pl.when(inside(z + way))(lambda: put_z(u, z, way).start())
        put_1(u, z).start()
        put_2(u, units[u][1], z).start()

    def piece(k, zb):
        if k == 2:
            return dn.at[block_of(zb)]
        return gu.at[:, pl.ds(pl.multiple_of(zb * 192 + (y if k == 0 else 1 - y) * 96, 32), 96), :]

    def put_e(k, zb, way):
        at = piece(k, zb)
        i = ((way + 1) // 2) * 12 + k * 4 + zb
        return remote(at, at, se.at[i], re.at[k * 4 + zb], device(x, c, jnp.clip(z + way, 0, 3), y))

    at_home = c == y
    half_rows = lambda yy: pl.ds(pl.multiple_of(z * 192 + yy * 96, 32), 96)

    def own_gu(q):
        there = gu.at[:, half_rows(y), 256 * q : 256 * q + 256]
        return pltpu.make_async_copy(gu_in.at[:, :, block_of(2 * q + c)], there, loc.at[3 + q])

    def put_y(cc, q):
        there = gu.at[:, half_rows(y), 256 * q : 256 * q + 256]
        return remote(gu_in.at[:, :, 512 * q + 256 * cc : 512 * q + 256 * cc + 256], there, sy.at[cc * 4 + q], ry.at[y * 4 + q], device(x, cc, z, c))

    def got_y(yo, q):
        here = gu.at[:, half_rows(yo), 256 * q : 256 * q + 256]
        return remote(gu_in.at[:, :, 512 * q : 512 * q + 256], here, sy.at[q], ry.at[yo * 4 + q], core)

    def own_dn():
        return pltpu.make_async_copy(dn_in, dn.at[block_of(z)], loc.at[2])

    def put_dn():
        return remote(dn_in, dn.at[block_of(z)], sy.at[8], ry.at[8], device(x, y, z, c))

    away = jnp.logical_not(at_home)

    def exchange_home():
        for q in range(4):
            for cc in range(2):
                pl.when(at_home & (c == cc))(lambda: own_gu(q).start())
                pl.when(at_home & (c != cc))(lambda: put_y(cc, q).start())
        pl.when(at_home)(lambda: own_dn().start())

    def exchange_away():
        for q in range(4):
            for cc in range(2):
                pl.when(away)(lambda: put_y(cc, q).start())

    def exchange_done():
        for q in range(4):
            for cc in range(2):
                pl.when(away | (c != cc))(lambda: put_y(cc, q).wait_send())
        pl.when(away)(lambda: put_dn().wait_send())

    def exchanged(yo):
        for q in range(4):
            home = at_home & (y == yo)
            pl.when(home)(lambda: own_gu(q).wait())
            pl.when(jnp.logical_not(home))(lambda: got_y(yo, q).wait_recv())

    def serve(k, r):
        for way in (1, -1):
            zb = z + way * r

            @pl.when(inside(zb))
            def _():
                put_e(k, zb, way).wait_recv()
                pl.when(inside(z - way))(lambda: put_e(k, zb, -way).start())

    def first_round(k):
        for way in (-1, 1):
            pl.when(inside(z + way))(lambda: put_e(k, z, way).start())

    exchange_home()

    r_t = routes_in[...]
    prev = prev_in[...]
    flat = jnp.concatenate(
        [jnp.zeros((8, 512), F32), r_t.astype(F32), blk_in[...].astype(F32), jnp.zeros((5, 512), F32), prev, jnp.zeros((104, 512), F32)],
        axis=0,
    )
    scal[...] = flat.T
    bias[...] = jnp.where(blk_in[...].astype(F32) <= scal[:, 10:11], 0.0, -1e30).astype(BF16)
    expert_row = iota((16, 512), 0)
    named = ((expert_row == r_t[0:1]) | (expert_row == r_t[1:2])).astype(BF16)
    upper = (iota((512, 512), 0) < iota((512, 512), 1)).astype(BF16)
    count_t = mm(named, upper).astype(jnp.int32) + expert_row * CAP
    for k, ref in ((0, p0), (1, p1)):
        r = r_t[k : k + 1]
        spot = jnp.sum(jnp.where((expert_row == r) & (r < 4), count_t, 0), axis=0, keepdims=True)
        spot = jnp.where(r < 4, spot, -1)
        ref[...] = (iota((640, 512), 0) == spot).astype(BF16)
    load_cot.wait()
    for ed in range(4):
        rows = slice(ed * CAP, ed * CAP + CAP)
        stage_c[rows, :] = mm(p0[rows, :] + p1[rows, :], cot[...]).astype(BF16)

    for r in range(1, 4):
        if r == 2:
            exchange_away()
        if r == 3:
            exchanged(y)
            first_round(0)
        for way in (1, -1):
            zb = z + way * r
            for u in range(2):

                @pl.when(inside(zb))
                def _():
                    put_z(u, zb, way).wait_recv()
                    pl.when(inside(z - way))(lambda: put_z(u, zb, -way).start())
                    put_1(u, zb).start()
                    put_2(u, units[u][1], zb).start()

    pl.when(away)(lambda: put_dn().start())

    for r in range(4):
        for way in (1, -1) if r else (1,):
            zb = z + way * r
            for u in range(2):

                @pl.when(inside(zb))
                def _():
                    put_1(u, zb, True).wait_recv()
                    put_2(u, 1 - units[u][1], zb).start()

        if r == 2:
            serve(0, 1)

    exchanged(1 - y)
    first_round(1)
    for u in range(2):
        put_c(u, units[u][2]).start()
    pl.when(at_home)(lambda: own_dn().wait())
    pl.when(jnp.logical_not(at_home))(lambda: put_dn().wait_recv())
    first_round(2)
    for u in range(2):
        h1 = units[u][1]
        for hh in (h1, 1 - h1):
            for zb in range(4):
                put_2(u, hh, zb, True).wait_recv()
        put_c(u, 1 - units[u][2]).start()
    for u in range(2):
        for hh in range(2):
            put_c(u, hh, True).wait_recv()

    def assemble(m, _):
        xx, cc, zz = m // 8, (m // 4) % 2, m % 4
        a = [((cc * 2 + xx) * 2 + yy) * 4 + zz for yy in range(2)]
        at = pl.ds(pl.multiple_of(m * 48, 16), 48)
        for j in range(2):
            rows = slice(24 * j, 24 * j + 24)
            w4[j, at, :] = jnp.concatenate([ga[a[0], rows, 0:768], ga[a[1], rows, 0:768]], axis=0)
            w4[2 + j, at, :] = jnp.concatenate([gb[a[0], rows, :], gb[a[1], rows, :]], axis=0)
        smalls[at, :] = jnp.concatenate([ga[a[0], 0:24, 768:896], ga[a[1], 0:24, 768:896]], axis=0)
        return 0

    lax.fori_loop(0, 16, assemble, 0)

    eye = (iota((128, 128), 0) == iota((128, 128), 1)).astype(BF16)
    across = mm(eye, smalls[...], NT)[0:16]
    load_tok.wait()
    for t in range(2):
        rows = slice(256 * t, 256 * t + 256)
        hidden = tok[rows, :].astype(F32)
        scale = lax.rsqrt(jnp.mean(hidden * hidden, axis=-1, keepdims=True) + EPSILON)
        first[rows, :] = (hidden * scale * across[12:13]).astype(BF16)

    def project(i, _):
        j = i // 2
        at = block_of(i % 2)
        qkv[block_of(i), :] = mm(first[at, :], w4[j]).astype(BF16)
        return 0

    lax.fori_loop(0, 6, project, 0)

    expert = x * 2 + y
    me = c * 4 + expert

    def dispatch(stage, landing, sends, recvs, j, got=False):
        eo = (expert + j) % 4
        if got:
            return remote(stage.at[0:CAP], landing.at[c * 4 + eo], sends.at[j], recvs.at[eo], core)
        src = stage.at[pl.ds(pl.multiple_of(eo * CAP, 32), CAP)]
        return remote(src, landing.at[me], sends.at[j], recvs.at[expert], device(eo // 2, c, z, eo % 2))

    def share(landing, sends, recvs, j, got=False):
        eo = (expert + j) % 4
        at = landing.at[((1 - c) if got else c) * 4 + eo]
        return remote(at, at, sends.at[4 + j], recvs.at[4 + eo], core)

    for j in (3, 1, 2):
        dispatch(stage_c, rc, sd, rd, j).start()
    my_rows = pl.ds(pl.multiple_of(expert * CAP, 32), CAP)
    own_c = pltpu.make_async_copy(stage_c.at[my_rows], rc.at[me], own.at[0])
    own_c.start()
    lane = iota((256, 128), 1)

    def head_store(head, half):
        return pltpu.make_async_copy(pbuf.at[half], probs.at[head], lp.at[half])

    def heads(pair, _):
        cols = block_of(pair, 128)
        outs = [[], []]
        for hh in range(2):
            pl.when(pair > 0)(lambda: head_store(2 * pair + hh - 2, hh).wait())
            for t in range(2):
                rows = slice(256 * t, 256 * t + 256)
                q = jnp.where((lane < 64) == (hh == 0), qkv[rows, cols] * BF16(0.125), BF16(0))
                s = mm(q, qkv[512:1024, cols], NT) + bias[rows, :].astype(F32)
                ex = jnp.exp(s - jnp.max(s, axis=-1, keepdims=True))
                p = (ex * (1.0 / jnp.sum(ex, axis=-1, keepdims=True))).astype(BF16)
                pbuf[hh, rows, :] = p
                outs[t].append(mm(p, qkv[1024:1536, cols]))
            head_store(2 * pair + hh, hh).start()
        for t in range(2):
            mixed[256 * t : 256 * t + 256, cols] = jnp.where(lane < 64, outs[t][0], outs[t][1]).astype(BF16)
        return 0

    lax.fori_loop(0, 2, heads, 0)
    serve(1, 1)
    lax.fori_loop(2, 5, heads, 0)
    serve(0, 2)
    lax.fori_loop(5, 6, heads, 0)
    serve(2, 1)
    serve(1, 2)

    lanes = iota((512, 128), 1)
    named_c = ((lanes == scal[:, 8:9].astype(jnp.int32)) | (lanes == scal[:, 9:10].astype(jnp.int32))).astype(BF16)
    lower = (iota((512, 512), 1) < iota((512, 512), 0)).astype(BF16)
    count = mm(lower, named_c) + lanes.astype(F32) * CAP
    for t in range(2):
        rows = slice(256 * t, 256 * t + 256)
        after = tok[rows, :].astype(F32) + mm(mixed[rows, :], w4[3])
        in_grad[rows, :] = after
        scale = lax.rsqrt(jnp.mean(after * after, axis=-1, keepdims=True) + EPSILON)
        second[rows, :] = (after * scale * across[13:14]).astype(BF16)
        score = mm(second[rows, :], smalls[...])
        r = (scal[rows, 8:9].astype(jnp.int32), scal[rows, 9:10].astype(jnp.int32))
        lane8 = iota((256, 8), 1)
        logits = score[:, 0:8] + scal[rows, 16:24]
        picked = [jnp.sum(jnp.where(lane8 == r[k], logits, 0.0), axis=-1, keepdims=True) for k in range(2)]
        g0 = jax.nn.sigmoid(picked[0] - picked[1])
        values = [g0, 1.0 - g0]
        for m in range(2):
            diff = score[:, 8 + 2 * m : 9 + 2 * m] - score[:, 9 + 2 * m : 10 + 2 * m]
            values += [jax.nn.sigmoid(diff), jax.nn.sigmoid(-diff)]
        for k in range(2):
            spot = jnp.sum(jnp.where(lane == r[k], count[rows], 0.0), axis=-1, keepdims=True)
            values.append(jnp.where(r[k] < 4, spot, -1.0))
        filled = scal[rows, :]
        for i, v in enumerate(values):
            filled = jnp.where(lane == i, v, filled)
        scal[rows, :] = filled

    def three_lanes(v, width):
        hi, mid, lo = split3(v)
        zero, at = BF16(0), iota((width, 128), 1)
        return jnp.where(at == 0, hi, zero) + jnp.where(at == 1, mid, zero) + jnp.where(at == 2, lo, zero)

    parts = [three_lanes(scal[:, k : k + 1], 512) for k in range(2)]
    for j in (3, 1, 2, 0):
        eo = (expert + j) % 4
        at = pl.ds(pl.multiple_of(eo * CAP, 32), CAP)
        stage_x[at, 0:768] = mm(p0[at, :] + p1[at, :], second[...]).astype(BF16)
        stage_x[at, 768:896] = (mm(p0[at, :], parts[0]) + mm(p1[at, :], parts[1])).astype(BF16)
        if j:
            dispatch(stage_x, rx, sx, rx_, j).start()
    own_x = pltpu.make_async_copy(stage_x.at[my_rows], rx.at[me], own.at[1])
    own_x.start()
    own_c.wait()
    share(rc, sd, rd, 0).start()
    for j in (1, 2, 3):
        dispatch(stage_c, rc, sd, rd, j, True).wait_recv()
        share(rc, sd, rd, j).start()
    own_x.wait()
    share(rx, sx, rx_, 0).start()
    for u in range(2):
        for zb in range(4):
            put_1(u, zb).wait_send()
            put_2(u, 0, zb).wait_send()
            put_2(u, 1, zb).wait_send()
            pl.when((zb >= z) & (z > 0))(lambda: put_z(u, zb, -1).wait_send())
            pl.when((zb <= z) & (z < 3))(lambda: put_z(u, zb, 1).wait_send())
        for hh in range(2):
            put_c(u, hh).wait_send()
    for hh in range(2):
        head_store(10 + hh, hh).wait()
    for j in (1, 2, 3):
        dispatch(stage_x, rx, sx, rx_, j, True).wait_recv()
        share(rx, sx, rx_, j).start()
    serve(2, 2)
    for j in range(4):
        share(rc, sd, rd, j, True).wait_recv()
        share(rc, sd, rd, j).wait_send()
        share(rx, sx, rx_, j, True).wait_recv()
        share(rx, sx, rx_, j).wait_send()
        if j:
            dispatch(stage_c, rc, sd, rd, j).wait_send()
            dispatch(stage_x, rx, sx, rx_, j).wait_send()

    def scaled(i, _):
        g = jnp.sum(rx[i, :, 768:896].astype(F32), axis=-1, keepdims=True)
        deo[pl.ds(pl.multiple_of(i * CAP, 32), CAP), :] = (g * rc[i].astype(F32)).astype(BF16)
        return 0

    lax.fori_loop(0, 8, scaled, 0)
    for t in range(5):
        turned[:, 256 * t : 256 * t + 256] = rx2[256 * t : 256 * t + 256, 0:768].T

    def nth(n):
        one = jnp.where(n == 0, 1, jnp.where(n == 1, 0, n))
        two = jnp.where(n == 0, 2, jnp.where(n == 1, 3, 3 - n))
        return jnp.where(z == 0, n, jnp.where(z == 3, 3 - n, jnp.where(z == 1, one, two)))

    def hidden_part(n):
        q = nth(n)
        cols = block_of(q)

        def some(i, _):
            at = pl.ds(pl.multiple_of(i * 320, 64), 320)
            rows = rx2[at, 0:768]
            u, w = mm(rows, gu[0, :, cols]), mm(rows, gu[1, :, cols])
            dact = mm(deo[at, :], dn[cols, :], NT)
            sig = jax.nn.sigmoid(u)
            silu = u * sig
            act[at, cols] = (silu * w).astype(BF16)
            dgate2[at, cols] = (dact * w * sig * (1.0 + u * (1.0 - sig))).astype(BF16)
            dup2[at, cols] = (dact * silu).astype(BF16)
            return 0

        lax.fori_loop(0, 4, some, 0)

    def is_down(k):
        return isinstance(k, int) and k == 4

    def put_g(zb, k, up):
        land = zb if up else jnp.where(zb == z - 1, 4, zb)
        src, dst = (gdn.at[zb], rdn.at[land]) if is_down(k) else (ggu.at[zb, k], rgu.at[land, k])
        to = device(x, c, jnp.clip(z + (1 if up else -1), 0, 3), y)
        return remote(src, dst, sg.at[zb * 5 + k], rg.at[land * 5 + k], to)

    def got_g(land, k):
        src, dst = (gdn.at[0], rdn.at[land]) if is_down(k) else (ggu.at[0, k], rgu.at[land, k])
        return remote(src, dst, sg.at[k], rg.at[land * 5 + k], core)

    def grad_part(n):
        q = nth(n)
        cols = block_of(q)
        for i, ref in ((0, dgate2), (1, dup2)):
            for h in range(2):
                got = mm(turned[384 * h : 384 * h + 384, :], ref[0:1280, cols]).astype(BF16)
                for s in range(4):
                    ggu[2 * h + s // 2, q, s % 2, i] = got[96 * s : 96 * s + 96]
        gdn[q] = mm(act[0:1280, cols], deo[...], TN).astype(BF16)

    def first_send(n):
        far = {
            0: ((3, 0), (2, 0), (1, 0)),
            1: ((3, 1), (2, 1), (1, 1)),
            2: ((3, 2), (2, 2)),
            3: ((3, 3), (3, 4), (2, 3), (2, 4), (1, 2), (1, 3), (1, 4)),
        }

        def up(i):
            for zb, k in far[i]:
                put_g(zb, k, True).start()

        def down(i):
            for zb, k in far[i]:
                put_g(3 - zb, k if k == 4 else 3 - k, False).start()

        for i in range(4):
            pl.when((z == 0) & (n == i))(lambda: up(i))
            pl.when((z == 3) & (n == i))(lambda: down(i))

    def add_block(zb, land, k):
        if is_down(k):
            gdn[zb] = (gdn[zb].astype(F32) + rdn[land].astype(F32)).astype(BF16)
        else:
            ggu[zb, k] = (ggu[zb, k].astype(F32) + rgu[land, k].astype(F32)).astype(BF16)

    def pass_on(zb, k, up, at):
        @pl.when(z == at)
        def _():
            got_g(zb, k).wait_recv()
            add_block(zb, zb, k)
            put_g(zb, k, up).start()

    def hop1(n):
        for zb, k in ((3, n), (2, n)) if n < 3 else ((3, 3), (3, 4), (2, 3), (2, 4)):
            pass_on(zb, k, True, 1)
            pass_on(3 - zb, k if k == 4 else 3 - k, False, 2)

    def hop2(n):
        for k in (n,) if n < 3 else (3, 4):
            pass_on(3, k, True, 2)
            pass_on(0, k if k == 4 else 3 - k, False, 1)

    def early(n, _):
        hidden_part(n)
        grad_part(n)
        first_send(n)
        return 0

    def middle(n, _):
        pl.when(n == 3)(lambda: serve(2, 3))
        hidden_part(n)
        return 0

    def late(n, _):
        grad_part(n)
        first_send(n)
        return 0

    def halve(src, landing, sends, recvs, k):
        return remote(src.at[(1 - c) * 4 + k], landing.at[k], sends.at[k], recvs.at[k], core)

    def back(src, landing, sends, recvs, j, got=False):
        eo = (expert + j) % 4
        if got:
            return remote(src.at[0], landing.at[eo], sends.at[4 + j], recvs.at[4 + eo], core)
        return remote(
            src.at[c * 4 + eo], landing.at[expert], sends.at[4 + j], recvs.at[4 + expert], device(eo // 2, c, z, eo % 2)
        )

    def own_back(src, landing, i):
        return pltpu.make_async_copy(src.at[me], landing.at[expert], own.at[i])

    def wait_back(src, landing, sends, recvs, i):
        own_back(src, landing, i).wait()
        for j in (1, 2, 3):
            back(src, landing, sends, recvs, j, True).wait_recv()

    def row_part(i, _):
        group = jnp.where(i < 2, 1 - c, c)
        at = pl.ds(pl.multiple_of((group * 4 + 2 * (i % 2)) * CAP, 64), 320)
        dbuf = mm(dgate2[at, :], gu[0], NT) + mm(dup2[at, :], gu[1], NT)
        rx2[at, 0:768] = dbuf.astype(BF16)
        eo = mm(act[at, :], dn[...])
        dg = jnp.sum(eo * rc2[at, :].astype(F32), axis=-1, keepdims=True)
        rx2[at, 768:896] = three_lanes(dg, 320)
        rc2[at, :] = eo.astype(BF16)

        @pl.when(i < 2)
        def _():
            for k in (2 * i, 2 * i + 1):
                halve(rx, half_b, sb, rb, k).start()

        return 0

    def join(j, _):
        eo = (expert + j) % 4
        halve(rx, half_b, sb, rb, eo).wait_recv()
        at = c * 4 + eo
        more = rx[at, :, 768:896].astype(F32) + half_b[eo, :, 768:896].astype(F32)
        rx[at, :, 768:896] = three_lanes(jnp.sum(more, axis=-1, keepdims=True), CAP)
        rx[at, :, 0:768] = (rx[at, :, 0:768].astype(F32) + half_b[eo, :, 0:768].astype(F32)).astype(BF16)
        pl.when(j != 0)(lambda: back(rx, land_b, sb, rb, j).start())
        pl.when(j == 0)(lambda: own_back(rx, land_b, 2).start())
        return 0

    def join_out(j, _):
        eo = (expert + j) % 4
        halve(rc, half_e, sv, rv, eo).wait_recv()
        at = c * 4 + eo
        rc[at] = (rc[at].astype(F32) + half_e[eo].astype(F32)).astype(BF16)
        pl.when(j != 0)(lambda: back(rc, land_e, sv, rv, j).start())
        pl.when(j == 0)(lambda: own_back(rc, land_e, 3).start())
        return 0

    serve(0, 3)
    serve(1, 3)
    lax.fori_loop(0, 2, early, 0)
    lax.fori_loop(2, 4, middle, 0)
    lax.fori_loop(0, 4, row_part, 0)
    lax.fori_loop(1, 4, join, 0)
    lax.fori_loop(0, 1, join, 0)
    for k in range(4):
        halve(rc, half_e, sv, rv, k).start()
    lax.fori_loop(2, 4, late, 0)

    for t in range(2):
        rows = slice(256 * t, 256 * t + 256)
        turned[:, 512 + 256 * t : 768 + 256 * t] = mixed[rows, :].T
        hidden = tok[rows, :].astype(F32)
        scale = lax.rsqrt(jnp.mean(hidden * hidden, axis=-1, keepdims=True) + EPSILON)
        turned[:, rows] = (hidden * scale * across[12:13]).astype(BF16).T

    def head_load(head, half):
        return pltpu.make_async_copy(probs.at[head], pbuf.at[half], lp.at[half])

    head_load(0, 0).start()
    hop1(0)
    wait_back(rx, land_b, sb, rb, 2)
    lax.fori_loop(0, 4, join_out, 0)
    hop1(1)
    hop2(0)

    def of_tile(rows):
        at = lambda i: scal[rows, i : i + 1]
        r = (at(8).astype(jnp.int32), at(9).astype(jnp.int32))
        place = [(iota((256, 640), 1) == at(6 + k).astype(jnp.int32)).astype(BF16) for k in range(2)]
        return (at(0), at(1)), ((at(2), at(3)), (at(4), at(5))), r, place

    total = jnp.zeros((128, 768), F32)
    gain_two = jnp.zeros((1, 768), F32)
    for t in range(2):
        rows = slice(256 * t, 256 * t + 256)
        g, a, r, place = of_tile(rows)
        dsec = jnp.zeros((256, 768), F32)
        dg = [jnp.zeros((256, 1), F32)] * 2
        got = land_b.reshape(640, 896)
        dsec = dsec + mm(place[0] + place[1], got[:, 0:768])
        for k in range(2):
            dg[k] = dg[k] + jnp.sum(mm(place[k], got[:, 768:896]), axis=-1, keepdims=True)
        dx2 = cot[rows, :].astype(F32)
        sec = second[rows, :].astype(F32)
        dot_s = jnp.sum(dx2 * sec, axis=-1, keepdims=True)
        coef = jnp.zeros((256, 1), F32)
        dz = jnp.zeros((256, 128), F32)
        for k in range(2):
            dg[k] = dg[k] + jnp.where(r[k] == 5, dot_s, 0.0)
            coef = coef + jnp.where(r[k] == 5, g[k], 0.0)
        const = jnp.zeros((256, 128), F32)
        for m in range(2):
            dot_v = jnp.sum(dx2 * across[14 + m : 15 + m], axis=-1, keepdims=True)
            weight = jnp.zeros((256, 1), F32)
            for k in range(2):
                chosen = r[k] == 6 + m
                dg[k] = dg[k] + jnp.where(chosen, a[m][0] * dot_s + a[m][1] * dot_v, 0.0)
                weight = weight + jnp.where(chosen, g[k], 0.0)
            coef = coef + a[m][0] * weight
            const = const + jnp.where(lane == 14 + m, a[m][1] * weight, 0.0)
            da = (weight * dot_s, weight * dot_v)
            mean = a[m][0] * da[0] + a[m][1] * da[1]
            for i in range(2):
                dz = jnp.where(lane == 8 + 2 * m + i, a[m][i] * (da[i] - mean), dz)
        diff = g[0] * g[1] * (dg[0] - dg[1])
        dz = dz + jnp.where(lane == r[0], diff, 0.0) - jnp.where(lane == r[1], diff, 0.0)
        gate_grad[:, rows] = dz.T[0:8]
        hi, mid, _ = split3(dz)
        dsec = dsec + coef * dx2 + mm(hi, smalls[...], NT) + mm(mid, smalls[...], NT)
        total = total + mm(hi, second[rows, :], TN) + mm(mid, second[rows, :], TN)
        hi, mid, _ = split3(const)
        total = total + mm(hi, cot[rows, :], TN) + mm(mid, cot[rows, :], TN)
        after = in_grad[rows, :]
        scale = lax.rsqrt(jnp.mean(after * after, axis=-1, keepdims=True) + EPSILON)
        normal = after * scale
        gain_two = gain_two + jnp.sum(dsec * normal, axis=0, keepdims=True)
        lift = dsec * across[13:14]
        dx1 = dx2 + scale * (lift - normal * jnp.mean(lift * normal, axis=-1, keepdims=True))
        in_grad[rows, :] = dx1
        deo[rows, :] = mm(dx1.astype(BF16), w4[3], NT).astype(BF16)
    row16 = iota((16, 768), 0)
    sm[...] = total[0:16] + jnp.where(row16 == 13, gain_two, 0.0)
    hop1(2)
    hop2(1)

    def place_a(d):
        xx, cc, zz, yy = d // 16, (d // 8) % 2, (d // 2) % 4, d % 2
        return ((cc * 2 + xx) * 2 + yy) * 4 + zz

    def place_b(d):
        xx, cc, zz, yy = d // 16, (d // 8) % 2, (d // 2) % 4, d % 2
        return ((cc * 2 + yy) * 2 + xx) * 4 + zz

    def stage(ref, place_of, i, left, right, cols):
        for h in range(2):
            got = mm(turned[384 * h : 384 * h + 384, left], right).astype(BF16)
            for d in range(16):
                ref[place_of(16 * h + d), 24 * i : 24 * i + 24, cols] = got[24 * d : 24 * d + 24]

    groups = [slice(256 * g, 256 * g + 256) for g in range(3)]
    for g in range(3):
        stage(dup, place_b, 1, slice(512, 1024), in_grad[:, groups[g]].astype(BF16), groups[g])

    stages = (dgate, dup)
    owners = (
        (ga, y, x, device(x, c, z, 1 - y), device(1 - x, c, z, y)),
        (gb, x, y, device(1 - x, c, z, y), device(x, c, z, 1 - y)),
    )

    def give_c(u, hh, g):
        src = stages[u].at[pl.ds(((1 - c) * 2 + hh) * 8, 8), :, groups[g]]
        i = (u * 2 + hh) * 3 + g
        return remote(src, owners[u][0].at[pl.ds(hh * 8, 8), :, groups[g]], tc.at[i], qc.at[i], core)

    def give_2(u, hh, g):
        h2 = owners[u][2]
        src = stages[u].at[pl.ds(((c * 2 + 1 - h2) * 2 + hh) * 4, 4), :, groups[g]]
        i = (u * 2 + hh) * 3 + g
        return remote(src, owners[u][0].at[pl.ds(16 + hh * 4, 4), :, groups[g]], t2.at[i], q2.at[i], owners[u][4])

    def give_1(u, g):
        h1, h2 = owners[u][1:3]
        src = stages[u].at[pl.ds(((c * 2 + h2) * 2 + 1 - h1) * 4, 4), :, groups[g]]
        return remote(src, owners[u][0].at[24:28, :, groups[g]], t1.at[u * 3 + g], q1.at[u * 3 + g], owners[u][3])

    def base(u):
        return ((c * 2 + owners[u][2]) * 2 + owners[u][1]) * 4

    def give_z(u, zb, up, g):
        land = zb if up else jnp.where(zb == z - 1, 4, zb)
        to = device(x, c, jnp.clip(z + (1 if up else -1), 0, 3), y)
        src = stages[u].at[base(u) + zb, :, groups[g]]
        return remote(src, z_in.at[u, land, :, groups[g]], tz.at[(u * 4 + zb) * 3 + g], qz.at[(u * 5 + land) * 3 + g], to)

    def come_z(u, land, g):
        src = stages[u].at[0, :, groups[g]]
        return remote(src, z_in.at[u, land, :, groups[g]], tz.at[g], qz.at[(u * 5 + land) * 3 + g], core)

    def add_in(u, at, n, other, g):
        def one(i, _):
            got = owners[u][0][other + i, :, groups[g]]
            stages[u][at + i, :, groups[g]] = (stages[u][at + i, :, groups[g]].astype(F32) + got.astype(F32)).astype(BF16)
            return 0

        lax.fori_loop(0, n, one, 0)

    def step_c(g):
        for u in range(2):
            h2 = owners[u][2]
            give_c(u, 1 - h2, g).start()
            give_c(u, h2, g).start()

    def step_2(g):
        for u in range(2):
            h1, h2 = owners[u][1:3]
            give_c(u, 1 - h2, g).wait_recv()
            add_in(u, (c * 2 + 1 - h2) * 8, 8, (1 - h2) * 8, g)
            for hh in (1 - h1, h1):
                give_2(u, hh, g).start()
        for u in range(2):
            h2 = owners[u][2]
            give_c(u, h2, g).wait_recv()
            add_in(u, (c * 2 + h2) * 8, 8, h2 * 8, g)

    def step_1(g):
        for u in range(2):
            h1, h2 = owners[u][1:3]
            give_2(u, 1 - h1, g).wait_recv()
            add_in(u, ((c * 2 + h2) * 2 + 1 - h1) * 4, 4, 16 + (1 - h1) * 4, g)
            give_1(u, g).start()
        for u in range(2):
            h1, h2 = owners[u][1:3]
            give_2(u, h1, g).wait_recv()
            add_in(u, base(u), 4, 16 + h1 * 4, g)

    def step_z(g):
        for u in range(2):
            give_1(u, g).wait_recv()
            add_in(u, base(u), 4, 24, g)
            for i in range(3):
                pl.when(z == 0)(lambda: give_z(u, 3 - i, True, g).start())
                pl.when(z == 3)(lambda: give_z(u, i, False, g).start())

    def pass_z(zb, up, at, g):
        @pl.when(z == at)
        def _():
            for u in range(2):
                come_z(u, zb, g).wait_recv()
                i = base(u) + zb
                got = z_in[u, zb, :, groups[g]]
                stages[u][i, :, groups[g]] = (stages[u][i, :, groups[g]].astype(F32) + got.astype(F32)).astype(BF16)
                give_z(u, zb, up, g).start()

    def hop1_z(g):
        for zb in (3, 2):
            pass_z(zb, True, 1, g)
            pass_z(3 - zb, False, 2, g)

    def hop2_z(g):
        pass_z(3, True, 2, g)
        pass_z(0, False, 1, g)

    lane5 = iota((512, 128), 1)

    def heads_back(pair, _):
        cols = block_of(pair, 128)
        grads = []
        for hh in range(2):
            head_load(2 * pair + hh, hh).wait()
            if hh == 0:
                head_load(2 * pair + 1, 1).start()
            else:
                pl.when(pair < 5)(lambda: head_load(2 * pair + 2, 0).start())
            do = jnp.where((lane5 < 64) == (hh == 0), deo[0:512, cols], BF16(0))
            inner = jnp.sum(do.astype(F32) * mixed[:, cols].astype(F32), axis=-1, keepdims=True)
            dq, dk, dv = [], jnp.zeros((512, 128), F32), jnp.zeros((512, 128), F32)
            for t in range(2):
                rows = slice(256 * t, 256 * t + 256)
                p = pbuf[hh, rows, :]
                ds = (p.astype(F32) * (mm(do[rows], qkv[1024:1536, cols], NT) - inner[rows])).astype(BF16)
                dq.append(mm(ds, qkv[512:1024, cols]))
                dk = dk + mm(ds, qkv[rows, cols], TN)
                dv = dv + mm(p, deo[rows, cols], TN)
            grads.append((jnp.concatenate(dq, axis=0) * 0.125, dk * 0.125, dv))
        for j in range(3):
            act[512 * j : 512 * j + 512, cols] = jnp.where(lane5 < 64, grads[0][j], grads[1][j]).astype(BF16)
        return 0

    for g in range(3):
        lax.fori_loop(2 * g, 2 * g + 2, heads_back, 0)
        for ref, place_of, i, j in ((dgate, place_a, 0, 0), (dgate, place_a, 1, 1), (dup, place_b, 0, 2)):
            stage(ref, place_of, i, slice(0, 512), act[512 * j : 512 * j + 512, groups[g]], groups[g])
        step_c(g)
        if g == 0:
            hop2(2)
        if g == 1:
            step_2(0)
        if g == 2:
            step_2(1)
            step_1(0)
            hop1(3)

    gain_one = jnp.zeros((1, 768), F32)
    for t in range(2):
        rows = slice(256 * t, 256 * t + 256)
        dfirst = mm(act[256 * t : 256 * t + 256, 0:768], w4[0], NT)
        dfirst = dfirst + mm(act[512 + 256 * t : 768 + 256 * t, 0:768], w4[1], NT)
        dfirst = dfirst + mm(act[1024 + 256 * t : 1280 + 256 * t, 0:768], w4[2], NT)
        hidden = tok[rows, :].astype(F32)
        scale = lax.rsqrt(jnp.mean(hidden * hidden, axis=-1, keepdims=True) + EPSILON)
        normal = hidden * scale
        gain_one = gain_one + jnp.sum(dfirst * normal, axis=0, keepdims=True)
        lift = dfirst * across[12:13]
        in_grad[rows, :] = in_grad[rows, :] + scale * (lift - normal * jnp.mean(lift * normal, axis=-1, keepdims=True))
    sm[...] = sm[...] + jnp.where(row16 == 12, gain_one, 0.0)

    def small_step(i):
        to = (core, device(1 - x, c, z, y), device(x, c, z, 1 - y))[i]
        return remote(sm.at[...], sm_in.at[i], ss.at[i], rs.at[i], to)

    def small_z(way, got=False):
        zt = lax.rem(z + way, 4)
        if got:
            zt = lax.rem(z - way + 4, 4)
            return remote(sm.at[...], sm_in.at[3 + zt], ss.at[2 + way], rs.at[3 + zt], core)
        return remote(sm.at[...], sm_in.at[3 + z], ss.at[2 + way], rs.at[3 + z], device(x, c, zt, y))

    def swap(q, yo):
        at = gu_out.at[:, :, block_of(2 * q + c)]
        return remote(ggu.at[z, q, yo], at, sw.at[q * 2 + yo], rw.at[q * 2 + c], device(x, y, z, yo))

    def swap_got(q, cc):
        at = gu_out.at[:, :, 512 * q + 256 * cc : 512 * q + 256 * cc + 256]
        return remote(ggu.at[z, q, 0], at, sw.at[q * 2], rw.at[q * 2 + cc], core)

    def keep(q):
        return pltpu.make_async_copy(ggu.at[z, q, y], gu_out.at[:, :, block_of(2 * q + c)], loc.at[3 + q])

    def swap_dn():
        return remote(gdn.at[z], dn_out, sw.at[8], rw.at[8], device(x, y, z, c))

    def keep_dn():
        return pltpu.make_async_copy(gdn.at[z], dn_out, loc.at[2])

    def final(n):
        k = 4 if n == 4 else jnp.where(z % 2 == 0, 3 - n, n)

        @pl.when(z > 0)
        def _():
            got_g(z, k).wait_recv()
            add_block(z, z, k)

        @pl.when(z < 3)
        def _():
            got_g(4, k).wait_recv()
            add_block(z, 4, k)

        if n < 4:
            for yo in range(2):
                home = at_home & (y == yo)
                pl.when(home)(lambda: keep(k).start())
                pl.when(jnp.logical_not(home))(lambda: swap(k, yo).start())
        else:
            pl.when(at_home)(lambda: keep_dn().start())
            pl.when(jnp.logical_not(at_home))(lambda: swap_dn().start())

    small_step(0).start()
    step_2(2)
    step_1(1)
    step_z(0)
    small_step(0).wait()
    sm[...] = sm[...] + sm_in[0]
    small_step(1).start()
    wait_back(rc, land_e, sv, rv, 3)
    for t in range(2):
        rows = slice(256 * t, 256 * t + 256)
        g, a, r, place = of_tile(rows)
        result = tok[rows, :].astype(F32) + mm(mixed[rows, :], w4[3])
        coef = jnp.zeros((256, 1), F32)
        for k in range(2):
            result = result + g[k] * mm(place[k], land_e.reshape(640, 768)[...])
            coef = coef + jnp.where(r[k] == 5, g[k], 0.0)
        for m in range(2):
            weight = jnp.zeros((256, 1), F32)
            for k in range(2):
                weight = weight + jnp.where(r[k] == 6 + m, g[k], 0.0)
            coef = coef + a[m][0] * weight
            result = result + a[m][1] * weight * across[14 + m : 15 + m]
        out[rows, :] = (result + coef * second[rows, :].astype(F32)).astype(BF16)

    step_1(2)
    hop2(3)
    step_z(1)
    small_step(1).wait()
    sm[...] = sm[...] + sm_in[1]
    small_step(2).start()
    step_z(2)
    small_step(2).wait()
    sm[...] = sm[...] + sm_in[2]
    for way in (1, 2, 3):
        small_z(way).start()
    final(0)
    final(1)
    hop1_z(0)
    hop1_z(1)
    hop2_z(0)
    hop1_z(2)
    final(2)
    hop2_z(1)
    hop2_z(2)
    final(3)
    final(4)

    for way in (1, 2, 3):
        small_z(way, True).wait_recv()
    result = sm[...]
    for way in (1, 2, 3):
        result = result + sm_in[3 + lax.rem(z + way, 4)]
    chosen = (iota((768, 128), 0) == iota((768, 128), 1) + 24 * (e * 8 + z * 2 + y)).astype(BF16)
    result = sum(mm(part, chosen) for part in split3(result))
    router_grad[...] = result[0:12, 0:24]
    gain_grad[...] = result[12:14, 0:24]
    const_grad[...] = result[14:16, 0:24]

    for u, ref in ((0, (attn_in_grad.at[0], attn_in_grad.at[1])), (1, (attn_in_grad.at[2], attn_out_grad))):
        for i in range(2):
            ref[i][...] = stages[u][base(u) + z, 24 * i : 24 * i + 24, 0:768].astype(F32)
        for land, there in ((z, z > 0), (4, z < 3)):

            @pl.when(there)
            def _():
                for g in range(3):
                    come_z(u, land, g).wait_recv()
                for i in range(2):
                    ref[i][...] = ref[i][...] + z_in[u, land, 24 * i : 24 * i + 24, :].astype(F32)

    for q in range(4):
        pl.when(at_home)(lambda: keep(q).wait())
        for i in range(2):
            pl.when(jnp.logical_not(at_home & (y == i)))(lambda: swap(q, i).wait_send())
            pl.when(jnp.logical_not(at_home & (c == i)))(lambda: swap_got(q, i).wait_recv())
    pl.when(at_home)(lambda: keep_dn().wait())
    pl.when(jnp.logical_not(at_home))(lambda: swap_dn().wait())
    exchange_done()
    for way in (1, 2, 3):
        small_z(way).wait_send()
    for k in range(4):
        halve(rx, half_b, sb, rb, k).wait_send()
        halve(rc, half_e, sv, rv, k).wait_send()
        if k:
            back(rx, land_b, sb, rb, k).wait_send()
            back(rc, land_e, sv, rv, k).wait_send()

    for zb in range(4):
        for k in range(3):
            pl.when((zb >= z) & (z > 0))(lambda: put_e(k, zb, -1).wait_send())
            pl.when((zb <= z) & (z < 3))(lambda: put_e(k, zb, 1).wait_send())
        for k in range(5):
            pl.when(zb > z)(lambda: put_g(zb, k, True).wait_send())
            pl.when(zb < z)(lambda: put_g(zb, k, False).wait_send())
        for u in range(2):
            for g in range(3):
                pl.when(zb > z)(lambda: give_z(u, zb, True, g).wait_send())
                pl.when(zb < z)(lambda: give_z(u, zb, False, g).wait_send())
    for u in range(2):
        for g in range(3):
            give_1(u, g).wait_send()
            for hh in range(2):
                give_c(u, hh, g).wait_send()
                give_2(u, hh, g).wait_send()


def small_body(
    tokens, gate_input, routes, block_ids, cotangent, norm_gain, attn_in, attn_out, router, const_vec, expert_gu, expert_down
):
    out = lambda *shape, t=F32: jax.ShapeDtypeStruct(shape, t)
    dma = lambda n: pltpu.SemaphoreType.DMA((n,))
    mem = lambda *shape, t=BF16: pltpu.VMEM(shape, t)
    vm = pl.BlockSpec(memory_space=pltpu.VMEM)
    hbm = pl.BlockSpec(memory_space=pl.ANY)
    outs = pl.pallas_call(
        layer_kernel,
        out_shape=(
            out(512, 768, t=BF16), out(512, 768), out(8, 512), out(3, 24, 768), out(24, 768), out(12, 24), out(2, 24), out(2, 24),
            out(2, 96, 2048, t=BF16), out(256, 768, t=BF16), out(12, 512, 512, t=BF16),
        ),
        in_specs=[vm] * 8 + [hbm] * 4,
        out_specs=(vm,) * 8 + (hbm,) * 3,
        scratch_shapes=[
            mem(512, 768), mem(512, 768), mem(2, 768, 1024), mem(1024, 768), mem(4, 768, 768), mem(768, 128),
            mem(32, 48, 896), mem(32, 48, 768), mem(1536, 768), mem(1536, 1024), mem(32, 48, 1024), mem(32, 48, 1024),
            mem(1280, 768), mem(768, 1280), mem(8, CAP, 896), mem(8, CAP, 768),
            mem(4, 4, 2, 2, 96, 256), mem(4, 256, 768), mem(5, 4, 2, 2, 96, 256), mem(5, 256, 768),
            mem(4, CAP, 896), mem(4, CAP, 768), mem(4, CAP, 896), mem(4, CAP, 768), mem(2, 512, 512), mem(512, 768), mem(512, 768), mem(512, 128, t=F32),
            mem(2, 5, 48, 768), mem(16, 768, t=F32), mem(7, 16, 768, t=F32),
            *(dma(n) for n in (8, 16, 8, 8, 8, 16, 16, 4, 4, 24, 12, 9, 9, 8, 8, 8, 8, 4)),
            *(dma(n) for n in (8, 8, 8, 8, 20, 25, 9, 9, 2, 12, 12, 12, 12, 6, 6, 24, 30, 6, 7)),
        ],
        compiler_params=pltpu.CompilerParams(has_side_effects=True, collective_id=0, vmem_limit_bytes=63_200_000),
        name="layer",
    )(
        attn_in[0], attn_out[0], router[0].T, norm_gain[0], const_vec[0], routes.T, gate_input.T, block_ids,
        tokens, cotangent, expert_gu[0, 0], expert_down[0, 0],
    )
    result, in_grad, gate, ai, ao, ro, ng, cv, gu, dn, _ = outs
    return (
        result, in_grad, gate.T, ng[None], ai[None], ao[None], ro.T[None], cv[None],
        gu.astype(F32)[None, None], dn.astype(F32)[None, None],
    )


LAYERS = 1
HIGHEST = lax.Precision.HIGHEST


def normed(values):
    inv_scale = lax.rsqrt(jnp.mean(values * values, axis=-1, keepdims=True) + EPSILON)
    return (values * inv_scale, inv_scale)


def norm_back(upstream, normal, inv_scale):
    return inv_scale * (upstream - normal * jnp.mean(upstream * normal, axis=-1, keepdims=True))


def slot_table(route_pair, ffn_count, capacity):
    flat_route = route_pair.reshape(-1)
    pair_count = flat_route.shape[0]
    one_hot = (flat_route[:, None] == jnp.arange(ffn_count, dtype=jnp.int32)[None, :]).astype(
        jnp.int32
    )
    earlier = jnp.arange(pair_count)[None, :] < jnp.arange(pair_count)[:, None]
    running = jnp.dot(
        earlier.astype(jnp.bfloat16), one_hot.astype(jnp.bfloat16), preferred_element_type=jnp.float32
    ).astype(jnp.int32)
    position = jnp.sum(running * one_hot, axis=1)
    is_routed = flat_route < ffn_count
    destination = jnp.where(is_routed, flat_route * capacity + position, ffn_count * capacity)
    pair_index = jnp.arange(pair_count, dtype=jnp.int32)
    owner_pair = (
        jnp.zeros((ffn_count * capacity,), jnp.int32).at[destination].set(pair_index, mode="drop")
    )
    filled = (
        jnp.zeros((ffn_count * capacity,), jnp.int32)
        .at[destination]
        .set(jnp.ones_like(pair_index), mode="drop")
    )
    return (destination, is_routed, owner_pair, filled)


def masked_scores(queries, key_rows, allowed):
    raw_scores = (
        jnp.einsum("thd,shd->hts", queries, key_rows, preferred_element_type=jnp.float32) * 0.125
    )
    return jnp.where(allowed[None, :, :], raw_scores, -1e30)


def layer_forward(hidden, previous, route_pair, blocks, dense_set, expert_set):
    w_in, w_out, gain_rows, w_router, vectors = dense_set
    w_gate_up, w_down = expert_set
    tok_count, model_width = hidden.shape
    head_size = model_width // H
    experts = previous.shape[1]
    gain_float = gain_rows.astype(jnp.float32)
    normal_one, scale_one = normed(hidden)
    first_in = (normal_one * gain_float[0]).astype(jnp.bfloat16)
    projected = jnp.einsum(
        "td,jde->jte", first_in, w_in, preferred_element_type=jnp.float32
    ).astype(jnp.bfloat16)
    projected = projected.reshape(3, tok_count, H, head_size)
    queries, key_rows, value_rows = (projected[0], projected[1], projected[2])
    allowed = blocks[None, :] <= blocks[:, None]
    raw_scores = masked_scores(queries, key_rows, allowed)
    row_peak = jnp.max(raw_scores, axis=-1, keepdims=True)
    log_total = row_peak + jnp.log(jnp.sum(jnp.exp(raw_scores - row_peak), axis=-1, keepdims=True))
    attn_probs = jnp.exp(raw_scores - log_total).astype(jnp.bfloat16)
    mixed_heads = jnp.einsum(
        "hts,shd->thd", attn_probs, value_rows, preferred_element_type=jnp.float32
    )
    mixed_heads = mixed_heads.reshape(tok_count, model_width).astype(jnp.bfloat16)
    after_attn = hidden + jnp.dot(mixed_heads, w_out, preferred_element_type=jnp.float32)
    normal_two, scale_two = normed(after_attn)
    second_in = (normal_two * gain_float[1]).astype(jnp.bfloat16)
    second_float = second_in.astype(jnp.float32)
    all_logits = jnp.dot(second_in, w_router, preferred_element_type=jnp.float32)
    logits = all_logits[:, :experts] + previous
    picked = route_pair[:, :, None] == jnp.arange(experts, dtype=jnp.int32)[None, None, :]
    chosen = jnp.sum(jnp.where(picked, logits[:, None, :], 0.0), axis=-1)
    first_gate = jax.nn.sigmoid(chosen[:, 0] - chosen[:, 1])
    gate_pair = jnp.stack([first_gate, 1.0 - first_gate], axis=1)
    const_weights = jax.nn.softmax(all_logits[:, experts:].reshape(tok_count, 2, 2), axis=-1)
    ffn_count = lax.axis_size("expert")
    destination, is_routed, owner_pair, filled = slot_table(route_pair, ffn_count, CAP)
    has_row = filled[:, None] > 0
    send_rows = jnp.where(has_row, second_in[owner_pair // 2], jnp.zeros((), jnp.bfloat16))
    send_rows = send_rows.reshape(ffn_count, CAP, model_width)
    slot_rows = lax.all_to_all(
        send_rows, "expert", split_axis=0, concat_axis=0, tiled=True
    ).reshape(ffn_count * CAP, model_width)
    gate_pre = jnp.dot(slot_rows, w_gate_up[0, 0], preferred_element_type=jnp.float32)
    up_pre = jnp.dot(slot_rows, w_gate_up[0, 1], preferred_element_type=jnp.float32)
    activated = (jax.nn.silu(gate_pre) * up_pre).astype(jnp.bfloat16)
    expert_out = jnp.dot(activated, w_down[0], preferred_element_type=jnp.float32).astype(
        jnp.bfloat16
    )
    expert_out = expert_out.reshape(ffn_count, CAP, model_width)
    returned = lax.all_to_all(
        expert_out, "expert", split_axis=0, concat_axis=0, tiled=True
    ).reshape(ffn_count * CAP, model_width)
    safe_dest = jnp.minimum(destination, ffn_count * CAP - 1)
    ffn_rows = jnp.where(is_routed[:, None], returned[safe_dest].astype(jnp.float32), 0.0)
    ffn_rows = ffn_rows.reshape(tok_count, 2, model_width)
    vector_float = vectors.astype(jnp.float32)
    const_rows = (
        const_weights[:, :, 0:1] * second_float[:, None, :]
        + const_weights[:, :, 1:2] * vector_float[None, :, :]
    )
    pair_out = ffn_rows + jnp.where(
        (route_pair == ffn_count + 1)[:, :, None], second_float[:, None, :], 0.0
    )
    for member in range(2):
        chosen_const = (route_pair == ffn_count + 2 + member)[:, :, None]
        pair_out = pair_out + jnp.where(chosen_const, const_rows[:, member][:, None, :], 0.0)
    result = after_attn + jnp.sum(gate_pair[:, :, None] * pair_out, axis=1)
    kept_state = SimpleNamespace(
        normal_one=normal_one,
        scale_one=scale_one,
        first_in=first_in,
        queries=queries,
        key_rows=key_rows,
        value_rows=value_rows,
        allowed=allowed,
        log_total=log_total,
        mixed_heads=mixed_heads,
        normal_two=normal_two,
        scale_two=scale_two,
        second_float=second_float,
        picked=picked,
        first_gate=first_gate,
        gate_pair=gate_pair,
        const_weights=const_weights,
        safe_dest=safe_dest,
        is_routed=is_routed,
        owner_pair=owner_pair,
        has_row=has_row,
        slot_rows=slot_rows,
        gate_pre=gate_pre,
        up_pre=up_pre,
        pair_out=pair_out,
        route_pair=route_pair,
    )
    return (result, logits, kept_state)


def layer_backward(upstream, kept_state, dense_set, expert_set):
    w_in, w_out, gain_rows, w_router, vectors = dense_set
    w_gate_up, w_down = expert_set
    tok_count, model_width = upstream.shape
    head_size = model_width // H
    ffn_count = lax.axis_size("expert")
    gain_float = gain_rows.astype(jnp.float32)
    vector_float = vectors.astype(jnp.float32)
    route_pair = kept_state.route_pair
    gate_pair = kept_state.gate_pair
    second_float = kept_state.second_float
    const_weights = kept_state.const_weights
    scaled = gate_pair[:, :, None] * upstream[:, None, :]
    grad_gates = jnp.sum(kept_state.pair_out * upstream[:, None, :], axis=-1)
    grad_slots = jnp.where(
        kept_state.has_row, scaled.reshape(-1, model_width)[kept_state.owner_pair], 0.0
    )
    grad_slots = grad_slots.astype(jnp.bfloat16).reshape(ffn_count, CAP, model_width)
    grad_rows = lax.all_to_all(
        grad_slots, "expert", split_axis=0, concat_axis=0, tiled=True
    ).reshape(ffn_count * CAP, model_width)
    gate_pre = kept_state.gate_pre
    up_pre = kept_state.up_pre
    slot_rows = kept_state.slot_rows
    sigmoid_gate = jax.nn.sigmoid(gate_pre)
    silu_gate = gate_pre * sigmoid_gate
    activated = (silu_gate * up_pre).astype(jnp.bfloat16)
    grad_down = jnp.einsum("rf,rd->fd", activated, grad_rows, preferred_element_type=jnp.float32)
    grad_act = jnp.einsum("rd,fd->rf", grad_rows, w_down[0], preferred_element_type=jnp.float32)
    grad_gate_pre = (
        grad_act * up_pre * sigmoid_gate * (1.0 + gate_pre * (1.0 - sigmoid_gate))
    ).astype(jnp.bfloat16)
    grad_up_pre = (grad_act * silu_gate).astype(jnp.bfloat16)
    grad_w_gate = jnp.einsum(
        "rd,rf->df", slot_rows, grad_gate_pre, preferred_element_type=jnp.float32
    )
    grad_w_up = jnp.einsum("rd,rf->df", slot_rows, grad_up_pre, preferred_element_type=jnp.float32)
    expert_grads = (jnp.stack([grad_w_gate, grad_w_up], axis=1), grad_down)
    grad_in_rows = jnp.einsum(
        "rf,df->rd", grad_gate_pre, w_gate_up[0, 0], preferred_element_type=jnp.float32
    )
    grad_in_rows = grad_in_rows + jnp.einsum(
        "rf,df->rd", grad_up_pre, w_gate_up[0, 1], preferred_element_type=jnp.float32
    )
    grad_back = lax.all_to_all(
        grad_in_rows.reshape(ffn_count, CAP, model_width).astype(jnp.bfloat16),
        "expert",
        split_axis=0,
        concat_axis=0,
        tiled=True,
    ).astype(jnp.float32)
    grad_back = grad_back.reshape(ffn_count * CAP, model_width)
    grad_second = jnp.where(
        kept_state.is_routed[:, None], grad_back[kept_state.safe_dest], 0.0
    )
    grad_second = jnp.sum(grad_second.reshape(tok_count, 2, model_width), axis=1)
    grad_second = grad_second + jnp.sum(
        jnp.where((route_pair == ffn_count + 1)[:, :, None], scaled, 0.0), axis=1
    )
    grad_vectors = []
    grad_const = []
    for member in range(2):
        grad_member = jnp.sum(
            jnp.where((route_pair == ffn_count + 2 + member)[:, :, None], scaled, 0.0), axis=1
        )
        grad_second = grad_second + const_weights[:, member, 0:1] * grad_member
        grad_vectors.append(jnp.sum(const_weights[:, member, 1:2] * grad_member, axis=0))
        grad_first_weight = jnp.sum(grad_member * second_float, axis=-1)
        grad_second_weight = jnp.sum(grad_member * vector_float[member][None, :], axis=-1)
        weight_mean = (
            const_weights[:, member, 0] * grad_first_weight
            + const_weights[:, member, 1] * grad_second_weight
        )
        grad_const.append(const_weights[:, member, 0] * (grad_first_weight - weight_mean))
        grad_const.append(const_weights[:, member, 1] * (grad_second_weight - weight_mean))
    first_gate = kept_state.first_gate
    grad_diff = first_gate * (1.0 - first_gate) * (grad_gates[:, 0] - grad_gates[:, 1])
    grad_chosen = jnp.stack([grad_diff, -grad_diff], axis=1)
    grad_logits = jnp.sum(jnp.where(kept_state.picked, grad_chosen[:, :, None], 0.0), axis=1)
    grad_all = jnp.concatenate([grad_logits, jnp.stack(grad_const, axis=1)], axis=1)
    grad_router = jnp.einsum(
        "td,tc->dc", second_float, grad_all, precision=HIGHEST, preferred_element_type=jnp.float32
    )
    grad_second = grad_second + jnp.einsum(
        "tc,dc->td",
        grad_all,
        w_router.astype(jnp.float32),
        precision=HIGHEST,
        preferred_element_type=jnp.float32,
    )
    normal_two = kept_state.normal_two
    grad_gain_two = jnp.sum(grad_second * normal_two, axis=0)
    grad_after = upstream + norm_back(
        grad_second * gain_float[1], normal_two, kept_state.scale_two
    )
    grad_attn = grad_after.astype(jnp.bfloat16)
    grad_w_out = jnp.einsum(
        "td,te->de", kept_state.mixed_heads, grad_attn, preferred_element_type=jnp.float32
    )
    grad_mixed = jnp.einsum(
        "te,de->td", grad_attn, w_out, preferred_element_type=jnp.float32
    ).astype(jnp.bfloat16)
    grad_mixed = grad_mixed.reshape(tok_count, H, head_size)
    queries = kept_state.queries
    key_rows = kept_state.key_rows
    value_rows = kept_state.value_rows
    raw_scores = masked_scores(queries, key_rows, kept_state.allowed)
    attn_probs = jnp.exp(raw_scores - kept_state.log_total)
    grad_probs = jnp.einsum(
        "thd,shd->hts", grad_mixed, value_rows, preferred_element_type=jnp.float32
    )
    grad_values = jnp.einsum(
        "hts,thd->shd",
        attn_probs.astype(jnp.bfloat16),
        grad_mixed,
        preferred_element_type=jnp.float32,
    )
    row_sum = jnp.sum(grad_probs * attn_probs, axis=-1, keepdims=True)
    grad_raw = (attn_probs * (grad_probs - row_sum)).astype(jnp.bfloat16)
    grad_queries = (
        jnp.einsum("hts,shd->thd", grad_raw, key_rows, preferred_element_type=jnp.float32) * 0.125
    )
    grad_keys = (
        jnp.einsum("hts,thd->shd", grad_raw, queries, preferred_element_type=jnp.float32) * 0.125
    )
    stacked = (
        jnp.stack([grad_queries, grad_keys, grad_values])
        .reshape(3, tok_count, model_width)
        .astype(jnp.bfloat16)
    )
    grad_w_in = jnp.einsum(
        "td,jte->dje", kept_state.first_in, stacked, preferred_element_type=jnp.float32
    )
    grad_first = jnp.einsum("jte,jde->td", stacked, w_in, preferred_element_type=jnp.float32)
    normal_one = kept_state.normal_one
    grad_gain_one = jnp.sum(grad_first * normal_one, axis=0)
    grad_hidden = grad_after + norm_back(
        grad_first * gain_float[0], normal_one, kept_state.scale_one
    )
    dense_grads = (
        grad_w_in,
        grad_w_out,
        jnp.stack([grad_gain_one, grad_gain_two], axis=1),
        grad_router,
        jnp.stack(grad_vectors, axis=1),
    )
    return (grad_hidden, grad_logits, dense_grads, expert_grads)


def plain_body(
    tokens,
    gate_input,
    routes,
    block_ids,
    cotangent,
    norm_gain,
    attn_in,
    attn_out,
    router,
    const_vec,
    expert_gu,
    expert_down,
):
    hidden = tokens.astype(jnp.float32)
    previous = gate_input
    blocks = block_ids[0]
    dense_kept = []
    expert_kept = []
    level_index = 0
    dense_set = (
        lax.all_gather(attn_in[level_index], EVERY, axis=1, tiled=True),
        lax.all_gather(attn_out[level_index], EVERY, axis=0, tiled=True),
        lax.all_gather(norm_gain[level_index], EVERY, axis=1, tiled=True),
        lax.all_gather(router[level_index], EVERY, axis=0, tiled=True),
        lax.all_gather(const_vec[level_index], EVERY, axis=1, tiled=True),
    )
    expert_set = (
        lax.all_gather(expert_gu[level_index], "shard", axis=2, tiled=True),
        lax.all_gather(expert_down[level_index], "shard", axis=1, tiled=True),
    )
    hidden, previous, kept_state = layer_forward(
        hidden, previous, routes, blocks, dense_set, expert_set
    )
    dense_kept.append(dense_set)
    expert_kept.append(expert_set)
    states = [kept_state]
    upstream = cotangent.astype(jnp.float32)
    logits_next = jnp.zeros(gate_input.shape, jnp.float32)
    dense_out = [None] * LAYERS
    expert_out = [None] * LAYERS
    for level_index in reversed(range(LAYERS)):
        dense_set = (
            lax.all_gather(attn_in[level_index], EVERY, axis=1, tiled=True),
            lax.all_gather(attn_out[level_index], EVERY, axis=0, tiled=True),
            lax.all_gather(norm_gain[level_index], EVERY, axis=1, tiled=True),
            lax.all_gather(router[level_index], EVERY, axis=0, tiled=True),
            lax.all_gather(const_vec[level_index], EVERY, axis=1, tiled=True),
        )
        expert_set = (
            lax.all_gather(expert_gu[level_index], "shard", axis=2, tiled=True),
            lax.all_gather(expert_down[level_index], "shard", axis=1, tiled=True),
        )
        upstream, logits_next, dense_grads, expert_grads = layer_backward(
            upstream, states[level_index], dense_set, expert_set
        )
        dense_done = (
            lax.psum_scatter(dense_grads[0], EVERY, scatter_dimension=0, tiled=True),
            lax.psum_scatter(dense_grads[1], EVERY, scatter_dimension=0, tiled=True),
            lax.psum_scatter(dense_grads[2], EVERY, scatter_dimension=0, tiled=True),
            lax.psum_scatter(dense_grads[3], EVERY, scatter_dimension=0, tiled=True),
            lax.psum_scatter(dense_grads[4], EVERY, scatter_dimension=0, tiled=True),
        )
        expert_grads = (
            lax.psum_scatter(expert_grads[0], "shard", scatter_dimension=0, tiled=True),
            lax.psum_scatter(expert_grads[1], "shard", scatter_dimension=0, tiled=True),
        )
        dense_out[level_index] = (
            jnp.transpose(dense_done[0], (1, 0, 2)),
            dense_done[1],
            dense_done[2].T,
            dense_done[3],
            dense_done[4].T,
        )
        expert_out[level_index] = (
            jnp.transpose(expert_grads[0], (1, 0, 2))[None],
            expert_grads[1][None],
        )
    dense_pairs = tuple((jnp.stack([dense_out[0][member]]) for member in range(5)))
    expert_pairs = tuple((jnp.stack([expert_out[0][member]]) for member in range(2)))
    attn_in_grad, attn_out_grad, norm_gain_grad, router_grad, const_vec_grad = dense_pairs
    expert_gu_grad, expert_down_grad = expert_pairs
    return (
        hidden.astype(jnp.bfloat16),
        upstream,
        logits_next,
        norm_gain_grad,
        attn_in_grad,
        attn_out_grad,
        router_grad,
        const_vec_grad,
        expert_gu_grad,
        expert_down_grad,
    )


def solution(mesh):
    in_specs = (
        P(EVERY, None),
        P(EVERY, None),
        P(EVERY, None),
        P(EVERY, None),
        P(EVERY, None),
        P(None, None, EVERY),
        P(None, None, EVERY, None),
        P(None, EVERY, None),
        P(None, EVERY, None),
        P(None, None, EVERY),
        P(None, "expert", None, "shard", None),
        P(None, "expert", "shard", None),
    )
    out_specs = (
        P(EVERY, None),
        P(EVERY, None),
        P(EVERY, None),
        P(None, None, EVERY),
        P(None, None, EVERY, None),
        P(None, EVERY, None),
        P(None, EVERY, None),
        P(None, None, EVERY),
        P(None, "expert", None, "shard", None),
        P(None, "expert", "shard", None),
    )
    step = small_body if dict(mesh.shape) == {"expert": 4, "shard": 8} else plain_body
    return jax.shard_map(step, mesh=mesh, in_specs=in_specs, out_specs=out_specs, check_vma=False)
```

```python
from types import SimpleNamespace

import jax
import jax.numpy as jnp
from jax import lax
from jax.experimental import pallas as pl
from jax.experimental.pallas import tpu as pltpu
from jax.sharding import PartitionSpec as P

EVERY = ("expert", "shard")
H = 12
CAP = 160
EPSILON = 1e-06
MESH = pl.DeviceIdType.MESH
F32 = jnp.float32
BF16 = jnp.bfloat16
NN = (((1,), (0,)), ((), ()))
NT = (((1,), (1,)), ((), ()))
TN = (((0,), (0,)), ((), ()))


def mm(a, b, dims=NN):
    return lax.dot_general(a, b, dims, preferred_element_type=F32)


def iota(shape, dim):
    return lax.broadcasted_iota(jnp.int32, shape, dim)


def where_am_i():
    e, s = lax.axis_index("expert"), lax.axis_index("shard")
    return e // 2, e % 2, s // 2, s % 2


def device(x, c, z, y):
    return (x * 2 + c, z * 2 + y)


def remote(src, dst, send, recv, to):
    return pltpu.make_async_remote_copy(
        src_ref=src, dst_ref=dst, send_sem=send, recv_sem=recv, device_id=to, device_id_type=MESH
    )


def split3(v):
    hi = v.astype(BF16)
    rest = v - hi.astype(F32)
    mid = rest.astype(BF16)
    return hi, mid, (rest - mid.astype(F32)).astype(BF16)


def inside(v):
    return (v >= 0) & (v <= 3)


def layer_kernel(
    ai_in, ao_in, router_in, gain_in, const_in, routes_in, prev_in, blk_in,
    tokens, cotangent, gu_in, dn_in,
    out, in_grad, gate_grad, attn_in_grad, attn_out_grad, router_grad, gain_grad, const_grad,
    gu_out, dn_out, probs,
    tok, cot, gu, dn, w4, smalls, ga, gb, qkv, act, dgate, dup, deo, turned, rx, rc, ggu, gdn, rgu, rdn,
    land_b, land_e, half_b, half_e, pbuf, mixed, second, scal, z_in, sm, sm_in,
    loc, sz, rz, s1, r1, s2, r2, sc_, rc_, se, re, sy, ry, sd, rd, sx, rx_, own,
    sb, rb, sv, rv, sg, rg, sw, rw, lp, tc, qc, t2, q2, t1, q1, tz, qz, ss, rs,
):
    x, c, z, y = where_am_i()
    e = x * 2 + c
    met = pltpu.get_barrier_semaphore()
    friends = [device(x, c, lax.rem(z + i, 4), y) for i in (1, 2, 3)]
    friends += [device(x, 1 - c, z, y), device(1 - x, c, z, y), device(x, c, z, 1 - y), device(1 - x, c, z, 1 - y)]
    friends += [device(x, 1 - c, z, 1 - y)]
    for friend in friends:
        pl.semaphore_signal(met, inc=1, device_id=friend, device_id_type=MESH)
    pl.semaphore_wait(met, 8)
    act2, dgate2, dup2 = act, dgate.reshape(1536, 1024), dup.reshape(1536, 1024)
    rx2, rc2 = rx.reshape(1280, 896), rc.reshape(1280, 768)
    p0, p1, bias = dup2.at[0:640, 0:512], dup2.at[0:640, 512:1024], dup2.at[640:1152, 0:512]
    first, stage_x, stage_c = dgate2.at[0:512, 0:768], dgate2.at[640:1280, 0:896], act.at[0:640, 0:768]
    units = (
        (ga, y, x, device(x, c, z, 1 - y), device(1 - x, c, z, y)),
        (gb, y, x, device(x, c, z, 1 - y), device(1 - x, c, z, y)),
    )
    core = device(x, 1 - c, z, y)

    def block_of(i, size=256):
        return pl.ds(pl.multiple_of(i * size, size), size)

    load_tok = pltpu.make_async_copy(tokens, tok, loc.at[0])
    load_cot = pltpu.make_async_copy(cotangent, cot, loc.at[1])
    load_cot.start()
    load_tok.start()

    def slot(h2, h1, zb):
        return ((c * 2 + h2) * 2 + h1) * 4 + zb

    def put_z(u, zb, way):
        g, h1, h2, _, _ = units[u]
        at = g.at[slot(h2, h1, zb)]
        i = (u * 2 + (way + 1) // 2) * 4 + zb
        return remote(at, at, sz.at[i], rz.at[u * 4 + zb], device(x, c, jnp.clip(z + way, 0, 3), y))

    def put_1(u, zb, got=False):
        g, h1, h2, to1, _ = units[u]
        at = g.at[slot(h2, (1 - h1) if got else h1, zb)]
        return remote(at, at, s1.at[u * 4 + zb], r1.at[u * 4 + zb], to1)

    def put_2(u, hh, zb, got=False):
        g, h1, h2, _, to2 = units[u]
        at = g.at[slot((1 - h2) if got else h2, hh, zb)]
        i = u * 8 + hh * 4 + zb
        return remote(at, at, s2.at[i], r2.at[i], to2)

    def put_c(u, hh, got=False):
        at = units[u][0].at[pl.ds((((1 - c) if got else c) * 2 + hh) * 8, 8)]
        return remote(at, at, sc_.at[u * 2 + hh], rc_.at[u * 2 + hh], core)

    few = jnp.concatenate([router_in[...].astype(F32), gain_in[...].astype(F32), const_in[...].astype(F32)], axis=0)
    spread = (iota((16, 128), 0) == iota((16, 128), 1)).astype(BF16)
    few = mm(few.astype(BF16), spread, TN).astype(BF16)
    mine_a = mine_b = slot(x, y, z)
    ga[mine_a, 0:24, 0:768] = ai_in[0]
    ga[mine_a, 24:48, 0:768] = ai_in[1]
    ga[mine_a, 0:24, 768:896] = few
    ga[mine_a, 24:48, 768:896] = jnp.zeros((24, 128), BF16)
    gb[mine_b, 0:24, :] = ai_in[2]
    gb[mine_b, 24:48, :] = ao_in[...]
    for u in range(2):
        for way in (-1, 1):
            pl.when(inside(z + way))(lambda: put_z(u, z, way).start())
        put_1(u, z).start()
        put_2(u, units[u][1], z).start()

    def piece(k, zb):
        if k == 2:
            return dn.at[block_of(zb)]
        rows = pl.ds(pl.multiple_of(zb * 192 + (y if k == 0 else 1 - y) * 96, 32), 96)
        return gu.at[:, rows, slice(0, 1024) if k == 0 else slice(0, 512) if k == 1 else slice(512, 1024)]

    def put_e(k, zb, way):
        at = piece(k, zb)
        i = ((way + 1) // 2) * 16 + k * 4 + zb
        return remote(at, at, se.at[i], re.at[k * 4 + zb], device(x, c, jnp.clip(z + way, 0, 3), y))

    at_home = c == y
    half_rows = lambda yy: pl.ds(pl.multiple_of(z * 192 + yy * 96, 32), 96)

    def own_gu(q):
        there = gu.at[:, half_rows(y), 256 * q : 256 * q + 256]
        return pltpu.make_async_copy(gu_in.at[:, :, block_of(2 * q + c)], there, loc.at[3 + q])

    def put_y(cc, q):
        there = gu.at[:, half_rows(y), 256 * q : 256 * q + 256]
        return remote(gu_in.at[:, :, 512 * q + 256 * cc : 512 * q + 256 * cc + 256], there, sy.at[cc * 4 + q], ry.at[y * 4 + q], device(x, cc, z, c))

    def got_y(yo, q):
        here = gu.at[:, half_rows(yo), 256 * q : 256 * q + 256]
        return remote(gu_in.at[:, :, 512 * q : 512 * q + 256], here, sy.at[q], ry.at[yo * 4 + q], core)

    def own_dn():
        return pltpu.make_async_copy(dn_in, dn.at[block_of(z)], loc.at[2])

    def put_dn():
        return remote(dn_in, dn.at[block_of(z)], sy.at[8], ry.at[8], device(x, y, z, c))

    away = jnp.logical_not(at_home)

    def exchange_home():
        for q in range(4):
            for cc in range(2):
                pl.when(at_home & (c == cc))(lambda: own_gu(q).start())
                pl.when(at_home & (c != cc))(lambda: put_y(cc, q).start())
        pl.when(at_home)(lambda: own_dn().start())

    def exchange_away():
        for q in range(4):
            for cc in range(2):
                pl.when(away)(lambda: put_y(cc, q).start())

    def exchange_done():
        for q in range(4):
            for cc in range(2):
                pl.when(away | (c != cc))(lambda: put_y(cc, q).wait_send())
        pl.when(away)(lambda: put_dn().wait_send())

    def exchanged(yo):
        for q in range(4):
            home = at_home & (y == yo)
            pl.when(home)(lambda: own_gu(q).wait())
            pl.when(jnp.logical_not(home))(lambda: got_y(yo, q).wait_recv())

    def halves(k, down):
        return (k,) if k != 1 else (1, 3) if down else (3, 1)

    def serve(k, r):
        for way in (1, -1):
            zb = z + way * r

            @pl.when(inside(zb) & (z > 0) & (z < 3))
            def _():
                for part in halves(k, way > 0):
                    put_e(part, zb, way).wait_recv()
                    pl.when(inside(z - way))(lambda: put_e(part, zb, -way).start())

    def await_end(k, r, other=None):
        pl.when(z == 0)(lambda: put_e(k, r, 1).wait_recv())
        pl.when(z == 3)(lambda: put_e(k if other is None else other, 3 - r, -1).wait_recv())

    def first_round(k):
        for way in (-1, 1):
            for part in halves(k, way < 0):
                pl.when(inside(z + way))(lambda: put_e(part, z, way).start())

    exchange_home()

    r_t = routes_in[...]
    prev = prev_in[...]
    flat = jnp.concatenate(
        [jnp.zeros((8, 512), F32), r_t.astype(F32), blk_in[...].astype(F32), jnp.zeros((5, 512), F32), prev, jnp.zeros((104, 512), F32)],
        axis=0,
    )
    scal[...] = flat.T
    bias[...] = jnp.where(blk_in[...].astype(F32) <= scal[:, 10:11], 0.0, -1e30).astype(BF16)
    expert_row = iota((16, 512), 0)
    named = ((expert_row == r_t[0:1]) | (expert_row == r_t[1:2])).astype(BF16)
    upper = (iota((512, 512), 0) < iota((512, 512), 1)).astype(BF16)
    count_t = mm(named, upper).astype(jnp.int32) + expert_row * CAP
    for k, ref in ((0, p0), (1, p1)):
        r = r_t[k : k + 1]
        spot = jnp.sum(jnp.where((expert_row == r) & (r < 4), count_t, 0), axis=0, keepdims=True)
        spot = jnp.where(r < 4, spot, -1)
        ref[...] = (iota((640, 512), 0) == spot).astype(BF16)
    load_cot.wait()
    for ed in range(4):
        rows = slice(ed * CAP, ed * CAP + CAP)
        stage_c[rows, :] = mm(p0[rows, :] + p1[rows, :], cot[...]).astype(BF16)

    for r in range(1, 4):
        if r == 2:
            exchange_away()
        if r == 3:
            exchanged(y)
            first_round(0)
        for way in (1, -1):
            zb = z + way * r
            for u in range(2):

                @pl.when(inside(zb))
                def _():
                    put_z(u, zb, way).wait_recv()
                    pl.when(inside(z - way))(lambda: put_z(u, zb, -way).start())
                    put_1(u, zb).start()
                    put_2(u, units[u][1], zb).start()

    pl.when(away)(lambda: put_dn().start())

    for r in range(4):
        for way in (1, -1) if r else (1,):
            zb = z + way * r
            for u in range(2):

                @pl.when(inside(zb))
                def _():
                    put_1(u, zb, True).wait_recv()
                    put_2(u, 1 - units[u][1], zb).start()

        if r == 2:
            serve(0, 1)

    exchanged(1 - y)
    first_round(1)
    for u in range(2):
        put_c(u, units[u][2]).start()
    pl.when(at_home)(lambda: own_dn().wait())
    pl.when(jnp.logical_not(at_home))(lambda: put_dn().wait_recv())
    pl.when(z < 2)(lambda: put_e(2, z, 1).start())
    pl.when(z > 1)(lambda: put_e(2, z, -1).start())
    for u in range(2):
        h1 = units[u][1]
        for hh in (h1, 1 - h1):
            for zb in range(4):
                put_2(u, hh, zb, True).wait_recv()
        put_c(u, 1 - units[u][2]).start()
    for u in range(2):
        for hh in range(2):
            put_c(u, hh, True).wait_recv()

    def assemble(m, _):
        xx, cc, zz = m // 8, (m // 4) % 2, m % 4
        a = [((cc * 2 + xx) * 2 + yy) * 4 + zz for yy in range(2)]
        at = pl.ds(pl.multiple_of(m * 48, 16), 48)
        for j in range(2):
            rows = slice(24 * j, 24 * j + 24)
            w4[j, at, :] = jnp.concatenate([ga[a[0], rows, 0:768], ga[a[1], rows, 0:768]], axis=0)
            w4[2 + j, at, :] = jnp.concatenate([gb[a[0], rows, :], gb[a[1], rows, :]], axis=0)
        smalls[at, :] = jnp.concatenate([ga[a[0], 0:24, 768:896], ga[a[1], 0:24, 768:896]], axis=0)
        return 0

    lax.fori_loop(0, 16, assemble, 0)

    eye = (iota((128, 128), 0) == iota((128, 128), 1)).astype(BF16)
    across = mm(eye, smalls[...], NT)[0:16]
    load_tok.wait()
    for t in range(2):
        rows = slice(256 * t, 256 * t + 256)
        hidden = tok[rows, :].astype(F32)
        scale = lax.rsqrt(jnp.mean(hidden * hidden, axis=-1, keepdims=True) + EPSILON)
        first[rows, :] = (hidden * scale * across[12:13]).astype(BF16)

    def project(i, _):
        j = i // 2
        at = block_of(i % 2)
        qkv[block_of(i), :] = mm(first[at, :], w4[j]).astype(BF16)
        return 0

    lax.fori_loop(0, 6, project, 0)

    expert = x * 2 + y
    me = c * 4 + expert

    def dispatch(stage, landing, sends, recvs, j, got=False):
        eo = (expert + j) % 4
        if got:
            return remote(stage.at[0:CAP], landing.at[c * 4 + eo], sends.at[j], recvs.at[eo], core)
        src = stage.at[pl.ds(pl.multiple_of(eo * CAP, 32), CAP)]
        return remote(src, landing.at[me], sends.at[j], recvs.at[expert], device(eo // 2, c, z, eo % 2))

    def share(landing, sends, recvs, j, got=False):
        eo = (expert + j) % 4
        at = landing.at[((1 - c) if got else c) * 4 + eo]
        return remote(at, at, sends.at[4 + j], recvs.at[4 + eo], core)

    for j in (3, 1, 2):
        dispatch(stage_c, rc, sd, rd, j).start()
    my_rows = pl.ds(pl.multiple_of(expert * CAP, 32), CAP)
    own_c = pltpu.make_async_copy(stage_c.at[my_rows], rc.at[me], own.at[0])
    own_c.start()
    lane = iota((256, 128), 1)

    def head_store(head, half):
        return pltpu.make_async_copy(pbuf.at[half], probs.at[head], lp.at[half])

    def heads(pair, _):
        cols = block_of(pair, 128)
        outs = [[], []]
        for hh in range(2):
            pl.when(pair > 0)(lambda: head_store(2 * pair + hh - 2, hh).wait())
            for t in range(2):
                rows = slice(256 * t, 256 * t + 256)
                q = jnp.where((lane < 64) == (hh == 0), qkv[rows, cols] * BF16(0.125), BF16(0))
                s = mm(q, qkv[512:1024, cols], NT) + bias[rows, :].astype(F32)
                ex = jnp.exp(s - jnp.max(s, axis=-1, keepdims=True))
                p = (ex * (1.0 / jnp.sum(ex, axis=-1, keepdims=True))).astype(BF16)
                pbuf[hh, rows, :] = p
                outs[t].append(mm(p, qkv[1024:1536, cols]))
            head_store(2 * pair + hh, hh).start()
        for t in range(2):
            mixed[256 * t : 256 * t + 256, cols] = jnp.where(lane < 64, outs[t][0], outs[t][1]).astype(BF16)
        return 0

    lax.fori_loop(0, 2, heads, 0)
    serve(1, 1)
    lax.fori_loop(2, 5, heads, 0)
    serve(0, 2)
    lax.fori_loop(5, 6, heads, 0)

    lanes = iota((512, 128), 1)
    named_c = ((lanes == scal[:, 8:9].astype(jnp.int32)) | (lanes == scal[:, 9:10].astype(jnp.int32))).astype(BF16)
    lower = (iota((512, 512), 1) < iota((512, 512), 0)).astype(BF16)
    count = mm(lower, named_c) + lanes.astype(F32) * CAP
    for t in range(2):
        rows = slice(256 * t, 256 * t + 256)
        after = tok[rows, :].astype(F32) + mm(mixed[rows, :], w4[3])
        in_grad[rows, :] = after
        scale = lax.rsqrt(jnp.mean(after * after, axis=-1, keepdims=True) + EPSILON)
        second[rows, :] = (after * scale * across[13:14]).astype(BF16)
        score = mm(second[rows, :], smalls[...])
        r = (scal[rows, 8:9].astype(jnp.int32), scal[rows, 9:10].astype(jnp.int32))
        lane8 = iota((256, 8), 1)
        logits = score[:, 0:8] + scal[rows, 16:24]
        picked = [jnp.sum(jnp.where(lane8 == r[k], logits, 0.0), axis=-1, keepdims=True) for k in range(2)]
        g0 = jax.nn.sigmoid(picked[0] - picked[1])
        values = [g0, 1.0 - g0]
        for m in range(2):
            diff = score[:, 8 + 2 * m : 9 + 2 * m] - score[:, 9 + 2 * m : 10 + 2 * m]
            values += [jax.nn.sigmoid(diff), jax.nn.sigmoid(-diff)]
        for k in range(2):
            spot = jnp.sum(jnp.where(lane == r[k], count[rows], 0.0), axis=-1, keepdims=True)
            values.append(jnp.where(r[k] < 4, spot, -1.0))
        filled = scal[rows, :]
        for i, v in enumerate(values):
            filled = jnp.where(lane == i, v, filled)
        scal[rows, :] = filled

    def three_lanes(v, width):
        hi, mid, lo = split3(v)
        zero, at = BF16(0), iota((width, 128), 1)
        return jnp.where(at == 0, hi, zero) + jnp.where(at == 1, mid, zero) + jnp.where(at == 2, lo, zero)

    parts = [three_lanes(scal[:, k : k + 1], 512) for k in range(2)]
    for j in (3, 1, 2, 0):
        eo = (expert + j) % 4
        at = pl.ds(pl.multiple_of(eo * CAP, 32), CAP)
        stage_x[at, 0:768] = mm(p0[at, :] + p1[at, :], second[...]).astype(BF16)
        stage_x[at, 768:896] = (mm(p0[at, :], parts[0]) + mm(p1[at, :], parts[1])).astype(BF16)
        if j:
            dispatch(stage_x, rx, sx, rx_, j).start()
    own_x = pltpu.make_async_copy(stage_x.at[my_rows], rx.at[me], own.at[1])
    own_x.start()
    serve(1, 2)
    pl.when(z == 1)(lambda: put_e(2, 1, -1).start())
    pl.when(z == 2)(lambda: put_e(2, 2, 1).start())
    serve(2, 1)
    own_c.wait()
    share(rc, sd, rd, 0).start()
    for j in (1, 2, 3):
        dispatch(stage_c, rc, sd, rd, j, True).wait_recv()
        share(rc, sd, rd, j).start()
    own_x.wait()
    share(rx, sx, rx_, 0).start()
    for u in range(2):
        for zb in range(4):
            put_1(u, zb).wait_send()
            put_2(u, 0, zb).wait_send()
            put_2(u, 1, zb).wait_send()
            pl.when((zb >= z) & (z > 0))(lambda: put_z(u, zb, -1).wait_send())
            pl.when((zb <= z) & (z < 3))(lambda: put_z(u, zb, 1).wait_send())
        for hh in range(2):
            put_c(u, hh).wait_send()
    for hh in range(2):
        head_store(10 + hh, hh).wait()
    for j in (1, 2, 3):
        dispatch(stage_x, rx, sx, rx_, j, True).wait_recv()
        share(rx, sx, rx_, j).start()
    serve(2, 2)
    for j in range(4):
        share(rc, sd, rd, j, True).wait_recv()
        share(rc, sd, rd, j).wait_send()
        share(rx, sx, rx_, j, True).wait_recv()
        share(rx, sx, rx_, j).wait_send()
        if j:
            dispatch(stage_c, rc, sd, rd, j).wait_send()
            dispatch(stage_x, rx, sx, rx_, j).wait_send()

    def scaled(i, _):
        g = jnp.sum(rx[i, :, 768:896].astype(F32), axis=-1, keepdims=True)
        deo[pl.ds(pl.multiple_of(i * CAP, 32), CAP), :] = (g * rc[i].astype(F32)).astype(BF16)
        return 0

    lax.fori_loop(0, 8, scaled, 0)
    for t in range(5):
        turned[:, 256 * t : 256 * t + 256] = rx2[256 * t : 256 * t + 256, 0:768].T

    def nth(n):
        one = jnp.where(n == 0, 1, jnp.where(n == 1, 0, n))
        two = jnp.where(n == 0, 2, jnp.where(n == 1, 3, 3 - n))
        return jnp.where(z == 0, n, jnp.where(z == 3, 3 - n, jnp.where(z == 1, one, two)))

    def hidden_part(n):
        q = nth(n)
        cols = block_of(q)

        def some(i, _):
            at = pl.ds(pl.multiple_of(i * 320, 64), 320)
            rows = rx2[at, 0:768]
            u, w = mm(rows, gu[0, :, cols]), mm(rows, gu[1, :, cols])
            dact = mm(deo[at, :], dn[cols, :], NT)
            sig = jax.nn.sigmoid(u)
            silu = u * sig
            act[at, cols] = (silu * w).astype(BF16)
            dgate2[at, cols] = (dact * w * sig * (1.0 + u * (1.0 - sig))).astype(BF16)
            dup2[at, cols] = (dact * silu).astype(BF16)
            return 0

        lax.fori_loop(0, 4, some, 0)

    def is_down(k):
        return isinstance(k, int) and k == 4

    def put_g(zb, k, up):
        land = zb if up else jnp.where(zb == z - 1, 4, zb)
        src, dst = (gdn.at[zb], rdn.at[land]) if is_down(k) else (ggu.at[zb, k], rgu.at[land, k])
        to = device(x, c, jnp.clip(z + (1 if up else -1), 0, 3), y)
        return remote(src, dst, sg.at[zb * 5 + k], rg.at[land * 5 + k], to)

    def got_g(land, k):
        src, dst = (gdn.at[0], rdn.at[land]) if is_down(k) else (ggu.at[0, k], rgu.at[land, k])
        return remote(src, dst, sg.at[k], rg.at[land * 5 + k], core)

    def grad_part(n):
        q = nth(n)
        cols = block_of(q)
        for i, ref in ((0, dgate2), (1, dup2)):
            for h in range(2):
                got = mm(turned[384 * h : 384 * h + 384, :], ref[0:1280, cols]).astype(BF16)
                for s in range(4):
                    ggu[2 * h + s // 2, q, s % 2, i] = got[96 * s : 96 * s + 96]
        gdn[q] = mm(act[0:1280, cols], deo[...], TN).astype(BF16)

    def first_send(n):
        far = {
            0: ((3, 0), (2, 0), (1, 0)),
            1: ((3, 1), (2, 1), (1, 1)),
            2: ((3, 2), (2, 2)),
            3: ((3, 3), (3, 4), (2, 3), (2, 4), (1, 2), (1, 3), (1, 4)),
        }

        def up(i):
            for zb, k in far[i]:
                put_g(zb, k, True).start()

        def down(i):
            for zb, k in far[i]:
                put_g(3 - zb, k if k == 4 else 3 - k, False).start()

        for i in range(4):
            pl.when((z == 0) & (n == i))(lambda: up(i))
            pl.when((z == 3) & (n == i))(lambda: down(i))

    def add_block(zb, land, k):
        if is_down(k):
            gdn[zb] = (gdn[zb].astype(F32) + rdn[land].astype(F32)).astype(BF16)
        else:
            ggu[zb, k] = (ggu[zb, k].astype(F32) + rgu[land, k].astype(F32)).astype(BF16)

    def pass_on(zb, k, up, at):
        @pl.when(z == at)
        def _():
            got_g(zb, k).wait_recv()
            add_block(zb, zb, k)
            put_g(zb, k, up).start()

    def hop1(n):
        for zb, k in ((3, n), (2, n)) if n < 3 else ((3, 3), (3, 4), (2, 3), (2, 4)):
            pass_on(zb, k, True, 1)
            pass_on(3 - zb, k if k == 4 else 3 - k, False, 2)

    def hop2(n):
        for k in (n,) if n < 3 else (3, 4):
            pass_on(3, k, True, 2)
            pass_on(0, k if k == 4 else 3 - k, False, 1)

    def early(n, _):
        pl.when(n == 1)(lambda: await_end(2, 1))
        hidden_part(n)
        grad_part(n)
        first_send(n)
        return 0

    def middle(n, _):
        @pl.when(n == 2)
        def _():
            for r in (1, 2, 3):
                await_end(3, r, 1)
            await_end(2, 2)

        pl.when(n == 3)(lambda: await_end(2, 3))
        hidden_part(n)
        return 0

    def late(n, _):
        grad_part(n)
        first_send(n)
        return 0

    def halve(src, landing, sends, recvs, k):
        return remote(src.at[(1 - c) * 4 + k], landing.at[k], sends.at[k], recvs.at[k], core)

    def back(src, landing, sends, recvs, j, got=False):
        eo = (expert + j) % 4
        if got:
            return remote(src.at[0], landing.at[eo], sends.at[4 + j], recvs.at[4 + eo], core)
        return remote(
            src.at[c * 4 + eo], landing.at[expert], sends.at[4 + j], recvs.at[4 + expert], device(eo // 2, c, z, eo % 2)
        )

    def own_back(src, landing, i):
        return pltpu.make_async_copy(src.at[me], landing.at[expert], own.at[i])

    def wait_back(src, landing, sends, recvs, i):
        own_back(src, landing, i).wait()
        for j in (1, 2, 3):
            back(src, landing, sends, recvs, j, True).wait_recv()

    def row_part(i, _):
        group = jnp.where(i < 2, 1 - c, c)
        at = pl.ds(pl.multiple_of((group * 4 + 2 * (i % 2)) * CAP, 64), 320)
        dbuf = mm(dgate2[at, :], gu[0], NT) + mm(dup2[at, :], gu[1], NT)
        rx2[at, 0:768] = dbuf.astype(BF16)
        eo = mm(act[at, :], dn[...])
        dg = jnp.sum(eo * rc2[at, :].astype(F32), axis=-1, keepdims=True)
        rx2[at, 768:896] = three_lanes(dg, 320)
        rc2[at, :] = eo.astype(BF16)

        @pl.when(i < 2)
        def _():
            for k in (2 * i, 2 * i + 1):
                halve(rx, half_b, sb, rb, k).start()

        return 0

    def join(j, _):
        eo = (expert + j) % 4
        halve(rx, half_b, sb, rb, eo).wait_recv()
        at = c * 4 + eo
        more = rx[at, :, 768:896].astype(F32) + half_b[eo, :, 768:896].astype(F32)
        rx[at, :, 768:896] = three_lanes(jnp.sum(more, axis=-1, keepdims=True), CAP)
        rx[at, :, 0:768] = (rx[at, :, 0:768].astype(F32) + half_b[eo, :, 0:768].astype(F32)).astype(BF16)
        pl.when(j != 0)(lambda: back(rx, land_b, sb, rb, j).start())
        pl.when(j == 0)(lambda: own_back(rx, land_b, 2).start())
        return 0

    def join_out(j, _):
        eo = (expert + j) % 4
        halve(rc, half_e, sv, rv, eo).wait_recv()
        at = c * 4 + eo
        rc[at] = (rc[at].astype(F32) + half_e[eo].astype(F32)).astype(BF16)
        pl.when(j != 0)(lambda: back(rc, land_e, sv, rv, j).start())
        pl.when(j == 0)(lambda: own_back(rc, land_e, 3).start())
        return 0

    for r in (1, 2, 3):
        await_end(0, r)
        await_end(1, r, 3)
    lax.fori_loop(0, 2, early, 0)
    lax.fori_loop(2, 4, middle, 0)
    lax.fori_loop(0, 4, row_part, 0)
    lax.fori_loop(1, 4, join, 0)
    lax.fori_loop(0, 1, join, 0)
    for k in range(4):
        halve(rc, half_e, sv, rv, k).start()
    lax.fori_loop(2, 4, late, 0)

    for t in range(2):
        rows = slice(256 * t, 256 * t + 256)
        turned[:, 512 + 256 * t : 768 + 256 * t] = mixed[rows, :].T
        hidden = tok[rows, :].astype(F32)
        scale = lax.rsqrt(jnp.mean(hidden * hidden, axis=-1, keepdims=True) + EPSILON)
        turned[:, rows] = (hidden * scale * across[12:13]).astype(BF16).T

    def head_load(head, half):
        return pltpu.make_async_copy(probs.at[head], pbuf.at[half], lp.at[half])

    head_load(0, 0).start()
    hop1(0)
    wait_back(rx, land_b, sb, rb, 2)
    lax.fori_loop(0, 4, join_out, 0)
    hop1(1)
    hop2(0)

    def of_tile(rows):
        at = lambda i: scal[rows, i : i + 1]
        r = (at(8).astype(jnp.int32), at(9).astype(jnp.int32))
        place = [(iota((256, 640), 1) == at(6 + k).astype(jnp.int32)).astype(BF16) for k in range(2)]
        return (at(0), at(1)), ((at(2), at(3)), (at(4), at(5))), r, place

    total = jnp.zeros((128, 768), F32)
    gain_two = jnp.zeros((1, 768), F32)
    for t in range(2):
        rows = slice(256 * t, 256 * t + 256)
        g, a, r, place = of_tile(rows)
        dsec = jnp.zeros((256, 768), F32)
        dg = [jnp.zeros((256, 1), F32)] * 2
        got = land_b.reshape(640, 896)
        dsec = dsec + mm(place[0] + place[1], got[:, 0:768])
        for k in range(2):
            dg[k] = dg[k] + jnp.sum(mm(place[k], got[:, 768:896]), axis=-1, keepdims=True)
        dx2 = cot[rows, :].astype(F32)
        sec = second[rows, :].astype(F32)
        dot_s = jnp.sum(dx2 * sec, axis=-1, keepdims=True)
        coef = jnp.zeros((256, 1), F32)
        dz = jnp.zeros((256, 128), F32)
        for k in range(2):
            dg[k] = dg[k] + jnp.where(r[k] == 5, dot_s, 0.0)
            coef = coef + jnp.where(r[k] == 5, g[k], 0.0)
        const = jnp.zeros((256, 128), F32)
        for m in range(2):
            dot_v = jnp.sum(dx2 * across[14 + m : 15 + m], axis=-1, keepdims=True)
            weight = jnp.zeros((256, 1), F32)
            for k in range(2):
                chosen = r[k] == 6 + m
                dg[k] = dg[k] + jnp.where(chosen, a[m][0] * dot_s + a[m][1] * dot_v, 0.0)
                weight = weight + jnp.where(chosen, g[k], 0.0)
            coef = coef + a[m][0] * weight
            const = const + jnp.where(lane == 14 + m, a[m][1] * weight, 0.0)
            da = (weight * dot_s, weight * dot_v)
            mean = a[m][0] * da[0] + a[m][1] * da[1]
            for i in range(2):
                dz = jnp.where(lane == 8 + 2 * m + i, a[m][i] * (da[i] - mean), dz)
        diff = g[0] * g[1] * (dg[0] - dg[1])
        dz = dz + jnp.where(lane == r[0], diff, 0.0) - jnp.where(lane == r[1], diff, 0.0)
        gate_grad[:, rows] = dz.T[0:8]
        hi, mid, _ = split3(dz)
        dsec = dsec + coef * dx2 + mm(hi, smalls[...], NT) + mm(mid, smalls[...], NT)
        total = total + mm(hi, second[rows, :], TN) + mm(mid, second[rows, :], TN)
        hi, mid, _ = split3(const)
        total = total + mm(hi, cot[rows, :], TN) + mm(mid, cot[rows, :], TN)
        after = in_grad[rows, :]
        scale = lax.rsqrt(jnp.mean(after * after, axis=-1, keepdims=True) + EPSILON)
        normal = after * scale
        gain_two = gain_two + jnp.sum(dsec * normal, axis=0, keepdims=True)
        lift = dsec * across[13:14]
        dx1 = dx2 + scale * (lift - normal * jnp.mean(lift * normal, axis=-1, keepdims=True))
        in_grad[rows, :] = dx1
        deo[rows, :] = mm(dx1.astype(BF16), w4[3], NT).astype(BF16)
    row16 = iota((16, 768), 0)
    sm[...] = total[0:16] + jnp.where(row16 == 13, gain_two, 0.0)
    hop1(2)
    hop2(1)

    def place_a(d):
        xx, cc, zz, yy = d // 16, (d // 8) % 2, (d // 2) % 4, d % 2
        return ((cc * 2 + xx) * 2 + yy) * 4 + zz

    def place_b(d):
        xx, cc, zz, yy = d // 16, (d // 8) % 2, (d // 2) % 4, d % 2
        return ((cc * 2 + yy) * 2 + xx) * 4 + zz

    def stage(ref, place_of, i, left, right, cols):
        for h in range(2):
            got = mm(turned[384 * h : 384 * h + 384, left], right).astype(BF16)
            for d in range(16):
                ref[place_of(16 * h + d), 24 * i : 24 * i + 24, cols] = got[24 * d : 24 * d + 24]

    groups = [slice(256 * g, 256 * g + 256) for g in range(3)]
    for g in range(3):
        stage(dup, place_b, 1, slice(512, 1024), in_grad[:, groups[g]].astype(BF16), groups[g])

    stages = (dgate, dup)
    owners = (
        (ga, y, x, device(x, c, z, 1 - y), device(1 - x, c, z, y)),
        (gb, x, y, device(1 - x, c, z, y), device(x, c, z, 1 - y)),
    )

    def give_c(u, hh, g):
        src = stages[u].at[pl.ds(((1 - c) * 2 + hh) * 8, 8), :, groups[g]]
        i = (u * 2 + hh) * 3 + g
        return remote(src, owners[u][0].at[pl.ds(hh * 8, 8), :, groups[g]], tc.at[i], qc.at[i], core)

    def give_2(u, hh, g):
        h2 = owners[u][2]
        src = stages[u].at[pl.ds(((c * 2 + 1 - h2) * 2 + hh) * 4, 4), :, groups[g]]
        i = (u * 2 + hh) * 3 + g
        return remote(src, owners[u][0].at[pl.ds(16 + hh * 4, 4), :, groups[g]], t2.at[i], q2.at[i], owners[u][4])

    def give_1(u, g):
        h1, h2 = owners[u][1:3]
        src = stages[u].at[pl.ds(((c * 2 + h2) * 2 + 1 - h1) * 4, 4), :, groups[g]]
        return remote(src, owners[u][0].at[24:28, :, groups[g]], t1.at[u * 3 + g], q1.at[u * 3 + g], owners[u][3])

    def base(u):
        return ((c * 2 + owners[u][2]) * 2 + owners[u][1]) * 4

    def give_z(u, zb, up, g):
        land = zb if up else jnp.where(zb == z - 1, 4, zb)
        to = device(x, c, jnp.clip(z + (1 if up else -1), 0, 3), y)
        src = stages[u].at[base(u) + zb, :, groups[g]]
        return remote(src, z_in.at[u, land, :, groups[g]], tz.at[(u * 4 + zb) * 3 + g], qz.at[(u * 5 + land) * 3 + g], to)

    def come_z(u, land, g):
        src = stages[u].at[0, :, groups[g]]
        return remote(src, z_in.at[u, land, :, groups[g]], tz.at[g], qz.at[(u * 5 + land) * 3 + g], core)

    def add_in(u, at, n, other, g):
        def one(i, _):
            got = owners[u][0][other + i, :, groups[g]]
            stages[u][at + i, :, groups[g]] = (stages[u][at + i, :, groups[g]].astype(F32) + got.astype(F32)).astype(BF16)
            return 0

        lax.fori_loop(0, n, one, 0)

    def step_c(g):
        for u in range(2):
            h2 = owners[u][2]
            give_c(u, 1 - h2, g).start()
            give_c(u, h2, g).start()

    def step_2(g):
        for u in range(2):
            h1, h2 = owners[u][1:3]
            give_c(u, 1 - h2, g).wait_recv()
            add_in(u, (c * 2 + 1 - h2) * 8, 8, (1 - h2) * 8, g)
            for hh in (1 - h1, h1):
                give_2(u, hh, g).start()
        for u in range(2):
            h2 = owners[u][2]
            give_c(u, h2, g).wait_recv()
            add_in(u, (c * 2 + h2) * 8, 8, h2 * 8, g)

    def step_1(g):
        for u in range(2):
            h1, h2 = owners[u][1:3]
            give_2(u, 1 - h1, g).wait_recv()
            add_in(u, ((c * 2 + h2) * 2 + 1 - h1) * 4, 4, 16 + (1 - h1) * 4, g)
            give_1(u, g).start()
        for u in range(2):
            h1, h2 = owners[u][1:3]
            give_2(u, h1, g).wait_recv()
            add_in(u, base(u), 4, 16 + h1 * 4, g)

    def step_z(g):
        for u in range(2):
            give_1(u, g).wait_recv()
            add_in(u, base(u), 4, 24, g)
            for i in range(3):
                pl.when(z == 0)(lambda: give_z(u, 3 - i, True, g).start())
                pl.when(z == 3)(lambda: give_z(u, i, False, g).start())

    def pass_z(zb, up, at, g):
        @pl.when(z == at)
        def _():
            for u in range(2):
                come_z(u, zb, g).wait_recv()
                i = base(u) + zb
                got = z_in[u, zb, :, groups[g]]
                stages[u][i, :, groups[g]] = (stages[u][i, :, groups[g]].astype(F32) + got.astype(F32)).astype(BF16)
                give_z(u, zb, up, g).start()

    def hop1_z(g):
        for zb in (3, 2):
            pass_z(zb, True, 1, g)
            pass_z(3 - zb, False, 2, g)

    def hop2_z(g):
        pass_z(3, True, 2, g)
        pass_z(0, False, 1, g)

    lane5 = iota((512, 128), 1)

    def heads_back(pair, _):
        cols = block_of(pair, 128)
        grads = []
        for hh in range(2):
            head_load(2 * pair + hh, hh).wait()
            if hh == 0:
                head_load(2 * pair + 1, 1).start()
            else:
                pl.when(pair < 5)(lambda: head_load(2 * pair + 2, 0).start())
            do = jnp.where((lane5 < 64) == (hh == 0), deo[0:512, cols], BF16(0))
            inner = jnp.sum(do.astype(F32) * mixed[:, cols].astype(F32), axis=-1, keepdims=True)
            dq, dk, dv = [], jnp.zeros((512, 128), F32), jnp.zeros((512, 128), F32)
            for t in range(2):
                rows = slice(256 * t, 256 * t + 256)
                p = pbuf[hh, rows, :]
                ds = (p.astype(F32) * (mm(do[rows], qkv[1024:1536, cols], NT) - inner[rows])).astype(BF16)
                dq.append(mm(ds, qkv[512:1024, cols]))
                dk = dk + mm(ds, qkv[rows, cols], TN)
                dv = dv + mm(p, deo[rows, cols], TN)
            grads.append((jnp.concatenate(dq, axis=0) * 0.125, dk * 0.125, dv))
        for j in range(3):
            act[512 * j : 512 * j + 512, cols] = jnp.where(lane5 < 64, grads[0][j], grads[1][j]).astype(BF16)
        return 0

    for g in range(3):
        lax.fori_loop(2 * g, 2 * g + 2, heads_back, 0)
        for ref, place_of, i, j in ((dgate, place_a, 0, 0), (dgate, place_a, 1, 1), (dup, place_b, 0, 2)):
            stage(ref, place_of, i, slice(0, 512), act[512 * j : 512 * j + 512, groups[g]], groups[g])
        step_c(g)
        if g == 0:
            hop2(2)
        if g == 1:
            step_2(0)
        if g == 2:
            step_2(1)
            step_1(0)
            hop1(3)

    gain_one = jnp.zeros((1, 768), F32)
    for t in range(2):
        rows = slice(256 * t, 256 * t + 256)
        dfirst = mm(act[256 * t : 256 * t + 256, 0:768], w4[0], NT)
        dfirst = dfirst + mm(act[512 + 256 * t : 768 + 256 * t, 0:768], w4[1], NT)
        dfirst = dfirst + mm(act[1024 + 256 * t : 1280 + 256 * t, 0:768], w4[2], NT)
        hidden = tok[rows, :].astype(F32)
        scale = lax.rsqrt(jnp.mean(hidden * hidden, axis=-1, keepdims=True) + EPSILON)
        normal = hidden * scale
        gain_one = gain_one + jnp.sum(dfirst * normal, axis=0, keepdims=True)
        lift = dfirst * across[12:13]
        in_grad[rows, :] = in_grad[rows, :] + scale * (lift - normal * jnp.mean(lift * normal, axis=-1, keepdims=True))
    sm[...] = sm[...] + jnp.where(row16 == 12, gain_one, 0.0)

    def small_step(i):
        to = (core, device(1 - x, c, z, y), device(x, c, z, 1 - y))[i]
        return remote(sm.at[...], sm_in.at[i], ss.at[i], rs.at[i], to)

    def small_z(way, got=False):
        zt = lax.rem(z + way, 4)
        if got:
            zt = lax.rem(z - way + 4, 4)
            return remote(sm.at[...], sm_in.at[3 + zt], ss.at[2 + way], rs.at[3 + zt], core)
        return remote(sm.at[...], sm_in.at[3 + z], ss.at[2 + way], rs.at[3 + z], device(x, c, zt, y))

    def swap(q, yo):
        at = gu_out.at[:, :, block_of(2 * q + c)]
        return remote(ggu.at[z, q, yo], at, sw.at[q * 2 + yo], rw.at[q * 2 + c], device(x, y, z, yo))

    def swap_got(q, cc):
        at = gu_out.at[:, :, 512 * q + 256 * cc : 512 * q + 256 * cc + 256]
        return remote(ggu.at[z, q, 0], at, sw.at[q * 2], rw.at[q * 2 + cc], core)

    def keep(q):
        return pltpu.make_async_copy(ggu.at[z, q, y], gu_out.at[:, :, block_of(2 * q + c)], loc.at[3 + q])

    def swap_dn():
        return remote(gdn.at[z], dn_out, sw.at[8], rw.at[8], device(x, y, z, c))

    def keep_dn():
        return pltpu.make_async_copy(gdn.at[z], dn_out, loc.at[2])

    def final(n):
        k = 4 if n == 4 else jnp.where(z % 2 == 0, 3 - n, n)

        @pl.when(z > 0)
        def _():
            got_g(z, k).wait_recv()
            add_block(z, z, k)

        @pl.when(z < 3)
        def _():
            got_g(4, k).wait_recv()
            add_block(z, 4, k)

        if n < 4:
            for yo in range(2):
                home = at_home & (y == yo)
                pl.when(home)(lambda: keep(k).start())
                pl.when(jnp.logical_not(home))(lambda: swap(k, yo).start())
        else:
            pl.when(at_home)(lambda: keep_dn().start())
            pl.when(jnp.logical_not(at_home))(lambda: swap_dn().start())

    small_step(0).start()
    step_2(2)
    step_1(1)
    step_z(0)
    small_step(0).wait()
    sm[...] = sm[...] + sm_in[0]
    small_step(1).start()
    wait_back(rc, land_e, sv, rv, 3)
    for t in range(2):
        rows = slice(256 * t, 256 * t + 256)
        g, a, r, place = of_tile(rows)
        result = tok[rows, :].astype(F32) + mm(mixed[rows, :], w4[3])
        coef = jnp.zeros((256, 1), F32)
        for k in range(2):
            result = result + g[k] * mm(place[k], land_e.reshape(640, 768)[...])
            coef = coef + jnp.where(r[k] == 5, g[k], 0.0)
        for m in range(2):
            weight = jnp.zeros((256, 1), F32)
            for k in range(2):
                weight = weight + jnp.where(r[k] == 6 + m, g[k], 0.0)
            coef = coef + a[m][0] * weight
            result = result + a[m][1] * weight * across[14 + m : 15 + m]
        out[rows, :] = (result + coef * second[rows, :].astype(F32)).astype(BF16)

    step_1(2)
    hop2(3)
    step_z(1)
    small_step(1).wait()
    sm[...] = sm[...] + sm_in[1]
    small_step(2).start()
    step_z(2)
    small_step(2).wait()
    sm[...] = sm[...] + sm_in[2]
    for way in (1, 2, 3):
        small_z(way).start()
    final(0)
    final(1)
    hop1_z(0)
    hop1_z(1)
    hop2_z(0)
    hop1_z(2)
    final(2)
    hop2_z(1)
    hop2_z(2)
    final(3)
    final(4)

    for way in (1, 2, 3):
        small_z(way, True).wait_recv()
    result = sm[...]
    for way in (1, 2, 3):
        result = result + sm_in[3 + lax.rem(z + way, 4)]
    chosen = (iota((768, 128), 0) == iota((768, 128), 1) + 24 * (e * 8 + z * 2 + y)).astype(BF16)
    result = sum(mm(part, chosen) for part in split3(result))
    router_grad[...] = result[0:12, 0:24]
    gain_grad[...] = result[12:14, 0:24]
    const_grad[...] = result[14:16, 0:24]

    for u, ref in ((0, (attn_in_grad.at[0], attn_in_grad.at[1])), (1, (attn_in_grad.at[2], attn_out_grad))):
        for i in range(2):
            ref[i][...] = stages[u][base(u) + z, 24 * i : 24 * i + 24, 0:768].astype(F32)
        for land, there in ((z, z > 0), (4, z < 3)):

            @pl.when(there)
            def _():
                for g in range(3):
                    come_z(u, land, g).wait_recv()
                for i in range(2):
                    ref[i][...] = ref[i][...] + z_in[u, land, 24 * i : 24 * i + 24, :].astype(F32)

    for q in range(4):
        pl.when(at_home)(lambda: keep(q).wait())
        for i in range(2):
            pl.when(jnp.logical_not(at_home & (y == i)))(lambda: swap(q, i).wait_send())
            pl.when(jnp.logical_not(at_home & (c == i)))(lambda: swap_got(q, i).wait_recv())
    pl.when(at_home)(lambda: keep_dn().wait())
    pl.when(jnp.logical_not(at_home))(lambda: swap_dn().wait())
    exchange_done()
    for way in (1, 2, 3):
        small_z(way).wait_send()
    for k in range(4):
        halve(rx, half_b, sb, rb, k).wait_send()
        halve(rc, half_e, sv, rv, k).wait_send()
        if k:
            back(rx, land_b, sb, rb, k).wait_send()
            back(rc, land_e, sv, rv, k).wait_send()

    for zb in range(4):
        for k in range(4):
            pl.when((zb >= z) & (z > 0))(lambda: put_e(k, zb, -1).wait_send())
            pl.when((zb <= z) & (z < 3))(lambda: put_e(k, zb, 1).wait_send())
        for k in range(5):
            pl.when(zb > z)(lambda: put_g(zb, k, True).wait_send())
            pl.when(zb < z)(lambda: put_g(zb, k, False).wait_send())
        for u in range(2):
            for g in range(3):
                pl.when(zb > z)(lambda: give_z(u, zb, True, g).wait_send())
                pl.when(zb < z)(lambda: give_z(u, zb, False, g).wait_send())
    for u in range(2):
        for g in range(3):
            give_1(u, g).wait_send()
            for hh in range(2):
                give_c(u, hh, g).wait_send()
                give_2(u, hh, g).wait_send()


def small_body(
    tokens, gate_input, routes, block_ids, cotangent, norm_gain, attn_in, attn_out, router, const_vec, expert_gu, expert_down
):
    out = lambda *shape, t=F32: jax.ShapeDtypeStruct(shape, t)
    dma = lambda n: pltpu.SemaphoreType.DMA((n,))
    mem = lambda *shape, t=BF16: pltpu.VMEM(shape, t)
    vm = pl.BlockSpec(memory_space=pltpu.VMEM)
    hbm = pl.BlockSpec(memory_space=pl.ANY)
    outs = pl.pallas_call(
        layer_kernel,
        out_shape=(
            out(512, 768, t=BF16), out(512, 768), out(8, 512), out(3, 24, 768), out(24, 768), out(12, 24), out(2, 24), out(2, 24),
            out(2, 96, 2048, t=BF16), out(256, 768, t=BF16), out(12, 512, 512, t=BF16),
        ),
        in_specs=[vm] * 8 + [hbm] * 4,
        out_specs=(vm,) * 8 + (hbm,) * 3,
        scratch_shapes=[
            mem(512, 768), mem(512, 768), mem(2, 768, 1024), mem(1024, 768), mem(4, 768, 768), mem(768, 128),
            mem(32, 48, 896), mem(32, 48, 768), mem(1536, 768), mem(1536, 1024), mem(32, 48, 1024), mem(32, 48, 1024),
            mem(1280, 768), mem(768, 1280), mem(8, CAP, 896), mem(8, CAP, 768),
            mem(4, 4, 2, 2, 96, 256), mem(4, 256, 768), mem(5, 4, 2, 2, 96, 256), mem(5, 256, 768),
            mem(4, CAP, 896), mem(4, CAP, 768), mem(4, CAP, 896), mem(4, CAP, 768), mem(2, 512, 512), mem(512, 768), mem(512, 768), mem(512, 128, t=F32),
            mem(2, 5, 48, 768), mem(16, 768, t=F32), mem(7, 16, 768, t=F32),
            *(dma(n) for n in (8, 16, 8, 8, 8, 16, 16, 4, 4, 32, 16, 9, 9, 8, 8, 8, 8, 4)),
            *(dma(n) for n in (8, 8, 8, 8, 20, 25, 9, 9, 2, 12, 12, 12, 12, 6, 6, 24, 30, 6, 7)),
        ],
        compiler_params=pltpu.CompilerParams(has_side_effects=True, collective_id=0, vmem_limit_bytes=63_200_000),
        name="layer",
    )(
        attn_in[0], attn_out[0], router[0].T, norm_gain[0], const_vec[0], routes.T, gate_input.T, block_ids,
        tokens, cotangent, expert_gu[0, 0], expert_down[0, 0],
    )
    result, in_grad, gate, ai, ao, ro, ng, cv, gu, dn, _ = outs
    return (
        result, in_grad, gate.T, ng[None], ai[None], ao[None], ro.T[None], cv[None],
        gu.astype(F32)[None, None], dn.astype(F32)[None, None],
    )


LAYERS = 1
HIGHEST = lax.Precision.HIGHEST


def normed(values):
    inv_scale = lax.rsqrt(jnp.mean(values * values, axis=-1, keepdims=True) + EPSILON)
    return (values * inv_scale, inv_scale)


def norm_back(upstream, normal, inv_scale):
    return inv_scale * (upstream - normal * jnp.mean(upstream * normal, axis=-1, keepdims=True))


def slot_table(route_pair, ffn_count, capacity):
    flat_route = route_pair.reshape(-1)
    pair_count = flat_route.shape[0]
    one_hot = (flat_route[:, None] == jnp.arange(ffn_count, dtype=jnp.int32)[None, :]).astype(
        jnp.int32
    )
    earlier = jnp.arange(pair_count)[None, :] < jnp.arange(pair_count)[:, None]
    running = jnp.dot(
        earlier.astype(jnp.bfloat16), one_hot.astype(jnp.bfloat16), preferred_element_type=jnp.float32
    ).astype(jnp.int32)
    position = jnp.sum(running * one_hot, axis=1)
    is_routed = flat_route < ffn_count
    destination = jnp.where(is_routed, flat_route * capacity + position, ffn_count * capacity)
    pair_index = jnp.arange(pair_count, dtype=jnp.int32)
    owner_pair = (
        jnp.zeros((ffn_count * capacity,), jnp.int32).at[destination].set(pair_index, mode="drop")
    )
    filled = (
        jnp.zeros((ffn_count * capacity,), jnp.int32)
        .at[destination]
        .set(jnp.ones_like(pair_index), mode="drop")
    )
    return (destination, is_routed, owner_pair, filled)


def masked_scores(queries, key_rows, allowed):
    raw_scores = (
        jnp.einsum("thd,shd->hts", queries, key_rows, preferred_element_type=jnp.float32) * 0.125
    )
    return jnp.where(allowed[None, :, :], raw_scores, -1e30)


def layer_forward(hidden, previous, route_pair, blocks, dense_set, expert_set):
    w_in, w_out, gain_rows, w_router, vectors = dense_set
    w_gate_up, w_down = expert_set
    tok_count, model_width = hidden.shape
    head_size = model_width // H
    experts = previous.shape[1]
    gain_float = gain_rows.astype(jnp.float32)
    normal_one, scale_one = normed(hidden)
    first_in = (normal_one * gain_float[0]).astype(jnp.bfloat16)
    projected = jnp.einsum(
        "td,jde->jte", first_in, w_in, preferred_element_type=jnp.float32
    ).astype(jnp.bfloat16)
    projected = projected.reshape(3, tok_count, H, head_size)
    queries, key_rows, value_rows = (projected[0], projected[1], projected[2])
    allowed = blocks[None, :] <= blocks[:, None]
    raw_scores = masked_scores(queries, key_rows, allowed)
    row_peak = jnp.max(raw_scores, axis=-1, keepdims=True)
    log_total = row_peak + jnp.log(jnp.sum(jnp.exp(raw_scores - row_peak), axis=-1, keepdims=True))
    attn_probs = jnp.exp(raw_scores - log_total).astype(jnp.bfloat16)
    mixed_heads = jnp.einsum(
        "hts,shd->thd", attn_probs, value_rows, preferred_element_type=jnp.float32
    )
    mixed_heads = mixed_heads.reshape(tok_count, model_width).astype(jnp.bfloat16)
    after_attn = hidden + jnp.dot(mixed_heads, w_out, preferred_element_type=jnp.float32)
    normal_two, scale_two = normed(after_attn)
    second_in = (normal_two * gain_float[1]).astype(jnp.bfloat16)
    second_float = second_in.astype(jnp.float32)
    all_logits = jnp.dot(second_in, w_router, preferred_element_type=jnp.float32)
    logits = all_logits[:, :experts] + previous
    picked = route_pair[:, :, None] == jnp.arange(experts, dtype=jnp.int32)[None, None, :]
    chosen = jnp.sum(jnp.where(picked, logits[:, None, :], 0.0), axis=-1)
    first_gate = jax.nn.sigmoid(chosen[:, 0] - chosen[:, 1])
    gate_pair = jnp.stack([first_gate, 1.0 - first_gate], axis=1)
    const_weights = jax.nn.softmax(all_logits[:, experts:].reshape(tok_count, 2, 2), axis=-1)
    ffn_count = lax.axis_size("expert")
    destination, is_routed, owner_pair, filled = slot_table(route_pair, ffn_count, CAP)
    has_row = filled[:, None] > 0
    send_rows = jnp.where(has_row, second_in[owner_pair // 2], jnp.zeros((), jnp.bfloat16))
    send_rows = send_rows.reshape(ffn_count, CAP, model_width)
    slot_rows = lax.all_to_all(
        send_rows, "expert", split_axis=0, concat_axis=0, tiled=True
    ).reshape(ffn_count * CAP, model_width)
    gate_pre = jnp.dot(slot_rows, w_gate_up[0, 0], preferred_element_type=jnp.float32)
    up_pre = jnp.dot(slot_rows, w_gate_up[0, 1], preferred_element_type=jnp.float32)
    activated = (jax.nn.silu(gate_pre) * up_pre).astype(jnp.bfloat16)
    expert_out = jnp.dot(activated, w_down[0], preferred_element_type=jnp.float32).astype(
        jnp.bfloat16
    )
    expert_out = expert_out.reshape(ffn_count, CAP, model_width)
    returned = lax.all_to_all(
        expert_out, "expert", split_axis=0, concat_axis=0, tiled=True
    ).reshape(ffn_count * CAP, model_width)
    safe_dest = jnp.minimum(destination, ffn_count * CAP - 1)
    ffn_rows = jnp.where(is_routed[:, None], returned[safe_dest].astype(jnp.float32), 0.0)
    ffn_rows = ffn_rows.reshape(tok_count, 2, model_width)
    vector_float = vectors.astype(jnp.float32)
    const_rows = (
        const_weights[:, :, 0:1] * second_float[:, None, :]
        + const_weights[:, :, 1:2] * vector_float[None, :, :]
    )
    pair_out = ffn_rows + jnp.where(
        (route_pair == ffn_count + 1)[:, :, None], second_float[:, None, :], 0.0
    )
    for member in range(2):
        chosen_const = (route_pair == ffn_count + 2 + member)[:, :, None]
        pair_out = pair_out + jnp.where(chosen_const, const_rows[:, member][:, None, :], 0.0)
    result = after_attn + jnp.sum(gate_pair[:, :, None] * pair_out, axis=1)
    kept_state = SimpleNamespace(
        normal_one=normal_one,
        scale_one=scale_one,
        first_in=first_in,
        queries=queries,
        key_rows=key_rows,
        value_rows=value_rows,
        allowed=allowed,
        log_total=log_total,
        mixed_heads=mixed_heads,
        normal_two=normal_two,
        scale_two=scale_two,
        second_float=second_float,
        picked=picked,
        first_gate=first_gate,
        gate_pair=gate_pair,
        const_weights=const_weights,
        safe_dest=safe_dest,
        is_routed=is_routed,
        owner_pair=owner_pair,
        has_row=has_row,
        slot_rows=slot_rows,
        gate_pre=gate_pre,
        up_pre=up_pre,
        pair_out=pair_out,
        route_pair=route_pair,
    )
    return (result, logits, kept_state)


def layer_backward(upstream, kept_state, dense_set, expert_set):
    w_in, w_out, gain_rows, w_router, vectors = dense_set
    w_gate_up, w_down = expert_set
    tok_count, model_width = upstream.shape
    head_size = model_width // H
    ffn_count = lax.axis_size("expert")
    gain_float = gain_rows.astype(jnp.float32)
    vector_float = vectors.astype(jnp.float32)
    route_pair = kept_state.route_pair
    gate_pair = kept_state.gate_pair
    second_float = kept_state.second_float
    const_weights = kept_state.const_weights
    scaled = gate_pair[:, :, None] * upstream[:, None, :]
    grad_gates = jnp.sum(kept_state.pair_out * upstream[:, None, :], axis=-1)
    grad_slots = jnp.where(
        kept_state.has_row, scaled.reshape(-1, model_width)[kept_state.owner_pair], 0.0
    )
    grad_slots = grad_slots.astype(jnp.bfloat16).reshape(ffn_count, CAP, model_width)
    grad_rows = lax.all_to_all(
        grad_slots, "expert", split_axis=0, concat_axis=0, tiled=True
    ).reshape(ffn_count * CAP, model_width)
    gate_pre = kept_state.gate_pre
    up_pre = kept_state.up_pre
    slot_rows = kept_state.slot_rows
    sigmoid_gate = jax.nn.sigmoid(gate_pre)
    silu_gate = gate_pre * sigmoid_gate
    activated = (silu_gate * up_pre).astype(jnp.bfloat16)
    grad_down = jnp.einsum("rf,rd->fd", activated, grad_rows, preferred_element_type=jnp.float32)
    grad_act = jnp.einsum("rd,fd->rf", grad_rows, w_down[0], preferred_element_type=jnp.float32)
    grad_gate_pre = (
        grad_act * up_pre * sigmoid_gate * (1.0 + gate_pre * (1.0 - sigmoid_gate))
    ).astype(jnp.bfloat16)
    grad_up_pre = (grad_act * silu_gate).astype(jnp.bfloat16)
    grad_w_gate = jnp.einsum(
        "rd,rf->df", slot_rows, grad_gate_pre, preferred_element_type=jnp.float32
    )
    grad_w_up = jnp.einsum("rd,rf->df", slot_rows, grad_up_pre, preferred_element_type=jnp.float32)
    expert_grads = (jnp.stack([grad_w_gate, grad_w_up], axis=1), grad_down)
    grad_in_rows = jnp.einsum(
        "rf,df->rd", grad_gate_pre, w_gate_up[0, 0], preferred_element_type=jnp.float32
    )
    grad_in_rows = grad_in_rows + jnp.einsum(
        "rf,df->rd", grad_up_pre, w_gate_up[0, 1], preferred_element_type=jnp.float32
    )
    grad_back = lax.all_to_all(
        grad_in_rows.reshape(ffn_count, CAP, model_width).astype(jnp.bfloat16),
        "expert",
        split_axis=0,
        concat_axis=0,
        tiled=True,
    ).astype(jnp.float32)
    grad_back = grad_back.reshape(ffn_count * CAP, model_width)
    grad_second = jnp.where(
        kept_state.is_routed[:, None], grad_back[kept_state.safe_dest], 0.0
    )
    grad_second = jnp.sum(grad_second.reshape(tok_count, 2, model_width), axis=1)
    grad_second = grad_second + jnp.sum(
        jnp.where((route_pair == ffn_count + 1)[:, :, None], scaled, 0.0), axis=1
    )
    grad_vectors = []
    grad_const = []
    for member in range(2):
        grad_member = jnp.sum(
            jnp.where((route_pair == ffn_count + 2 + member)[:, :, None], scaled, 0.0), axis=1
        )
        grad_second = grad_second + const_weights[:, member, 0:1] * grad_member
        grad_vectors.append(jnp.sum(const_weights[:, member, 1:2] * grad_member, axis=0))
        grad_first_weight = jnp.sum(grad_member * second_float, axis=-1)
        grad_second_weight = jnp.sum(grad_member * vector_float[member][None, :], axis=-1)
        weight_mean = (
            const_weights[:, member, 0] * grad_first_weight
            + const_weights[:, member, 1] * grad_second_weight
        )
        grad_const.append(const_weights[:, member, 0] * (grad_first_weight - weight_mean))
        grad_const.append(const_weights[:, member, 1] * (grad_second_weight - weight_mean))
    first_gate = kept_state.first_gate
    grad_diff = first_gate * (1.0 - first_gate) * (grad_gates[:, 0] - grad_gates[:, 1])
    grad_chosen = jnp.stack([grad_diff, -grad_diff], axis=1)
    grad_logits = jnp.sum(jnp.where(kept_state.picked, grad_chosen[:, :, None], 0.0), axis=1)
    grad_all = jnp.concatenate([grad_logits, jnp.stack(grad_const, axis=1)], axis=1)
    grad_router = jnp.einsum(
        "td,tc->dc", second_float, grad_all, precision=HIGHEST, preferred_element_type=jnp.float32
    )
    grad_second = grad_second + jnp.einsum(
        "tc,dc->td",
        grad_all,
        w_router.astype(jnp.float32),
        precision=HIGHEST,
        preferred_element_type=jnp.float32,
    )
    normal_two = kept_state.normal_two
    grad_gain_two = jnp.sum(grad_second * normal_two, axis=0)
    grad_after = upstream + norm_back(
        grad_second * gain_float[1], normal_two, kept_state.scale_two
    )
    grad_attn = grad_after.astype(jnp.bfloat16)
    grad_w_out = jnp.einsum(
        "td,te->de", kept_state.mixed_heads, grad_attn, preferred_element_type=jnp.float32
    )
    grad_mixed = jnp.einsum(
        "te,de->td", grad_attn, w_out, preferred_element_type=jnp.float32
    ).astype(jnp.bfloat16)
    grad_mixed = grad_mixed.reshape(tok_count, H, head_size)
    queries = kept_state.queries
    key_rows = kept_state.key_rows
    value_rows = kept_state.value_rows
    raw_scores = masked_scores(queries, key_rows, kept_state.allowed)
    attn_probs = jnp.exp(raw_scores - kept_state.log_total)
    grad_probs = jnp.einsum(
        "thd,shd->hts", grad_mixed, value_rows, preferred_element_type=jnp.float32
    )
    grad_values = jnp.einsum(
        "hts,thd->shd",
        attn_probs.astype(jnp.bfloat16),
        grad_mixed,
        preferred_element_type=jnp.float32,
    )
    row_sum = jnp.sum(grad_probs * attn_probs, axis=-1, keepdims=True)
    grad_raw = (attn_probs * (grad_probs - row_sum)).astype(jnp.bfloat16)
    grad_queries = (
        jnp.einsum("hts,shd->thd", grad_raw, key_rows, preferred_element_type=jnp.float32) * 0.125
    )
    grad_keys = (
        jnp.einsum("hts,thd->shd", grad_raw, queries, preferred_element_type=jnp.float32) * 0.125
    )
    stacked = (
        jnp.stack([grad_queries, grad_keys, grad_values])
        .reshape(3, tok_count, model_width)
        .astype(jnp.bfloat16)
    )
    grad_w_in = jnp.einsum(
        "td,jte->dje", kept_state.first_in, stacked, preferred_element_type=jnp.float32
    )
    grad_first = jnp.einsum("jte,jde->td", stacked, w_in, preferred_element_type=jnp.float32)
    normal_one = kept_state.normal_one
    grad_gain_one = jnp.sum(grad_first * normal_one, axis=0)
    grad_hidden = grad_after + norm_back(
        grad_first * gain_float[0], normal_one, kept_state.scale_one
    )
    dense_grads = (
        grad_w_in,
        grad_w_out,
        jnp.stack([grad_gain_one, grad_gain_two], axis=1),
        grad_router,
        jnp.stack(grad_vectors, axis=1),
    )
    return (grad_hidden, grad_logits, dense_grads, expert_grads)


def plain_body(
    tokens,
    gate_input,
    routes,
    block_ids,
    cotangent,
    norm_gain,
    attn_in,
    attn_out,
    router,
    const_vec,
    expert_gu,
    expert_down,
):
    hidden = tokens.astype(jnp.float32)
    previous = gate_input
    blocks = block_ids[0]
    dense_kept = []
    expert_kept = []
    level_index = 0
    dense_set = (
        lax.all_gather(attn_in[level_index], EVERY, axis=1, tiled=True),
        lax.all_gather(attn_out[level_index], EVERY, axis=0, tiled=True),
        lax.all_gather(norm_gain[level_index], EVERY, axis=1, tiled=True),
        lax.all_gather(router[level_index], EVERY, axis=0, tiled=True),
        lax.all_gather(const_vec[level_index], EVERY, axis=1, tiled=True),
    )
    expert_set = (
        lax.all_gather(expert_gu[level_index], "shard", axis=2, tiled=True),
        lax.all_gather(expert_down[level_index], "shard", axis=1, tiled=True),
    )
    hidden, previous, kept_state = layer_forward(
        hidden, previous, routes, blocks, dense_set, expert_set
    )
    dense_kept.append(dense_set)
    expert_kept.append(expert_set)
    states = [kept_state]
    upstream = cotangent.astype(jnp.float32)
    logits_next = jnp.zeros(gate_input.shape, jnp.float32)
    dense_out = [None] * LAYERS
    expert_out = [None] * LAYERS
    for level_index in reversed(range(LAYERS)):
        dense_set = (
            lax.all_gather(attn_in[level_index], EVERY, axis=1, tiled=True),
            lax.all_gather(attn_out[level_index], EVERY, axis=0, tiled=True),
            lax.all_gather(norm_gain[level_index], EVERY, axis=1, tiled=True),
            lax.all_gather(router[level_index], EVERY, axis=0, tiled=True),
            lax.all_gather(const_vec[level_index], EVERY, axis=1, tiled=True),
        )
        expert_set = (
            lax.all_gather(expert_gu[level_index], "shard", axis=2, tiled=True),
            lax.all_gather(expert_down[level_index], "shard", axis=1, tiled=True),
        )
        upstream, logits_next, dense_grads, expert_grads = layer_backward(
            upstream, states[level_index], dense_set, expert_set
        )
        dense_done = (
            lax.psum_scatter(dense_grads[0], EVERY, scatter_dimension=0, tiled=True),
            lax.psum_scatter(dense_grads[1], EVERY, scatter_dimension=0, tiled=True),
            lax.psum_scatter(dense_grads[2], EVERY, scatter_dimension=0, tiled=True),
            lax.psum_scatter(dense_grads[3], EVERY, scatter_dimension=0, tiled=True),
            lax.psum_scatter(dense_grads[4], EVERY, scatter_dimension=0, tiled=True),
        )
        expert_grads = (
            lax.psum_scatter(expert_grads[0], "shard", scatter_dimension=0, tiled=True),
            lax.psum_scatter(expert_grads[1], "shard", scatter_dimension=0, tiled=True),
        )
        dense_out[level_index] = (
            jnp.transpose(dense_done[0], (1, 0, 2)),
            dense_done[1],
            dense_done[2].T,
            dense_done[3],
            dense_done[4].T,
        )
        expert_out[level_index] = (
            jnp.transpose(expert_grads[0], (1, 0, 2))[None],
            expert_grads[1][None],
        )
    dense_pairs = tuple((jnp.stack([dense_out[0][member]]) for member in range(5)))
    expert_pairs = tuple((jnp.stack([expert_out[0][member]]) for member in range(2)))
    attn_in_grad, attn_out_grad, norm_gain_grad, router_grad, const_vec_grad = dense_pairs
    expert_gu_grad, expert_down_grad = expert_pairs
    return (
        hidden.astype(jnp.bfloat16),
        upstream,
        logits_next,
        norm_gain_grad,
        attn_in_grad,
        attn_out_grad,
        router_grad,
        const_vec_grad,
        expert_gu_grad,
        expert_down_grad,
    )


def solution(mesh):
    in_specs = (
        P(EVERY, None),
        P(EVERY, None),
        P(EVERY, None),
        P(EVERY, None),
        P(EVERY, None),
        P(None, None, EVERY),
        P(None, None, EVERY, None),
        P(None, EVERY, None),
        P(None, EVERY, None),
        P(None, None, EVERY),
        P(None, "expert", None, "shard", None),
        P(None, "expert", "shard", None),
    )
    out_specs = (
        P(EVERY, None),
        P(EVERY, None),
        P(EVERY, None),
        P(None, None, EVERY),
        P(None, None, EVERY, None),
        P(None, EVERY, None),
        P(None, EVERY, None),
        P(None, None, EVERY),
        P(None, "expert", None, "shard", None),
        P(None, "expert", "shard", None),
    )
    step = small_body if dict(mesh.shape) == {"expert": 4, "shard": 8} else plain_body
    return jax.shard_map(step, mesh=mesh, in_specs=in_specs, out_specs=out_specs, check_vma=False)
```
